32 devices in a mesh: tm: 4 (over x, core), space: 8 (over z, y).
Axes of the slice: x: 2, y: 2, z: 4, core: 2. Of those that a mesh axis runs over, the one named last changes fastest.
Arguments:
- snapshots: bfloat16 [8, 32, 4, 512], P('tm', 'space'), may hold values from -6 to 6
- conv_weight: bfloat16 [32, 4, 3, 3, 3], replicated, may hold values from -0.625 to 0.625
- conv_bias: float32 [32], replicated, may hold values from -3 to 3
- tap_weight: bfloat16 [3, 32, 3, 32], replicated, may hold values from -0.625 to 0.625
- tap_bias: float32 [3, 32], replicated, may hold values from -3 to 3
- mix_weight: bfloat16 [3, 32, 32], replicated, may hold values from -1 to 1
- mix_bias: float32 [3, 32], replicated, may hold values from -3 to 3
Outputs:
- refined: bfloat16 [8, 32, 32, 512], P('tm', 'space')
The draws below stay inside these ranges and needn't reach their ends.
All inputs are finite; a program needn't handle non-finite values.
Results may differ from the reference program's by a relative error of at most 0.0063.
Values may be sent and summed in bfloat16 or wider, within the bound.
No kernel may reach another device: no remote copies, remote signals or barrier semaphores. Data moves between devices by JAX's collectives and lax.ppermute only.
A program may use at most 64 MiB of HBM per device.

```python
import jax
import jax.numpy as jnp
from jax import lax

CIN = 4
CH = 32
LEVELS = 3
XD = 4
NZ = 32
FRAMES = 8
NX = 32
NY = 16


def level_of(stream_key, dims, cuts, least, largest):
    level = 1.0
    for position, parts in cuts:
        heights = jax.random.uniform(jax.random.fold_in(jax.random.fold_in(stream_key, 6), position), (parts,), jnp.float32, least / len(cuts), largest / len(cuts))
        level = level * jnp.repeat(jnp.exp(heights), dims[position] // parts).reshape((-1,) + (1,) * (len(dims) - 1 - position))
    return level


def bell_draw(own_key, extent, width, reach, cuts=(), held_as=jnp.bfloat16):
    entries = width * jax.random.normal(own_key, extent, jnp.float32)
    if cuts:
        entries = entries * level_of(own_key, extent, cuts, -0.22, 0.18)
    return jnp.clip(entries, -reach, reach).astype(held_as)


def setup_inputs(seed: int = 0) -> dict:
    streams_of = jax.random.split(jax.random.key(seed), 8)
    return {
        "snapshots": bell_draw(streams_of[0], (FRAMES, NX, CIN, NY * NZ), 1.0, 6.0, ((0, 4), (1, 8))),
        "conv_weight": bell_draw(streams_of[1], (CH, CIN, 3, 3, 3), (CIN * 27) ** -0.5, 0.625),
        "conv_bias": bell_draw(streams_of[2], (CH,), 0.5, 3.0, (), jnp.float32),
        "tap_weight": bell_draw(streams_of[3], (LEVELS, CH, 3, CH), (3 * CH) ** -0.5, 0.625),
        "tap_bias": bell_draw(streams_of[4], (LEVELS, CH), 0.5, 3.0, (), jnp.float32),
        "mix_weight": bell_draw(streams_of[5], (LEVELS, CH, CH), CH ** -0.5, 1.0),
        "mix_bias": bell_draw(streams_of[6], (LEVELS, CH), 0.5, 3.0, (), jnp.float32),
    }


def spatial_ref(padded, conv_flat, conv_shift):
    frame_count, rows_pad, field_count, lines_pad, depth_count = padded.shape
    row_count = rows_pad - 2
    line_count = lines_pad - 2
    walled = jnp.pad(padded, ((0, 0), (0, 0), (0, 0), (0, 0), (1, 1)))
    pieces = []
    for delta_x in range(3):
        for delta_y in range(3):
            for delta_z in range(3):
                pieces.append(walled[:, delta_x:delta_x + row_count, :, delta_y:delta_y + line_count, delta_z:delta_z + depth_count])
    patches = jnp.stack(pieces, axis=3).reshape(frame_count, row_count, field_count * 27, line_count * depth_count)
    summed = jnp.einsum("ok,fxkc->fxoc", conv_flat.astype(jnp.float32), patches.astype(jnp.float32))
    return jax.nn.gelu(summed + conv_shift[None, None, :, None]).astype(jnp.bfloat16)


def level_ref(current, spacing, tap_flat, tap_shift, mix_flat, mix_shift):
    blank = jnp.zeros((spacing,) + current.shape[1:], current.dtype)
    before = jnp.concatenate([blank, current[:-spacing]], axis=0)
    after = jnp.concatenate([current[spacing:], blank], axis=0)
    stacked = jnp.concatenate([before, current, after], axis=2)
    summed = jnp.einsum("ok,txkc->txoc", tap_flat.astype(jnp.float32), stacked.astype(jnp.float32))
    gated = jax.nn.gelu(summed + tap_shift[None, None, :, None]).astype(jnp.bfloat16)
    gated = lax.optimization_barrier(gated)
    mixed = jnp.einsum("ok,txkc->txoc", mix_flat.astype(jnp.float32), gated.astype(jnp.float32))
    return (current.astype(jnp.float32) + mixed + mix_shift[None, None, :, None]).astype(jnp.bfloat16)


def reference(snapshots, conv_weight, conv_bias, tap_weight, tap_bias, mix_weight, mix_bias):
    frame_total = snapshots.shape[0]
    conv_flat = conv_weight.reshape(CH, CIN * 27)
    tap_flats = tap_weight.reshape(LEVELS, CH, 3 * CH)
    margined = jnp.concatenate([snapshots[:, -1:], snapshots, snapshots[:, :1]], axis=1)

    def block_work(block_index):
        start = (block_index * XD).astype(jnp.int32)
        piece = lax.dynamic_slice_in_dim(margined, start, XD + 2, axis=1)
        shaped = piece.reshape(frame_total, XD + 2, CIN, NY, NZ)
        wrapped = jnp.concatenate([shaped[:, :, :, -1:], shaped, shaped[:, :, :, :1]], axis=3)
        current = spatial_ref(wrapped, conv_flat, conv_bias)
        for level_index in range(LEVELS):
            current = level_ref(current, 2 ** level_index, tap_flats[level_index], tap_bias[level_index], mix_weight[level_index], mix_bias[level_index])
        return current

    blocks = lax.map(block_work, jnp.arange(NX // XD, dtype=jnp.int32))
    return jnp.moveaxis(blocks, 0, 1).reshape(frame_total, NX, CH, NY * NZ)
```

```python
import functools
import math

import jax
import jax.numpy as jnp
from jax import lax
from jax.experimental import pallas as pl
from jax.experimental.pallas import tpu as pltpu
from jax.sharding import PartitionSpec as P

LEVELS = 3
NZ = 32
GROUP = 4
SLOPE = math.sqrt(2.0 / math.pi)
CUBIC = SLOPE * 0.044715
BF16 = jnp.bfloat16
F32 = jnp.float32


def frame_blocks(axis_size, frames):
    needed = [0]
    counts = [1]
    for level in reversed(range(LEVELS)):
        reach = set()
        for offset in needed:
            for frame in range(frames):
                for step in (-(2**level), 2**level):
                    reach.add((offset + (frame + step) // frames) % axis_size)
        needed = needed + sorted(reach - set(needed))
        spare = [offset for offset in range(axis_size) if offset not in needed]
        while len(needed) * frames % GROUP and spare:
            needed.append(spare.pop(0))
        counts.append(len(needed))
    return needed, counts[::-1]


def gelu(value):
    half = 0.5 * value
    return (half + half * jnp.tanh(value * (SLOPE + CUBIC * (value * value)))).astype(BF16)


def column(row, copies):
    count = row.shape[1]
    down = lax.broadcasted_iota(jnp.int32, (count, count), 0)
    across = lax.broadcasted_iota(jnp.int32, (count, count), 1)
    tall = jnp.sum(jnp.where(down == across, row, 0.0), axis=1, keepdims=True)
    return jnp.broadcast_to(jnp.concatenate([tall] * copies, axis=0), (count * copies, 128))


def spread(block, rows, columns):
    channels = block.shape[0]
    tall = jnp.concatenate([block] * (rows // channels), axis=0)
    down = lax.broadcasted_iota(jnp.int32, (channels, columns), 0)
    across = lax.broadcasted_iota(jnp.int32, (channels, columns), 1)
    pick = jnp.where(across % channels == down, 1.0, 0.0).astype(BF16)
    return jnp.dot(tall, pick, preferred_element_type=F32)


def prepare_kernel(slot_of, frames, conv, conv_shift, taps, tap_shift, mix, mix_shift, *outs):
    conv_out, conv_shift_out = outs[0], outs[1]
    tap_outs = outs[2 : 2 + LEVELS]
    tap_shift_out, mix_out, mix_shift_out = outs[2 + LEVELS :]
    channels, depth = conv.shape
    fields = depth // 27
    wide = 27 * GROUP * fields
    down = lax.broadcasted_iota(jnp.int32, (depth, wide), 0)
    across = lax.broadcasted_iota(jnp.int32, (depth, wide), 1)
    same = (down // fields == across // (GROUP * fields)) & (down % fields == across % fields)
    pick = jnp.where(same, 1.0, 0.0).astype(BF16)
    tall = jnp.concatenate([conv[...]] * GROUP, axis=0)
    full = jnp.dot(tall, pick, preferred_element_type=F32)
    down = lax.broadcasted_iota(jnp.int32, full.shape, 0)
    across = lax.broadcasted_iota(jnp.int32, full.shape, 1)
    keep = down // channels == across // fields % GROUP
    conv_out[...] = jnp.where(keep, full, 0.0).astype(BF16)
    conv_shift_out[...] = column(conv_shift[...], GROUP)
    slots = slot_of(lax.axis_index("tm"))
    for level in range(LEVELS):
        rows, columns = tap_outs[level].shape

        def frame_of(axis):
            place = lax.broadcasted_iota(jnp.int32, (rows, columns), axis) // channels
            block = place // frames
            start = jnp.zeros((rows, columns), jnp.int32)
            for index, slot in enumerate(slots[: (rows, columns)[axis] // channels // frames]):
                start = jnp.where(block == index, slot * frames, start)
            return start + place % frames

        gap = frame_of(1) - frame_of(0)
        total = jnp.zeros((rows, columns), F32)
        for tap in range(3):
            block = taps[level, :, tap * channels : (tap + 1) * channels]
            total = jnp.where(
                gap == (tap - 1) * 2**level, spread(block, rows, columns), total
            )
        tap_outs[level][...] = total.astype(BF16)
        tap_shift_out[level] = column(tap_shift[level : level + 1], GROUP)
        size = GROUP * channels
        down = lax.broadcasted_iota(jnp.int32, (size, size), 0)
        across = lax.broadcasted_iota(jnp.int32, (size, size), 1)
        full = spread(mix[level], size, size)
        mix_out[level] = jnp.where(down // channels == across // channels, full, 0.0).astype(BF16)
        mix_shift_out[level] = column(mix_shift[level : level + 1], GROUP)


def shifted(lines):
    plane = lines.shape[-1]
    depth = lax.broadcasted_iota(jnp.int32, (1, plane), 1) % NZ
    blank = jnp.zeros_like(lines)
    below = jnp.where(depth == 0, blank, pltpu.roll(lines, 1, 1))
    above = jnp.where(depth == NZ - 1, blank, pltpu.roll(lines, plane - 1, 1))
    for delta_y in (-1, 0, 1):
        for piece in (below, lines, above):
            yield pltpu.roll(piece, -delta_y * NZ % plane, 1) if delta_y else piece


def wide(shift, plane):
    return jnp.concatenate([shift] * (plane // 128), axis=1)


def encode_kernel(low, own, high, conv, conv_shift, *rest):
    taps = rest[:LEVELS]
    tap_shift, mix, mix_shift, out, patches = rest[LEVELS:]
    row_count, depth, plane = own.shape
    chunk = math.gcd(plane, 512)
    channels = out.shape[2]
    tall = GROUP * channels
    for index in range(row_count + 2):
        if index == 0:
            lines = low[...]
        elif index == row_count + 1:
            lines = high[...]
        else:
            lines = own[index - 1]
        for place, piece in enumerate(shifted(lines)):
            patches[index, place] = piece
    fields = conv.shape[1] // 27
    for row in range(row_count):
        for start in range(0, plane, chunk):
            cells = slice(start, start + chunk)
            parts = []
            for group in range(depth // fields):
                lines = patches[row : row + 3, :, group * fields : (group + 1) * fields, cells]
                summed = jnp.dot(
                    conv[...], lines.reshape(27 * fields, chunk), preferred_element_type=F32
                )
                parts.append(gelu(summed + wide(conv_shift[...], chunk)))
            hidden = jnp.concatenate(parts, axis=0)
            for level, tap in enumerate(taps):
                rows, columns = tap.shape
                summed = jnp.dot(tap[...], hidden[:columns], preferred_element_type=F32)
                parts = []
                for first in range(0, rows, tall):
                    size = min(tall, rows - first)
                    piece = summed[first : first + size]
                    gated = gelu(piece + wide(tap_shift[level, :size], chunk))
                    mixed = jnp.dot(
                        mix[level, :size, :size], gated, preferred_element_type=F32
                    )
                    current = hidden[first : first + size].astype(F32)
                    parts.append(
                        (current + mixed + wide(mix_shift[level, :size], chunk)).astype(BF16)
                    )
                hidden = jnp.concatenate(parts, axis=0)
            for frame in range(out.shape[0]):
                out[frame, row, :, cells] = hidden[frame * channels : (frame + 1) * channels]


VMEM = pl.BlockSpec(memory_space=pltpu.VMEM)
PARAMS = pltpu.CompilerParams(vmem_limit_bytes=40 * 2**20)


def ring(count, step):
    return [(index, (index + step) % count) for index in range(count)]


def shards(snapshots, conv_weight, conv_bias, tap_weight, tap_bias, mix_weight, mix_bias):
    frames, row_count, fields, plane = snapshots.shape
    channels = conv_weight.shape[0]
    times = lax.axis_size("tm")
    spaces = lax.axis_size("space")
    offsets, counts = frame_blocks(times, frames)
    paired = times == 4 and sorted(offsets) == [0, 1, 2, 3]
    tall = GROUP * channels

    if paired:
        offsets = [0, 2, 1, 3]
        across = [(index, index ^ 2) for index in range(times)]
        beside = [(index, index ^ 1) for index in range(times)]
        far = lax.ppermute(snapshots, "tm", across)
        near = lax.ppermute(snapshots, "tm", beside)
        both = lax.ppermute(far, "tm", beside)
        blocks = [snapshots, far, near, both]
        slot_of = lambda index: [index ^ offset for offset in offsets]
    else:
        blocks = [snapshots] + [
            lax.ppermute(snapshots, "tm", ring(times, -offset)) for offset in offsets[1:]
        ]
        slot_of = lambda index: [(index + offset) % times for offset in offsets]

    total = len(blocks) * frames
    rows = jnp.concatenate(blocks, axis=0).transpose(1, 0, 2, 3)
    rows = rows.reshape(row_count, total * fields, plane)

    conv_flat = conv_weight.transpose(0, 2, 3, 4, 1).reshape(channels, 27 * fields)
    tap_flat = tap_weight.reshape(LEVELS, channels, 3 * channels)
    shapes = [
        jax.ShapeDtypeStruct((tall, 27 * GROUP * fields), BF16),
        jax.ShapeDtypeStruct((tall, 128), F32),
    ]
    for level in range(LEVELS):
        shapes.append(
            jax.ShapeDtypeStruct(
                (
                    counts[level + 1] * frames * channels,
                    counts[level] * frames * channels,
                ),
                BF16,
            )
        )
    shapes += [
        jax.ShapeDtypeStruct((LEVELS, tall, 128), F32),
        jax.ShapeDtypeStruct((LEVELS, tall, tall), BF16),
        jax.ShapeDtypeStruct((LEVELS, tall, 128), F32),
    ]
    weights = pl.pallas_call(
        functools.partial(prepare_kernel, slot_of, frames),
        out_shape=shapes,
        in_specs=[VMEM] * 6,
        out_specs=[VMEM] * len(shapes),
        compiler_params=PARAMS,
        name="prepare",
    )(conv_flat, conv_bias.reshape(1, channels), tap_flat, tap_bias, mix_weight, mix_bias)

    if paired:
        core = lax.axis_index("tm") % 2
        message = jnp.where(core == 0, rows[row_count - 1], rows[0])
        pairs = []
        for time in range(times):
            for space in range(spaces):
                target = (space + 1 - 2 * (time % 2)) % spaces
                pairs.append((time * spaces + space, time * spaces + target))
        mine = lax.ppermute(message, ("tm", "space"), pairs)
        other = lax.ppermute(mine, "tm", beside)
        half = total * fields // 2
        other = jnp.concatenate([other[half:], other[:half]], axis=0)
        low = jnp.where(core == 0, mine, other)
        high = jnp.where(core == 0, other, mine)
    else:
        low = lax.ppermute(rows[row_count - 1], "space", ring(spaces, 1))
        high = lax.ppermute(rows[0], "space", ring(spaces, -1))

    return pl.pallas_call(
        encode_kernel,
        out_shape=jax.ShapeDtypeStruct((frames, row_count, channels, plane), BF16),
        in_specs=[VMEM] * (3 + len(weights)),
        out_specs=VMEM,
        scratch_shapes=[pltpu.VMEM((row_count + 2, 9, total * fields, plane), BF16)],
        compiler_params=PARAMS,
        name="encode",
    )(low, rows, high, *weights)


def solution(mesh):
    in_specs = (P("tm", "space", None, None), P(), P(), P(), P(), P(), P())
    out_specs = P("tm", "space", None, None)
    return jax.shard_map(shards, mesh=mesh, in_specs=in_specs, out_specs=out_specs, check_vma=False)
```

```python
import functools
import math

import jax
import jax.numpy as jnp
from jax import lax
from jax.experimental import pallas as pl
from jax.experimental.pallas import tpu as pltpu
from jax.sharding import PartitionSpec as P

LEVELS = 3
NZ = 32
GROUP = 4
CELLS = 256
SLOPE = math.sqrt(2.0 / math.pi)
CUBIC = SLOPE * 0.044715
BF16 = jnp.bfloat16
F32 = jnp.float32


def frame_blocks(axis_size, frames):
    needed = [0]
    counts = [1]
    for level in reversed(range(LEVELS)):
        reach = set()
        for offset in needed:
            for frame in range(frames):
                for step in (-(2**level), 2**level):
                    reach.add((offset + (frame + step) // frames) % axis_size)
        needed = needed + sorted(reach - set(needed))
        spare = [offset for offset in range(axis_size) if offset not in needed]
        while len(needed) * frames % GROUP and spare:
            needed.append(spare.pop(0))
        counts.append(len(needed))
    return needed, counts[::-1]


def gelu(value):
    half = 0.5 * value
    return (half + half * jnp.tanh(value * (SLOPE + CUBIC * (value * value)))).astype(BF16)


def column(row, copies):
    count = row.shape[1]
    down = lax.broadcasted_iota(jnp.int32, (count, count), 0)
    across = lax.broadcasted_iota(jnp.int32, (count, count), 1)
    tall = jnp.sum(jnp.where(down == across, row, 0.0), axis=1, keepdims=True)
    return jnp.broadcast_to(jnp.concatenate([tall] * copies, axis=0), (count * copies, 128))


def spread(block, rows, columns):
    channels = block.shape[0]
    tall = jnp.concatenate([block] * (rows // channels), axis=0)
    down = lax.broadcasted_iota(jnp.int32, (channels, columns), 0)
    across = lax.broadcasted_iota(jnp.int32, (channels, columns), 1)
    pick = jnp.where(across % channels == down, 1.0, 0.0).astype(BF16)
    return jnp.dot(tall, pick, preferred_element_type=F32)


def prepare_kernel(slot_of, frames, own, conv, conv_shift, taps, tap_shift, mix, mix_shift, *outs):
    outs[0][...] = own[...]
    outs = outs[1:]
    conv_out, conv_shift_out = outs[0], outs[1]
    tap_outs = outs[2 : 2 + LEVELS]
    tap_shift_out, mix_out, mix_shift_out = outs[2 + LEVELS :]
    channels, depth = conv.shape
    fields = depth // 27
    wide = 27 * GROUP * fields
    down = lax.broadcasted_iota(jnp.int32, (depth, wide), 0)
    across = lax.broadcasted_iota(jnp.int32, (depth, wide), 1)
    same = (down // fields == across // (GROUP * fields)) & (down % fields == across % fields)
    pick = jnp.where(same, 1.0, 0.0).astype(BF16)
    tall = jnp.concatenate([conv[...]] * GROUP, axis=0)
    full = jnp.dot(tall, pick, preferred_element_type=F32)
    down = lax.broadcasted_iota(jnp.int32, full.shape, 0)
    across = lax.broadcasted_iota(jnp.int32, full.shape, 1)
    keep = down // channels == across // fields % GROUP
    conv_out[...] = jnp.where(keep, full, 0.0).astype(BF16)
    conv_shift_out[...] = column(conv_shift[...], GROUP)
    slots = slot_of(lax.axis_index("tm"))
    for level in range(LEVELS):
        rows, columns = tap_outs[level].shape

        def frame_of(axis):
            place = lax.broadcasted_iota(jnp.int32, (rows, columns), axis) // channels
            block = place // frames
            start = jnp.zeros((rows, columns), jnp.int32)
            for index, slot in enumerate(slots[: (rows, columns)[axis] // channels // frames]):
                start = jnp.where(block == index, slot * frames, start)
            return start + place % frames

        gap = frame_of(1) - frame_of(0)
        total = jnp.zeros((rows, columns), F32)
        for tap in range(3):
            block = taps[level, :, tap * channels : (tap + 1) * channels]
            total = jnp.where(
                gap == (tap - 1) * 2**level, spread(block, rows, columns), total
            )
        tap_outs[level][...] = total.astype(BF16)
        tap_shift_out[level] = column(tap_shift[level : level + 1], GROUP)
        size = GROUP * channels
        down = lax.broadcasted_iota(jnp.int32, (size, size), 0)
        across = lax.broadcasted_iota(jnp.int32, (size, size), 1)
        full = spread(mix[level], size, size)
        mix_out[level] = jnp.where(down // channels == across // channels, full, 0.0).astype(BF16)
        mix_shift_out[level] = column(mix_shift[level : level + 1], GROUP)


def shifted(lines):
    plane = lines.shape[-1]
    depth = lax.broadcasted_iota(jnp.int32, (1, plane), 1) % NZ
    blank = jnp.zeros_like(lines)
    below = jnp.where(depth == 0, blank, pltpu.roll(lines, 1, 1))
    above = jnp.where(depth == NZ - 1, blank, pltpu.roll(lines, plane - 1, 1))
    for delta_y in (-1, 0, 1):
        for piece in (below, lines, above):
            yield pltpu.roll(piece, -delta_y * NZ % plane, 1) if delta_y else piece


def joined(parts, axis):
    return parts[0] if len(parts) == 1 else jnp.concatenate(parts, axis=axis)


def wide(shift, cells):
    return joined([shift] * (cells // 128), 1)


def encode(windows, weights, frames, store):
    conv, conv_shift = weights[:2]
    taps = weights[2 : 2 + LEVELS]
    tap_shift, mix, mix_shift = weights[2 + LEVELS :]
    tall = conv.shape[0]
    channels = tall // GROUP
    groups = taps[0].shape[1] // tall
    hidden = []
    for window in windows:
        parts = []
        for group in range(groups):
            summed = jnp.dot(conv[...], window(group), preferred_element_type=F32)
            parts.append(gelu(summed + wide(conv_shift[...], summed.shape[1])))
        hidden.append(joined(parts, 0))
    for level, tap in enumerate(taps):
        rows, columns = tap.shape
        later = []
        for current in hidden:
            cells = current.shape[1]
            summed = jnp.dot(tap[...], current[:columns], preferred_element_type=F32)
            parts = []
            for first in range(0, rows, tall):
                size = min(tall, rows - first)
                piece = summed[first : first + size]
                gated = gelu(piece + wide(tap_shift[level, :size], cells))
                mixed = jnp.dot(mix[level, :size, :size], gated, preferred_element_type=F32)
                kept = current[first : first + size].astype(F32)
                parts.append((kept + mixed + wide(mix_shift[level, :size], cells)).astype(BF16))
            later.append(joined(parts, 0))
        hidden = later
    for index, final in enumerate(hidden):
        for frame in range(frames):
            store(index, frame, final[frame * channels : (frame + 1) * channels])


def stack(sources, group, depth, cells):
    part = slice(group * depth, (group + 1) * depth)
    return jnp.concatenate(
        [source[:, part, cells].reshape(9 * depth, -1) for source in sources], axis=0
    )


def inner_kernel(rows, *rest):
    weights, (patches, out) = rest[:-2], rest[-2:]
    row_count, _, plane = rows.shape
    depth = weights[0].shape[1] // 27
    width = math.gcd(plane, CELLS)
    for index in range(row_count):
        for place, piece in enumerate(shifted(rows[index])):
            patches[index, place] = piece
    places = [
        (row, slice(start, start + width))
        for row in range(1, row_count - 1)
        for start in range(0, plane, width)
    ]
    windows = [
        functools.partial(
            stack, [patches.at[row + step] for step in (-1, 0, 1)], depth=depth, cells=cells
        )
        for row, cells in places
    ]

    def store(index, frame, final):
        row, cells = places[index]
        out[frame, row - 1, :, cells] = final

    encode(windows, weights, out.shape[0], store)


def outer_kernel(paired, mine, other, patches, inner, *rest):
    weights, (out, edges, borders, sems) = rest[:-4], rest[-4:]
    row_count, _, lines, plane = patches.shape
    depth = weights[0].shape[1] // 27
    width = math.gcd(plane, CELLS)
    middle = pltpu.make_async_copy(inner, out.at[:, 1 : row_count - 1], sems.at[0])
    middle.start()
    first, second = mine[...], other[...]
    if paired:
        half = lines // 2
        second = jnp.concatenate([second[half:], second[:half]], axis=0)
        parity = lax.rem(lax.axis_index("space") + lax.axis_index("tm"), 2)
        first, second = (
            jnp.where(parity == 0, first, second),
            jnp.where(parity == 0, second, first),
        )
    for index, halo in enumerate((first, second)):
        for place, piece in enumerate(shifted(halo)):
            borders[index, place] = piece
    sources = [
        [borders.at[0], patches.at[0], patches.at[1]],
        [patches.at[row_count - 2], patches.at[row_count - 1], borders.at[1]],
    ]
    places = [
        (edge, slice(start, start + width)) for edge in range(2) for start in range(0, plane, width)
    ]
    windows = [
        functools.partial(stack, sources[edge], depth=depth, cells=cells) for edge, cells in places
    ]

    def store(index, frame, final):
        edge, cells = places[index]
        edges[frame, edge, :, cells] = final

    encode(windows, weights, out.shape[0], store)
    copies = [
        pltpu.make_async_copy(edges.at[:, edge], out.at[:, row], sems.at[edge + 1])
        for edge, row in ((0, 0), (1, row_count - 1))
    ]
    for copy in copies:
        copy.start()
    middle.wait()
    for copy in copies:
        copy.wait()


VMEM = pl.BlockSpec(memory_space=pltpu.VMEM)
PARAMS = pltpu.CompilerParams(vmem_limit_bytes=40 * 2**20)


def ring(count, step):
    return [(index, (index + step) % count) for index in range(count)]


def shards(snapshots, conv_weight, conv_bias, tap_weight, tap_bias, mix_weight, mix_bias):
    frames, row_count, fields, plane = snapshots.shape
    channels = conv_weight.shape[0]
    times = lax.axis_size("tm")
    spaces = lax.axis_size("space")
    offsets, counts = frame_blocks(times, frames)
    paired = times == 4 and sorted(offsets) == [0, 1, 2, 3] and spaces % 2 == 0
    tall = GROUP * channels
    total = len(offsets) * frames * fields

    if paired:
        offsets = [0, 2, 1, 3]
        slot_of = lambda index: [index ^ offset for offset in offsets]
    else:
        slot_of = lambda index: [(index + offset) % times for offset in offsets]

    conv_flat = conv_weight.transpose(0, 2, 3, 4, 1).reshape(channels, 27 * fields)
    tap_flat = tap_weight.reshape(LEVELS, channels, 3 * channels)
    shapes = [
        jax.ShapeDtypeStruct(snapshots.shape, BF16),
        jax.ShapeDtypeStruct((tall, 27 * GROUP * fields), BF16),
        jax.ShapeDtypeStruct((tall, 128), F32),
    ]
    for level in range(LEVELS):
        rows, columns = counts[level + 1], counts[level]
        shapes.append(
            jax.ShapeDtypeStruct((rows * frames * channels, columns * frames * channels), BF16)
        )
    shapes += [
        jax.ShapeDtypeStruct((LEVELS, tall, 128), F32),
        jax.ShapeDtypeStruct((LEVELS, tall, tall), BF16),
        jax.ShapeDtypeStruct((LEVELS, tall, 128), F32),
    ]
    own, *weights = pl.pallas_call(
        functools.partial(prepare_kernel, slot_of, frames),
        out_shape=shapes,
        in_specs=[VMEM] * 7,
        out_specs=[VMEM] * len(shapes),
        compiler_params=PARAMS,
        name="prepare",
    )(
        snapshots,
        conv_flat,
        conv_bias.reshape(1, channels),
        tap_flat,
        tap_bias,
        mix_weight,
        mix_bias,
    )

    if paired:
        across = [(index, index ^ 2) for index in range(times)]
        beside = [(index, index ^ 1) for index in range(times)]
        far = lax.ppermute(snapshots, "tm", across)
        near = lax.ppermute(snapshots, "tm", beside)
        far, own, *weights = lax.optimization_barrier((far, own, *weights))
        both = lax.ppermute(far, "tm", beside)
        blocks = [own, far, near, both]
    else:
        blocks = [own] + [
            lax.ppermute(snapshots, "tm", ring(times, -offset)) for offset in offsets[1:]
        ]

    if paired:
        parity = (lax.axis_index("space") + lax.axis_index("tm")) % 2
        message = jnp.concatenate(
            [jnp.where(parity == 0, block[:, 0], block[:, -1]) for block in blocks], axis=0
        )
        message = message.reshape(total, plane)
        pairs = []
        for time in range(times):
            for space in range(spaces):
                step = -1 if (space + time) % 2 == 0 else 1
                target = (space + step) % spaces
                pairs.append((time * spaces + space, time * spaces + target))
        mine = lax.ppermute(message, ("tm", "space"), pairs)

    rows = jnp.concatenate(blocks, axis=0).transpose(1, 0, 2, 3).reshape(row_count, total, plane)
    patches, inner = pl.pallas_call(
        inner_kernel,
        out_shape=[
            jax.ShapeDtypeStruct((row_count, 9, total, plane), BF16),
            jax.ShapeDtypeStruct((frames, row_count - 2, channels, plane), BF16),
        ],
        in_specs=[VMEM] * (1 + len(weights)),
        out_specs=[VMEM] * 2,
        compiler_params=PARAMS,
        name="inner",
    )(rows, *weights)

    if paired:
        mine, patches, inner = lax.optimization_barrier((mine, patches, inner))
        other = lax.ppermute(mine, "tm", beside)
    else:
        mine = lax.ppermute(rows[row_count - 1], "space", ring(spaces, 1))
        other = lax.ppermute(rows[0], "space", ring(spaces, -1))

    return pl.pallas_call(
        functools.partial(outer_kernel, paired),
        out_shape=jax.ShapeDtypeStruct((frames, row_count, channels, plane), BF16),
        in_specs=[VMEM] * (4 + len(weights)),
        out_specs=pl.BlockSpec(memory_space=pl.ANY),
        scratch_shapes=[
            pltpu.VMEM((frames, 2, channels, plane), BF16),
            pltpu.VMEM((2, 9, total, plane), BF16),
            pltpu.SemaphoreType.DMA((3,)),
        ],
        compiler_params=PARAMS,
        name="outer",
    )(mine, other, patches, inner, *weights)


def solution(mesh):
    in_specs = (P("tm", "space", None, None), P(), P(), P(), P(), P(), P())
    out_specs = P("tm", "space", None, None)
    return jax.shard_map(shards, mesh=mesh, in_specs=in_specs, out_specs=out_specs, check_vma=False)
```

```python
import functools
import math

import jax
import jax.numpy as jnp
from jax import lax
from jax.experimental import pallas as pl
from jax.experimental.pallas import tpu as pltpu
from jax.sharding import PartitionSpec as P

LEVELS = 3
NZ = 32
GROUP = 4
CELLS = 256
SLOPE = math.sqrt(2.0 / math.pi)
CUBIC = SLOPE * 0.044715
BF16 = jnp.bfloat16
F32 = jnp.float32


def frame_blocks(axis_size, frames):
    needed = [0]
    counts = [1]
    for level in reversed(range(LEVELS)):
        reach = set()
        for offset in needed:
            for frame in range(frames):
                for step in (-(2**level), 2**level):
                    reach.add((offset + (frame + step) // frames) % axis_size)
        needed = needed + sorted(reach - set(needed))
        spare = [offset for offset in range(axis_size) if offset not in needed]
        while len(needed) * frames % GROUP and spare:
            needed.append(spare.pop(0))
        counts.append(len(needed))
    return needed, counts[::-1]


def gelu(value):
    half = 0.5 * value
    return (half + half * jnp.tanh(value * (SLOPE + CUBIC * (value * value)))).astype(BF16)


def column(row, copies):
    count = row.shape[1]
    down = lax.broadcasted_iota(jnp.int32, (count, count), 0)
    across = lax.broadcasted_iota(jnp.int32, (count, count), 1)
    tall = jnp.sum(jnp.where(down == across, row, 0.0), axis=1, keepdims=True)
    return jnp.broadcast_to(jnp.concatenate([tall] * copies, axis=0), (count * copies, 128))


def spread(block, rows, columns):
    channels = block.shape[0]
    tall = jnp.concatenate([block] * (rows // channels), axis=0)
    down = lax.broadcasted_iota(jnp.int32, (channels, columns), 0)
    across = lax.broadcasted_iota(jnp.int32, (channels, columns), 1)
    pick = jnp.where(across % channels == down, 1.0, 0.0).astype(BF16)
    return jnp.dot(tall, pick, preferred_element_type=F32)


def prepare_kernel(slot_of, *refs):
    sources, outs, landed, sems = refs[:7], refs[7:-7], refs[-7:-1], refs[-1]
    copies = [
        pltpu.make_async_copy(source, target, sems.at[index])
        for index, (source, target) in enumerate(zip(sources, (outs[0], *landed)))
    ]
    for copy in copies:
        copy.start()
    for copy in copies:
        copy.wait()
    conv, conv_shift, taps, tap_shift, mix, mix_shift = landed
    frames = outs[0].shape[0]
    conv_out, conv_shift_out = outs[1], outs[2]
    tap_outs = outs[3 : 3 + LEVELS]
    tap_shift_out, mix_out, mix_shift_out = outs[3 + LEVELS :]
    places, fields, channels = conv.shape
    depth = places * fields
    wide = depth * GROUP
    flat = conv[...].astype(F32).reshape(depth, channels).astype(BF16)
    down = lax.broadcasted_iota(jnp.int32, (depth, wide), 0)
    across = lax.broadcasted_iota(jnp.int32, (depth, wide), 1)
    same = (down // fields == across // (GROUP * fields)) & (down % fields == across % fields)
    pick = jnp.where(same, 1.0, 0.0).astype(BF16)
    full = lax.dot_general(flat, pick, (((0,), (0,)), ((), ())), preferred_element_type=F32)
    full = jnp.concatenate([full] * GROUP, axis=0)
    down = lax.broadcasted_iota(jnp.int32, full.shape, 0)
    across = lax.broadcasted_iota(jnp.int32, full.shape, 1)
    keep = down // channels == across // fields % GROUP
    conv_out[...] = jnp.where(keep, full, 0.0).astype(BF16)
    conv_shift_out[...] = column(conv_shift[...], GROUP)
    slots = slot_of(lax.axis_index("tm"))
    for level in range(LEVELS):
        rows, columns = tap_outs[level].shape

        def frame_of(axis):
            place = lax.broadcasted_iota(jnp.int32, (rows, columns), axis) // channels
            block = place // frames
            start = jnp.zeros((rows, columns), jnp.int32)
            for index, slot in enumerate(slots[: (rows, columns)[axis] // channels // frames]):
                start = jnp.where(block == index, slot * frames, start)
            return start + place % frames

        gap = frame_of(1) - frame_of(0)
        total = jnp.zeros((rows, columns), F32)
        for tap in range(3):
            block = spread(taps[level, tap], rows, columns)
            total = jnp.where(gap == (tap - 1) * 2**level, block, total)
        tap_outs[level][...] = total.astype(BF16)
        tap_shift_out[level] = column(tap_shift[level : level + 1], GROUP)
        size = GROUP * channels
        down = lax.broadcasted_iota(jnp.int32, (size, size), 0)
        across = lax.broadcasted_iota(jnp.int32, (size, size), 1)
        full = spread(mix[level], size, size)
        mix_out[level] = jnp.where(down // channels == across // channels, full, 0.0).astype(BF16)
        mix_shift_out[level] = column(mix_shift[level : level + 1], GROUP)


def shifted(lines):
    plane = lines.shape[-1]
    depth = lax.broadcasted_iota(jnp.int32, (1, plane), 1) % NZ
    blank = jnp.zeros_like(lines)
    below = jnp.where(depth == 0, blank, pltpu.roll(lines, 1, 1))
    above = jnp.where(depth == NZ - 1, blank, pltpu.roll(lines, plane - 1, 1))
    for delta_y in (-1, 0, 1):
        for piece in (below, lines, above):
            yield pltpu.roll(piece, -delta_y * NZ % plane, 1) if delta_y else piece


def parity():
    return lax.rem(lax.axis_index("space") + lax.axis_index("tm"), 2)


def joined(parts, axis):
    return parts[0] if len(parts) == 1 else jnp.concatenate(parts, axis=axis)


def wide(shift, cells):
    return joined([shift] * (cells // 128), 1)


def encode(windows, weights, frames, store):
    conv, conv_shift = weights[:2]
    taps = weights[2 : 2 + LEVELS]
    tap_shift, mix, mix_shift = weights[2 + LEVELS :]
    tall = conv.shape[0]
    channels = tall // GROUP
    groups = taps[0].shape[1] // tall
    hidden = []
    for window in windows:
        parts = []
        for group in range(groups):
            summed = jnp.dot(conv[...], window(group), preferred_element_type=F32)
            parts.append(gelu(summed + wide(conv_shift[...], summed.shape[1])))
        hidden.append(joined(parts, 0))
    for level, tap in enumerate(taps):
        rows, columns = tap.shape
        later = []
        for current in hidden:
            cells = current.shape[1]
            summed = jnp.dot(tap[...], current[:columns], preferred_element_type=F32)
            parts = []
            for first in range(0, rows, tall):
                size = min(tall, rows - first)
                piece = summed[first : first + size]
                gated = gelu(piece + wide(tap_shift[level, :size], cells))
                mixed = jnp.dot(mix[level, :size, :size], gated, preferred_element_type=F32)
                kept = current[first : first + size].astype(F32)
                parts.append((kept + mixed + wide(mix_shift[level, :size], cells)).astype(BF16))
            later.append(joined(parts, 0))
        hidden = later
    for index, final in enumerate(hidden):
        for frame in range(frames):
            store(index, frame, final[frame * channels : (frame + 1) * channels])


def stack(sources, group, depth, cells):
    part = slice(group * depth, (group + 1) * depth)
    return jnp.concatenate(
        [source[:, part, cells].reshape(9 * depth, -1) for source in sources], axis=0
    )


def pack_kernel(*refs):
    blocks, out = refs[:-1], refs[-1]
    frames, row_count = blocks[0].shape[:2]
    first, last = [
        jnp.concatenate([block[frame, row] for block in blocks for frame in range(frames)], axis=0)
        for row in (0, row_count - 1)
    ]
    out[...] = jnp.where(parity() == 0, first, last)


def inner_kernel(count, *rest):
    blocks, weights, (patches, out) = rest[:count], rest[count:-2], rest[-2:]
    frames, row_count, _, plane = blocks[0].shape
    depth = weights[0].shape[1] // 27
    width = math.gcd(plane, CELLS)
    for index in range(row_count):
        lines = [block[frame, index] for block in blocks for frame in range(frames)]
        for place, piece in enumerate(shifted(jnp.concatenate(lines, axis=0))):
            patches[index, place] = piece
    places = [
        (row, slice(start, start + width))
        for row in range(1, row_count - 1)
        for start in range(0, plane, width)
    ]
    windows = [
        functools.partial(
            stack, [patches.at[row + step] for step in (-1, 0, 1)], depth=depth, cells=cells
        )
        for row, cells in places
    ]

    def store(index, frame, final):
        row, cells = places[index]
        out[frame, row - 1, :, cells] = final

    encode(windows, weights, out.shape[0], store)


def outer_kernel(paired, mine, other, patches, inner, *rest):
    weights, (out, edges, borders, sems) = rest[:-4], rest[-4:]
    row_count, _, lines, plane = patches.shape
    depth = weights[0].shape[1] // 27
    width = math.gcd(plane, CELLS)
    middle = pltpu.make_async_copy(inner, out.at[:, 1 : row_count - 1], sems.at[0])
    middle.start()
    first, second = mine[...], other[...]
    if paired:
        half = lines // 2
        second = jnp.concatenate([second[half:], second[:half]], axis=0)
        below = parity() == 0
        first, second = jnp.where(below, first, second), jnp.where(below, second, first)
    for index, halo in enumerate((first, second)):
        for place, piece in enumerate(shifted(halo)):
            borders[index, place] = piece
    sources = [
        [borders.at[0], patches.at[0], patches.at[1]],
        [patches.at[row_count - 2], patches.at[row_count - 1], borders.at[1]],
    ]
    places = [
        (edge, slice(start, start + width)) for edge in range(2) for start in range(0, plane, width)
    ]
    windows = [
        functools.partial(stack, sources[edge], depth=depth, cells=cells) for edge, cells in places
    ]

    def store(index, frame, final):
        edge, cells = places[index]
        edges[frame, edge, :, cells] = final

    encode(windows, weights, out.shape[0], store)
    copies = [
        pltpu.make_async_copy(edges.at[:, edge], out.at[:, row], sems.at[edge + 1])
        for edge, row in ((0, 0), (1, row_count - 1))
    ]
    for copy in copies:
        copy.start()
    middle.wait()
    for copy in copies:
        copy.wait()


VMEM = pl.BlockSpec(memory_space=pltpu.VMEM)
PARAMS = pltpu.CompilerParams(vmem_limit_bytes=40 * 2**20)


def ring(count, step):
    return [(index, (index + step) % count) for index in range(count)]


def shards(snapshots, conv_weight, conv_bias, tap_weight, tap_bias, mix_weight, mix_bias):
    frames, row_count, fields, plane = snapshots.shape
    channels = conv_weight.shape[0]
    times = lax.axis_size("tm")
    spaces = lax.axis_size("space")
    offsets, counts = frame_blocks(times, frames)
    paired = times == 4 and sorted(offsets) == [0, 1, 2, 3] and spaces % 2 == 0
    tall = GROUP * channels
    total = len(offsets) * frames * fields

    if paired:
        offsets = [0, 2, 1, 3]
        slot_of = lambda index: [index ^ offset for offset in offsets]
    else:
        slot_of = lambda index: [(index + offset) % times for offset in offsets]

    shapes = [
        jax.ShapeDtypeStruct(snapshots.shape, BF16),
        jax.ShapeDtypeStruct((tall, 27 * GROUP * fields), BF16),
        jax.ShapeDtypeStruct((tall, 128), F32),
    ]
    for level in range(LEVELS):
        rows, columns = counts[level + 1], counts[level]
        shapes.append(
            jax.ShapeDtypeStruct((rows * frames * channels, columns * frames * channels), BF16)
        )
    shapes += [
        jax.ShapeDtypeStruct((LEVELS, tall, 128), F32),
        jax.ShapeDtypeStruct((LEVELS, tall, tall), BF16),
        jax.ShapeDtypeStruct((LEVELS, tall, 128), F32),
    ]
    sources = [
        snapshots,
        conv_weight.transpose(2, 3, 4, 1, 0).reshape(27, fields, channels),
        conv_bias.reshape(1, channels),
        tap_weight.transpose(0, 2, 1, 3),
        tap_bias,
        mix_weight,
        mix_bias,
    ]
    sources = [pltpu.with_memory_space_constraint(source, pltpu.HBM) for source in sources]
    own, *weights = pl.pallas_call(
        functools.partial(prepare_kernel, slot_of),
        out_shape=shapes,
        in_specs=[pl.BlockSpec(memory_space=pl.ANY)] * len(sources),
        out_specs=[VMEM] * len(shapes),
        scratch_shapes=[pltpu.VMEM(source.shape, source.dtype) for source in sources[1:]]
        + [pltpu.SemaphoreType.DMA((len(sources),))],
        compiler_params=PARAMS,
        name="prepare",
    )(*sources)

    if paired:
        across = [(index, index ^ 2) for index in range(times)]
        beside = [(index, index ^ 1) for index in range(times)]
        far = lax.ppermute(snapshots, "tm", across)
        near = lax.ppermute(snapshots, "tm", beside)
        far, own, *weights = lax.optimization_barrier((far, own, *weights))
        both = lax.ppermute(far, "tm", beside)
        blocks = [own, far, near, both]
    else:
        blocks = [own] + [
            lax.ppermute(snapshots, "tm", ring(times, -offset)) for offset in offsets[1:]
        ]

    if paired:
        message = pl.pallas_call(
            pack_kernel,
            out_shape=jax.ShapeDtypeStruct((total, plane), BF16),
            in_specs=[VMEM] * len(blocks),
            out_specs=VMEM,
            compiler_params=PARAMS,
            name="pack",
        )(*blocks)
        pairs = []
        for time in range(times):
            for space in range(spaces):
                step = -1 if (space + time) % 2 == 0 else 1
                target = (space + step) % spaces
                pairs.append((time * spaces + space, time * spaces + target))
        mine = lax.ppermute(message, ("tm", "space"), pairs)

    patches, inner = pl.pallas_call(
        functools.partial(inner_kernel, len(blocks)),
        out_shape=[
            jax.ShapeDtypeStruct((row_count, 9, total, plane), BF16),
            jax.ShapeDtypeStruct((frames, row_count - 2, channels, plane), BF16),
        ],
        in_specs=[VMEM] * (len(blocks) + len(weights)),
        out_specs=[VMEM] * 2,
        compiler_params=PARAMS,
        name="inner",
    )(*blocks, *weights)

    if paired:
        mine, patches, inner = lax.optimization_barrier((mine, patches, inner))
        other = lax.ppermute(mine, "tm", beside)
    else:
        low, high = [
            jnp.concatenate([block[:, row] for block in blocks], axis=0).reshape(total, plane)
            for row in (0, row_count - 1)
        ]
        mine = lax.ppermute(high, "space", ring(spaces, 1))
        other = lax.ppermute(low, "space", ring(spaces, -1))

    return pl.pallas_call(
        functools.partial(outer_kernel, paired),
        out_shape=jax.ShapeDtypeStruct((frames, row_count, channels, plane), BF16),
        in_specs=[VMEM] * (4 + len(weights)),
        out_specs=pl.BlockSpec(memory_space=pl.ANY),
        scratch_shapes=[
            pltpu.VMEM((frames, 2, channels, plane), BF16),
            pltpu.VMEM((2, 9, total, plane), BF16),
            pltpu.SemaphoreType.DMA((3,)),
        ],
        compiler_params=PARAMS,
        name="outer",
    )(mine, other, patches, inner, *weights)


def solution(mesh):
    in_specs = (P("tm", "space", None, None), P(), P(), P(), P(), P(), P())
    out_specs = P("tm", "space", None, None)
    return jax.shard_map(shards, mesh=mesh, in_specs=in_specs, out_specs=out_specs, check_vma=False)
```

```python
import functools
import math

import jax
import jax.numpy as jnp
from jax import lax
from jax.experimental import pallas as pl
from jax.experimental.pallas import tpu as pltpu
from jax.sharding import PartitionSpec as P

LEVELS = 3
NZ = 32
GROUP = 4
CELLS = 256
SLOPE = math.sqrt(2.0 / math.pi)
CUBIC = SLOPE * 0.044715
BF16 = jnp.bfloat16
F32 = jnp.float32


def frame_blocks(axis_size, frames):
    needed = [0]
    counts = [1]
    for level in reversed(range(LEVELS)):
        reach = set()
        for offset in needed:
            for frame in range(frames):
                for step in (-(2**level), 2**level):
                    reach.add((offset + (frame + step) // frames) % axis_size)
        needed = needed + sorted(reach - set(needed))
        spare = [offset for offset in range(axis_size) if offset not in needed]
        while len(needed) * frames % GROUP and spare:
            needed.append(spare.pop(0))
        counts.append(len(needed))
    return needed, counts[::-1]


def gelu(value):
    half = 0.5 * value
    return (half + half * jnp.tanh(value * (SLOPE + CUBIC * (value * value)))).astype(BF16)


def column(row, copies):
    count = row.shape[1]
    down = lax.broadcasted_iota(jnp.int32, (count, count), 0)
    across = lax.broadcasted_iota(jnp.int32, (count, count), 1)
    tall = jnp.sum(jnp.where(down == across, row, 0.0), axis=1, keepdims=True)
    return jnp.broadcast_to(jnp.concatenate([tall] * copies, axis=0), (count * copies, 128))


def spread(block, rows, columns):
    channels = block.shape[0]
    tall = jnp.concatenate([block] * (rows // channels), axis=0)
    down = lax.broadcasted_iota(jnp.int32, (channels, columns), 0)
    across = lax.broadcasted_iota(jnp.int32, (channels, columns), 1)
    pick = jnp.where(across % channels == down, 1.0, 0.0).astype(BF16)
    return jnp.dot(tall, pick, preferred_element_type=F32)


def prepare_kernel(paired, slot_of, *refs):
    sources, outs, landed, sems = refs[:7], refs[7:-7], refs[-7:-1], refs[-1]
    copies = [
        pltpu.make_async_copy(source, target, sems.at[index])
        for index, (source, target) in enumerate(zip(sources, (outs[0], *landed)))
    ]
    for copy in copies:
        copy.start()
    for copy in copies:
        copy.wait()
    conv, conv_shift, taps, tap_shift, mix, mix_shift = landed
    frames = outs[0].shape[0]
    conv_outs, conv_shift_out = outs[1:4], outs[4]
    tap_outs = outs[5 : 5 + LEVELS]
    tap_shift_out, mix_out, mix_shift_out = outs[5 + LEVELS :]
    places, fields, channels = conv.shape
    depth = places * fields
    wide = depth * GROUP
    flat = conv[...].astype(F32).reshape(depth, channels).astype(BF16)
    down = lax.broadcasted_iota(jnp.int32, (depth, wide), 0)
    across = lax.broadcasted_iota(jnp.int32, (depth, wide), 1)
    same = (down // fields == across // (GROUP * fields)) & (down % fields == across % fields)
    pick = jnp.where(same, 1.0, 0.0).astype(BF16)
    full = lax.dot_general(flat, pick, (((0,), (0,)), ((), ())), preferred_element_type=F32)
    full = jnp.concatenate([full] * GROUP, axis=0)
    down = lax.broadcasted_iota(jnp.int32, full.shape, 0)
    across = lax.broadcasted_iota(jnp.int32, full.shape, 1)
    keep = down // channels == across // fields % GROUP
    full = jnp.where(keep, full, 0.0)
    third = wide // 3
    turned = jnp.concatenate([full[:, 2 * third :], full[:, third : -third], full[:, :third]], axis=1)
    even = parity(paired) == 0
    conv_outs[0][...] = full.astype(BF16)
    conv_outs[1][...] = jnp.where(even, full, turned).astype(BF16)
    conv_outs[2][...] = jnp.where(even, turned, full).astype(BF16)
    conv_shift_out[...] = column(conv_shift[...], GROUP)
    slots = slot_of(lax.axis_index("tm"))
    for level in range(LEVELS):
        rows, columns = tap_outs[level].shape

        def frame_of(axis):
            place = lax.broadcasted_iota(jnp.int32, (rows, columns), axis) // channels
            block = place // frames
            start = jnp.zeros((rows, columns), jnp.int32)
            for index, slot in enumerate(slots[: (rows, columns)[axis] // channels // frames]):
                start = jnp.where(block == index, slot * frames, start)
            return start + place % frames

        gap = frame_of(1) - frame_of(0)
        total = jnp.zeros((rows, columns), F32)
        for tap in range(3):
            block = spread(taps[level, tap], rows, columns)
            total = jnp.where(gap == (tap - 1) * 2**level, block, total)
        tap_outs[level][...] = total.astype(BF16)
        tap_shift_out[level] = column(tap_shift[level : level + 1], GROUP)
        size = GROUP * channels
        down = lax.broadcasted_iota(jnp.int32, (size, size), 0)
        across = lax.broadcasted_iota(jnp.int32, (size, size), 1)
        full = spread(mix[level], size, size)
        mix_out[level] = jnp.where(down // channels == across // channels, full, 0.0).astype(BF16)
        mix_shift_out[level] = column(mix_shift[level : level + 1], GROUP)


def shifted(lines):
    plane = lines.shape[-1]
    depth = lax.broadcasted_iota(jnp.int32, (1, plane), 1) % NZ
    blank = jnp.zeros_like(lines)
    below = jnp.where(depth == 0, blank, pltpu.roll(lines, 1, 1))
    above = jnp.where(depth == NZ - 1, blank, pltpu.roll(lines, plane - 1, 1))
    for delta_y in (-1, 0, 1):
        for piece in (below, lines, above):
            yield pltpu.roll(piece, -delta_y * NZ % plane, 1) if delta_y else piece


def parity(paired):
    return lax.rem(lax.axis_index("space"), 2) if paired else 0


def joined(parts, axis):
    return parts[0] if len(parts) == 1 else jnp.concatenate(parts, axis=axis)


def wide(shift, cells):
    return joined([shift] * (cells // 128), 1)


def encode(windows, weights, frames, store):
    conv, conv_shift = weights[:2]
    taps = weights[2 : 2 + LEVELS]
    tap_shift, mix, mix_shift = weights[2 + LEVELS :]
    tall = conv.shape[0]
    channels = tall // GROUP
    groups = taps[0].shape[1] // tall
    hidden = []
    for window in windows:
        parts = []
        for group in range(groups):
            summed = jnp.dot(conv[...], window(group), preferred_element_type=F32)
            parts.append(gelu(summed + wide(conv_shift[...], summed.shape[1])))
        hidden.append(joined(parts, 0))
    for level, tap in enumerate(taps):
        rows, columns = tap.shape
        later = []
        for current in hidden:
            cells = current.shape[1]
            summed = jnp.dot(tap[...], current[:columns], preferred_element_type=F32)
            parts = []
            for first in range(0, rows, tall):
                size = min(tall, rows - first)
                piece = summed[first : first + size]
                gated = gelu(piece + wide(tap_shift[level, :size], cells))
                mixed = jnp.dot(mix[level, :size, :size], gated, preferred_element_type=F32)
                kept = current[first : first + size].astype(F32)
                parts.append((kept + mixed + wide(mix_shift[level, :size], cells)).astype(BF16))
            later.append(joined(parts, 0))
        hidden = later
    for index, final in enumerate(hidden):
        for frame in range(frames):
            store(index, frame, final[frame * channels : (frame + 1) * channels])


def stack(sources, group, depth, cells):
    part = slice(group * depth, (group + 1) * depth)
    return jnp.concatenate(
        [source[:, part, cells].reshape(9 * depth, -1) for source in sources], axis=0
    )


def pack_kernel(edges, near, *outs):
    frames, row_count = near.shape[:2]
    even = parity(True) == 0
    first = lax.rem(lax.axis_index("tm"), 2) == 0
    for place, (out, row, other) in enumerate(
        zip(outs, (0, row_count - 1), (row_count - 1, 0))
    ):
        mine = jnp.concatenate([edges[frame, place] for frame in range(frames)], axis=0)
        beside = jnp.concatenate(
            [jnp.where(even, near[frame, row], near[frame, other]) for frame in range(frames)],
            axis=0,
        )
        out[...] = jnp.concatenate(
            [jnp.where(first, mine, beside), jnp.where(first, beside, mine)], axis=0
        )


def inner_kernel(count, *rest):
    blocks, weights, (patches, out) = rest[:count], rest[count:-2], rest[-2:]
    frames, row_count, _, plane = blocks[0].shape
    depth = weights[0].shape[1] // 27
    width = math.gcd(plane, CELLS)
    for index in range(row_count):
        lines = [block[frame, index] for block in blocks for frame in range(frames)]
        for place, piece in enumerate(shifted(jnp.concatenate(lines, axis=0))):
            patches[index, place] = piece
    places = [
        (row, slice(start, start + width))
        for row in range(1, row_count - 1)
        for start in range(0, plane, width)
    ]
    windows = [
        functools.partial(
            stack, [patches.at[row + step] for step in (-1, 0, 1)], depth=depth, cells=cells
        )
        for row, cells in places
    ]

    def store(index, frame, final):
        row, cells = places[index]
        out[frame, row - 1, :, cells] = final

    encode(windows, weights, out.shape[0], store)


def halo_lines(halos):
    if len(halos) == 1:
        return halos[0][...]
    first = lax.rem(lax.axis_index("tm"), 2) == 0
    got, other = halos[0][...], halos[1][...]
    half = got.shape[0] // 2
    parts = [[], []]
    for held in (jnp.where(first, got, other), jnp.where(first, other, got)):
        upper, lower = held[:half], held[half:]
        parts[0].append(jnp.where(first, upper, lower))
        parts[1].append(jnp.where(first, lower, upper))
    return jnp.concatenate(parts[0] + parts[1], axis=0)


def edge_row(paired, far, row_count):
    top = (parity(paired) == 0) == far
    return jnp.where(top, 0, row_count - 1), jnp.where(top, 1, row_count - 2)


def encode_edge(paired, far, halos, patches, weights, border, frames, store):
    row_count, _, _, plane = patches.shape
    depth = weights[0].shape[1] // 27
    width = math.gcd(plane, CELLS)
    for place, piece in enumerate(shifted(halo_lines(halos))):
        border[place] = piece
    edge, inside = edge_row(paired, far, row_count)
    cells = [slice(start, start + width) for start in range(0, plane, width)]
    sources = [border, patches.at[edge], patches.at[inside]]
    windows = [functools.partial(stack, sources, depth=depth, cells=part) for part in cells]
    encode(windows, weights, frames, lambda index, frame, final: store(frame, cells[index], final))


def near_kernel(paired, count, *refs):
    halos, patches, weights, (out, border) = refs[:count], refs[count], refs[count + 1 : -2], refs[-2:]

    def store(frame, cells, final):
        out[frame, :, cells] = final

    encode_edge(paired, False, halos, patches, weights, border, out.shape[0], store)


def far_kernel(paired, count, *refs):
    halos, patches, inner, near = refs[:count], *refs[count : count + 3]
    weights, (out, border, done, sems) = refs[count + 3 : -4], refs[-4:]
    row_count = patches.shape[0]
    far_row, _ = edge_row(paired, True, row_count)
    near_row, _ = edge_row(paired, False, row_count)
    copies = [
        pltpu.make_async_copy(inner, out.at[:, 1 : row_count - 1], sems.at[0]),
        pltpu.make_async_copy(near, out.at[:, near_row], sems.at[1]),
    ]
    for copy in copies:
        copy.start()

    def store(frame, cells, final):
        done[frame, :, cells] = final

    encode_edge(paired, True, halos, patches, weights, border, out.shape[0], store)
    copies.append(pltpu.make_async_copy(done, out.at[:, far_row], sems.at[2]))
    copies[-1].start()
    for copy in copies:
        copy.wait()


VMEM = pl.BlockSpec(memory_space=pltpu.VMEM)
CHEAP = pl.CostEstimate(flops=1, bytes_accessed=1, transcendentals=0)
PARAMS = pltpu.CompilerParams(vmem_limit_bytes=40 * 2**20)


def ring(count, step):
    return [(index, (index + step) % count) for index in range(count)]


def shards(snapshots, conv_weight, conv_bias, tap_weight, tap_bias, mix_weight, mix_bias):
    frames, row_count, fields, plane = snapshots.shape
    channels = conv_weight.shape[0]
    times = lax.axis_size("tm")
    spaces = lax.axis_size("space")
    offsets, counts = frame_blocks(times, frames)
    paired = times == 4 and sorted(offsets) == [0, 1, 2, 3] and spaces % 2 == 0
    tall = GROUP * channels
    total = len(offsets) * frames * fields

    sources = [
        snapshots,
        conv_weight.transpose(2, 3, 4, 1, 0).reshape(27, fields, channels),
        conv_bias.reshape(1, channels),
        tap_weight.transpose(0, 2, 1, 3),
        tap_bias,
        mix_weight,
        mix_bias,
    ]
    if paired:
        offsets = [0, 2, 1, 3]
        slot_of = lambda index: [index ^ offset for offset in offsets]
        across = [(index, index ^ 2) for index in range(times)]
        beside = [(index, index ^ 1) for index in range(times)]
        near = lax.ppermute(snapshots, "tm", beside)
        far = lax.ppermute(snapshots, "tm", across)
        both = lax.ppermute(snapshots, "tm", [(index, index ^ 3) for index in range(times)])
        even = parity(True) == 0
        low, high = snapshots[:, 0], snapshots[:, -1]
        edges = jnp.where(even, jnp.stack([low, high], axis=1), jnp.stack([high, low], axis=1))
        to_far, to_near = pl.pallas_call(
            pack_kernel,
            out_shape=[jax.ShapeDtypeStruct((total // 2, plane), BF16)] * 2,
            in_specs=[VMEM] * 2,
            out_specs=[VMEM] * 2,
            compiler_params=PARAMS,
            cost_estimate=CHEAP,
            name="pack",
        )(edges, near)
        far_pairs, near_pairs = [], []
        for time in range(times):
            for space in range(spaces):
                target = (time ^ (time % 2 * 2)) * spaces
                step = 2 * (space % 2) - 1
                far_pairs.append((time * spaces + space, target + (space + step) % spaces))
                near_pairs.append((time * spaces + space, target + space - step))
        near_halo = lax.ppermute(to_near, ("tm", "space"), near_pairs)
        far_halo = lax.ppermute(to_far, ("tm", "space"), far_pairs)
        near_other = lax.ppermute(near_halo, "tm", beside)
        near_halos = [near_halo, near_other]
    else:
        slot_of = lambda index: [(index + offset) % times for offset in offsets]

    shapes = [
        jax.ShapeDtypeStruct(snapshots.shape, BF16),
        *[jax.ShapeDtypeStruct((tall, 27 * GROUP * fields), BF16)] * 3,
        jax.ShapeDtypeStruct((tall, 128), F32),
    ]
    for level in range(LEVELS):
        rows, columns = counts[level + 1], counts[level]
        shapes.append(
            jax.ShapeDtypeStruct((rows * frames * channels, columns * frames * channels), BF16)
        )
    shapes += [
        jax.ShapeDtypeStruct((LEVELS, tall, 128), F32),
        jax.ShapeDtypeStruct((LEVELS, tall, tall), BF16),
        jax.ShapeDtypeStruct((LEVELS, tall, 128), F32),
    ]
    sources = [pltpu.with_memory_space_constraint(source, pltpu.HBM) for source in sources]
    own, conv, conv_far, conv_near, *weights = pl.pallas_call(
        functools.partial(prepare_kernel, paired, slot_of),
        out_shape=shapes,
        in_specs=[pl.BlockSpec(memory_space=pl.ANY)] * len(sources),
        out_specs=[VMEM] * len(shapes),
        scratch_shapes=[pltpu.VMEM(source.shape, source.dtype) for source in sources[1:]]
        + [pltpu.SemaphoreType.DMA((len(sources),))],
        compiler_params=PARAMS,
        cost_estimate=CHEAP,
        name="prepare",
    )(*sources)

    if paired:
        blocks = [own, far, near, both]
    else:
        blocks = [own] + [
            lax.ppermute(snapshots, "tm", ring(times, -offset)) for offset in offsets[1:]
        ]
        low, high = [
            jnp.concatenate([block[:, row] for block in blocks], axis=0).reshape(total, plane)
            for row in (0, row_count - 1)
        ]
        far_halos = [lax.ppermute(high, "space", ring(spaces, 1))]
        near_halos = [lax.ppermute(low, "space", ring(spaces, -1))]

    patches, inner = pl.pallas_call(
        functools.partial(inner_kernel, len(blocks)),
        out_shape=[
            jax.ShapeDtypeStruct((row_count, 9, total, plane), BF16),
            jax.ShapeDtypeStruct((frames, row_count - 2, channels, plane), BF16),
        ],
        in_specs=[VMEM] * (len(blocks) + 1 + len(weights)),
        out_specs=[VMEM] * 2,
        compiler_params=PARAMS,
        cost_estimate=CHEAP,
        name="inner",
    )(*blocks, conv, *weights)

    if paired:
        far_halo, patches, inner = lax.optimization_barrier((far_halo, patches, inner))
        far_other = lax.ppermute(far_halo, "tm", beside)
        far_halos = [far_halo, far_other]

    near = pl.pallas_call(
        functools.partial(near_kernel, paired, len(near_halos)),
        out_shape=jax.ShapeDtypeStruct((frames, channels, plane), BF16),
        in_specs=[VMEM] * (len(near_halos) + 2 + len(weights)),
        out_specs=VMEM,
        scratch_shapes=[pltpu.VMEM((9, total, plane), BF16)],
        compiler_params=PARAMS,
        cost_estimate=CHEAP,
        name="near",
    )(*near_halos, patches, conv_near, *weights)

    return pl.pallas_call(
        functools.partial(far_kernel, paired, len(far_halos)),
        out_shape=jax.ShapeDtypeStruct((frames, row_count, channels, plane), BF16),
        in_specs=[VMEM] * (len(far_halos) + 4 + len(weights)),
        out_specs=pl.BlockSpec(memory_space=pl.ANY),
        scratch_shapes=[
            pltpu.VMEM((9, total, plane), BF16),
            pltpu.VMEM((frames, channels, plane), BF16),
            pltpu.SemaphoreType.DMA((3,)),
        ],
        compiler_params=PARAMS,
        cost_estimate=CHEAP,
        name="far",
    )(*far_halos, patches, inner, near, conv_far, *weights)


def solution(mesh):
    in_specs = (P("tm", "space", None, None), P(), P(), P(), P(), P(), P())
    out_specs = P("tm", "space", None, None)
    return jax.shard_map(shards, mesh=mesh, in_specs=in_specs, out_specs=out_specs, check_vma=False)
```

```python
import functools
import math

import jax
import jax.numpy as jnp
from jax import lax
from jax.experimental import pallas as pl
from jax.experimental.pallas import tpu as pltpu
from jax.sharding import PartitionSpec as P

LEVELS = 3
NZ = 32
GROUP = 4
CELLS = 256
SLOPE = math.sqrt(2.0 / math.pi)
CUBIC = SLOPE * 0.044715
BF16 = jnp.bfloat16
F32 = jnp.float32


def frame_blocks(axis_size, frames):
    needed = [0]
    counts = [1]
    for level in reversed(range(LEVELS)):
        reach = set()
        for offset in needed:
            for frame in range(frames):
                for step in (-(2**level), 2**level):
                    reach.add((offset + (frame + step) // frames) % axis_size)
        needed = needed + sorted(reach - set(needed))
        spare = [offset for offset in range(axis_size) if offset not in needed]
        while len(needed) * frames % GROUP and spare:
            needed.append(spare.pop(0))
        counts.append(len(needed))
    return needed, counts[::-1]


def gelu(value):
    half = 0.5 * value
    return (half + half * jnp.tanh(value * (SLOPE + CUBIC * (value * value)))).astype(BF16)


def column(row, copies):
    count = row.shape[1]
    down = lax.broadcasted_iota(jnp.int32, (count, count), 0)
    across = lax.broadcasted_iota(jnp.int32, (count, count), 1)
    tall = jnp.sum(jnp.where(down == across, row, 0.0), axis=1, keepdims=True)
    return jnp.broadcast_to(jnp.concatenate([tall] * copies, axis=0), (count * copies, 128))


def spread(block, rows, columns):
    channels = block.shape[0]
    tall = jnp.concatenate([block] * (rows // channels), axis=0)
    down = lax.broadcasted_iota(jnp.int32, (channels, columns), 0)
    across = lax.broadcasted_iota(jnp.int32, (channels, columns), 1)
    pick = jnp.where(across % channels == down, 1.0, 0.0).astype(BF16)
    return jnp.dot(tall, pick, preferred_element_type=F32)


def fetch_kernel(*refs):
    count = len(refs) // 2
    sems = refs[-1]
    copies = [
        pltpu.make_async_copy(refs[index], refs[count + index], sems.at[index])
        for index in range(count)
    ]
    for copy in copies:
        copy.start()
    for copy in copies:
        copy.wait()


def prepare_kernel(paired, slot_of, count, *refs):
    blocks, outs = refs[:count], refs[count + 6 :]
    conv, conv_shift, taps, tap_shift, mix, mix_shift = refs[count : count + 6]
    frames, row_count = blocks[0].shape[:2]
    patches, outs = outs[0], outs[1:]
    for row in range(row_count):
        lines = [block[frame, row] for block in blocks for frame in range(frames)]
        for place, piece in enumerate(shifted(jnp.concatenate(lines, axis=0))):
            patches[row, place] = piece
    conv_outs, conv_shift_out = outs[:3], outs[3]
    tap_outs = outs[4 : 4 + LEVELS]
    tap_shift_out, mix_out, mix_shift_out = outs[4 + LEVELS :]
    places, fields, channels = conv.shape
    depth = places * fields
    wide = depth * GROUP
    flat = conv[...].astype(F32).reshape(depth, channels).astype(BF16)
    down = lax.broadcasted_iota(jnp.int32, (depth, wide), 0)
    across = lax.broadcasted_iota(jnp.int32, (depth, wide), 1)
    same = (down // fields == across // (GROUP * fields)) & (down % fields == across % fields)
    pick = jnp.where(same, 1.0, 0.0).astype(BF16)
    full = lax.dot_general(flat, pick, (((0,), (0,)), ((), ())), preferred_element_type=F32)
    full = jnp.concatenate([full] * GROUP, axis=0)
    down = lax.broadcasted_iota(jnp.int32, full.shape, 0)
    across = lax.broadcasted_iota(jnp.int32, full.shape, 1)
    keep = down // channels == across // fields % GROUP
    full = jnp.where(keep, full, 0.0)
    third = wide // 3
    turned = jnp.concatenate([full[:, 2 * third :], full[:, third : -third], full[:, :third]], axis=1)
    even = parity(paired) == 0
    conv_outs[0][...] = full.astype(BF16)
    conv_outs[1][...] = jnp.where(even, full, turned).astype(BF16)
    conv_outs[2][...] = jnp.where(even, turned, full).astype(BF16)
    conv_shift_out[...] = column(conv_shift[...], GROUP)
    slots = slot_of(lax.axis_index("tm"))
    for level in range(LEVELS):
        rows, columns = tap_outs[level].shape

        def frame_of(axis):
            place = lax.broadcasted_iota(jnp.int32, (rows, columns), axis) // channels
            block = place // frames
            start = jnp.zeros((rows, columns), jnp.int32)
            for index, slot in enumerate(slots[: (rows, columns)[axis] // channels // frames]):
                start = jnp.where(block == index, slot * frames, start)
            return start + place % frames

        gap = frame_of(1) - frame_of(0)
        total = jnp.zeros((rows, columns), F32)
        for tap in range(3):
            block = spread(taps[level, tap], rows, columns)
            total = jnp.where(gap == (tap - 1) * 2**level, block, total)
        tap_outs[level][...] = total.astype(BF16)
        tap_shift_out[level] = column(tap_shift[level : level + 1], GROUP)
        size = GROUP * channels
        down = lax.broadcasted_iota(jnp.int32, (size, size), 0)
        across = lax.broadcasted_iota(jnp.int32, (size, size), 1)
        full = spread(mix[level], size, size)
        mix_out[level] = jnp.where(down // channels == across // channels, full, 0.0).astype(BF16)
        mix_shift_out[level] = column(mix_shift[level : level + 1], GROUP)


def shifted(lines):
    plane = lines.shape[-1]
    depth = lax.broadcasted_iota(jnp.int32, (1, plane), 1) % NZ
    blank = jnp.zeros_like(lines)
    below = jnp.where(depth == 0, blank, pltpu.roll(lines, 1, 1))
    above = jnp.where(depth == NZ - 1, blank, pltpu.roll(lines, plane - 1, 1))
    for delta_y in (-1, 0, 1):
        for piece in (below, lines, above):
            yield pltpu.roll(piece, -delta_y * NZ % plane, 1) if delta_y else piece


def parity(paired):
    return lax.rem(lax.axis_index("space"), 2) if paired else 0


def joined(parts, axis):
    return parts[0] if len(parts) == 1 else jnp.concatenate(parts, axis=axis)


def wide(shift, cells):
    return joined([shift] * (cells // 128), 1)


def encode(windows, weights, frames, store):
    conv_shift = weights[0]
    taps = weights[1 : 1 + LEVELS]
    tap_shift, mix, mix_shift = weights[1 + LEVELS :]
    tall = conv_shift.shape[0]
    channels = tall // GROUP
    groups = taps[0].shape[1] // tall
    hidden = []
    for conv, window in windows:
        parts = []
        for group in range(groups):
            summed = jnp.dot(conv[...], window(group), preferred_element_type=F32)
            parts.append(gelu(summed + wide(conv_shift[...], summed.shape[1])))
        hidden.append(joined(parts, 0))
    for level, tap in enumerate(taps):
        rows, columns = tap.shape
        later = []
        for current in hidden:
            cells = current.shape[1]
            summed = jnp.dot(tap[...], current[:columns], preferred_element_type=F32)
            parts = []
            for first in range(0, rows, tall):
                size = min(tall, rows - first)
                piece = summed[first : first + size]
                gated = gelu(piece + wide(tap_shift[level, :size], cells))
                mixed = jnp.dot(mix[level, :size, :size], gated, preferred_element_type=F32)
                kept = current[first : first + size].astype(F32)
                parts.append((kept + mixed + wide(mix_shift[level, :size], cells)).astype(BF16))
            later.append(joined(parts, 0))
        hidden = later
    for index, final in enumerate(hidden):
        for frame in range(frames):
            store(index, frame, final[frame * channels : (frame + 1) * channels])


def stack(sources, group, depth, cells):
    part = slice(group * depth, (group + 1) * depth)
    return jnp.concatenate(
        [source[:, part, cells].reshape(9 * depth, -1) for source in sources], axis=0
    )


def pack_kernel(own, near, *outs):
    frames, row_count = near.shape[:2]
    even = parity(True) == 0
    first = lax.rem(lax.axis_index("tm"), 2) == 0
    rows = []
    for row in (0, row_count - 1):
        mine, beside = [
            jnp.concatenate([block[frame, row] for frame in range(frames)], axis=0)
            for block in (own, near)
        ]
        rows.append(
            jnp.concatenate(
                [jnp.where(first, mine, beside), jnp.where(first, beside, mine)], axis=0
            )
        )
    outs[0][...] = jnp.where(even, rows[0], rows[1])
    outs[1][...] = jnp.where(even, rows[1], rows[0])


def inner_kernel(patches, conv, *rest):
    weights, out = rest[:-1], rest[-1]
    row_count, _, _, plane = patches.shape
    depth = conv.shape[1] // 27
    width = math.gcd(plane, CELLS)
    places = [
        (row, slice(start, start + width))
        for row in range(1, row_count - 1)
        for start in range(0, plane, width)
    ]
    windows = [
        (
            conv,
            functools.partial(
                stack, [patches.at[row + step] for step in (-1, 0, 1)], depth=depth, cells=cells
            ),
        )
        for row, cells in places
    ]

    def store(index, frame, final):
        row, cells = places[index]
        out[frame, row - 1, :, cells] = final

    encode(windows, weights, out.shape[0], store)


def halo_lines(halos):
    if len(halos) == 1:
        return halos[0][...]
    first = lax.rem(lax.axis_index("tm"), 2) == 0
    got, other = halos[0][...], halos[1][...]
    half = got.shape[0] // 2
    parts = [[], []]
    for held in (jnp.where(first, got, other), jnp.where(first, other, got)):
        upper, lower = held[:half], held[half:]
        parts[0].append(jnp.where(first, upper, lower))
        parts[1].append(jnp.where(first, lower, upper))
    return jnp.concatenate(parts[0] + parts[1], axis=0)


def edge_row(paired, far, row_count):
    top = (parity(paired) == 0) == far
    return jnp.where(top, 0, row_count - 1), jnp.where(top, 1, row_count - 2)


def outer_kernel(paired, count, *refs):
    halos = refs[count : 2 * count], refs[:count]
    patches, inner, *convs = refs[2 * count : 2 * count + 4]
    weights, (out, borders, done, sems) = refs[2 * count + 4 : -4], refs[-4:]
    row_count, _, _, plane = patches.shape
    depth = convs[0].shape[1] // 27
    width = math.gcd(plane, CELLS)
    rows = [edge_row(paired, far, row_count) for far in (True, False)]
    copies = [pltpu.make_async_copy(inner, out.at[:, 1 : row_count - 1], sems.at[0])]
    copies[0].start()
    windows = []
    places = []
    for side, (edge, inside) in enumerate(rows):
        for place, piece in enumerate(shifted(halo_lines(halos[side]))):
            borders[side, place] = piece
        sources = [borders.at[side], patches.at[edge], patches.at[inside]]
        for start in range(0, plane, width):
            cells = slice(start, start + width)
            places.append((side, cells))
            windows.append(
                (convs[side], functools.partial(stack, sources, depth=depth, cells=cells))
            )

    def store(index, frame, final):
        side, cells = places[index]
        done[side, frame, :, cells] = final

    encode(windows, weights, out.shape[0], store)
    for side, (edge, _) in enumerate(rows):
        copies.append(pltpu.make_async_copy(done.at[side], out.at[:, edge], sems.at[side + 1]))
        copies[-1].start()
    for copy in copies:
        copy.wait()


VMEM = pl.BlockSpec(memory_space=pltpu.VMEM)
PARAMS = pltpu.CompilerParams(vmem_limit_bytes=40 * 2**20)


def cost(microseconds):
    size = int(microseconds * 3.7e6)
    return pl.CostEstimate(flops=0, bytes_accessed=size, transcendentals=0)


def ring(count, step):
    return [(index, (index + step) % count) for index in range(count)]


def shards(snapshots, conv_weight, conv_bias, tap_weight, tap_bias, mix_weight, mix_bias):
    frames, row_count, fields, plane = snapshots.shape
    channels = conv_weight.shape[0]
    times = lax.axis_size("tm")
    spaces = lax.axis_size("space")
    offsets, counts = frame_blocks(times, frames)
    paired = times == 4 and sorted(offsets) == [0, 1, 2, 3] and spaces % 2 == 0
    tall = GROUP * channels
    total = len(offsets) * frames * fields

    sources = [
        snapshots,
        conv_weight.transpose(2, 3, 4, 1, 0).reshape(27, fields, channels),
        conv_bias.reshape(1, channels),
        tap_weight.transpose(0, 2, 1, 3),
        tap_bias,
        mix_weight,
        mix_bias,
    ]
    sources = [pltpu.with_memory_space_constraint(source, pltpu.HBM) for source in sources]
    own, *sources = pl.pallas_call(
        fetch_kernel,
        out_shape=[jax.ShapeDtypeStruct(source.shape, source.dtype) for source in sources],
        in_specs=[pl.BlockSpec(memory_space=pl.ANY)] * len(sources),
        out_specs=[VMEM] * len(sources),
        scratch_shapes=[pltpu.SemaphoreType.DMA((len(sources),))],
        compiler_params=PARAMS,
        cost_estimate=cost(0.8),
        name="fetch",
    )(*sources)

    if paired:
        offsets = [0, 2, 1, 3]
        slot_of = lambda index: [index ^ offset for offset in offsets]
        across = [(index, index ^ 2) for index in range(times)]
        beside = [(index, index ^ 1) for index in range(times)]
        near = lax.ppermute(snapshots, "tm", beside)
        both = lax.ppermute(snapshots, "tm", [(index, index ^ 3) for index in range(times)])
        far = lax.ppermute(snapshots, "tm", across)
        to_far, to_near = pl.pallas_call(
            pack_kernel,
            out_shape=[jax.ShapeDtypeStruct((total // 2, plane), BF16)] * 2,
            in_specs=[VMEM] * 2,
            out_specs=[VMEM] * 2,
            compiler_params=PARAMS,
            cost_estimate=cost(0.05),
            name="pack",
        )(own, near)
        far_pairs, near_pairs = [], []
        for time in range(times):
            for space in range(spaces):
                target = (time ^ (time % 2 * 2)) * spaces
                step = 2 * (space % 2) - 1
                far_pairs.append((time * spaces + space, target + (space + step) % spaces))
                near_pairs.append((time * spaces + space, target + space - step))
        near_halo = lax.ppermute(to_near, ("tm", "space"), near_pairs)
        far_halo = lax.ppermute(to_far, ("tm", "space"), far_pairs)
    else:
        slot_of = lambda index: [(index + offset) % times for offset in offsets]

    shapes = [
        jax.ShapeDtypeStruct((row_count, 9, total, plane), BF16),
        *[jax.ShapeDtypeStruct((tall, 27 * GROUP * fields), BF16)] * 3,
        jax.ShapeDtypeStruct((tall, 128), F32),
    ]
    for level in range(LEVELS):
        rows, columns = counts[level + 1], counts[level]
        shapes.append(
            jax.ShapeDtypeStruct((rows * frames * channels, columns * frames * channels), BF16)
        )
    shapes += [
        jax.ShapeDtypeStruct((LEVELS, tall, 128), F32),
        jax.ShapeDtypeStruct((LEVELS, tall, tall), BF16),
        jax.ShapeDtypeStruct((LEVELS, tall, 128), F32),
    ]
    if paired:
        blocks = [own, far, near, both]
    else:
        blocks = [own] + [
            lax.ppermute(snapshots, "tm", ring(times, -offset)) for offset in offsets[1:]
        ]
        low, high = [
            jnp.concatenate([block[:, row] for block in blocks], axis=0).reshape(total, plane)
            for row in (0, row_count - 1)
        ]
        far_halos = [lax.ppermute(high, "space", ring(spaces, 1))]
        near_halos = [lax.ppermute(low, "space", ring(spaces, -1))]

    patches, conv, conv_far, conv_near, *weights = pl.pallas_call(
        functools.partial(prepare_kernel, paired, slot_of, len(blocks)),
        out_shape=shapes,
        in_specs=[VMEM] * (len(blocks) + len(sources)),
        out_specs=[VMEM] * len(shapes),
        compiler_params=PARAMS,
        cost_estimate=cost(0.9),
        name="prepare",
    )(*blocks, *sources)

    inner = pl.pallas_call(
        inner_kernel,
        out_shape=jax.ShapeDtypeStruct((frames, row_count - 2, channels, plane), BF16),
        in_specs=[VMEM] * (2 + len(weights)),
        out_specs=VMEM,
        compiler_params=PARAMS,
        cost_estimate=cost(1.8),
        name="inner",
    )(patches, conv, *weights)

    if paired:
        near_halo, far_halo, inner = lax.optimization_barrier((near_halo, far_halo, inner))
        near_halos = [near_halo, lax.ppermute(near_halo, "tm", beside)]
        far_halos = [far_halo, lax.ppermute(far_halo, "tm", beside)]

    return pl.pallas_call(
        functools.partial(outer_kernel, paired, len(far_halos)),
        out_shape=jax.ShapeDtypeStruct((frames, row_count, channels, plane), BF16),
        in_specs=[VMEM] * (len(far_halos) + len(near_halos) + 4 + len(weights)),
        out_specs=pl.BlockSpec(memory_space=pl.ANY),
        scratch_shapes=[
            pltpu.VMEM((2, 9, total, plane), BF16),
            pltpu.VMEM((2, frames, channels, plane), BF16),
            pltpu.SemaphoreType.DMA((3,)),
        ],
        compiler_params=PARAMS,
        cost_estimate=cost(2.5),
        name="outer",
    )(*near_halos, *far_halos, patches, inner, conv_far, conv_near, *weights)


def solution(mesh):
    in_specs = (P("tm", "space", None, None), P(), P(), P(), P(), P(), P())
    out_specs = P("tm", "space", None, None)
    return jax.shard_map(shards, mesh=mesh, in_specs=in_specs, out_specs=out_specs, check_vma=False)
```

```python
import functools
import math

import jax
import jax.numpy as jnp
from jax import lax
from jax.experimental import pallas as pl
from jax.experimental.pallas import tpu as pltpu
from jax.sharding import PartitionSpec as P

LEVELS = 3
NZ = 32
GROUP = 4
CELLS = 256
SLOPE = math.sqrt(2.0 / math.pi)
CUBIC = SLOPE * 0.044715
BF16 = jnp.bfloat16
F32 = jnp.float32


def frame_blocks(axis_size, frames):
    needed = [0]
    counts = [1]
    for level in reversed(range(LEVELS)):
        reach = set()
        for offset in needed:
            for frame in range(frames):
                for step in (-(2**level), 2**level):
                    reach.add((offset + (frame + step) // frames) % axis_size)
        needed = needed + sorted(reach - set(needed))
        spare = [offset for offset in range(axis_size) if offset not in needed]
        while len(needed) * frames % GROUP and spare:
            needed.append(spare.pop(0))
        counts.append(len(needed))
    return needed, counts[::-1]


def gelu_of_double(half):
    inner = half * (2 * SLOPE + 8 * CUBIC * (half * half))
    return (half + half * jnp.tanh(inner)).astype(BF16)


def joined(parts, axis):
    return parts[0] if len(parts) == 1 else jnp.concatenate(parts, axis=axis)


def wide(shift, cells):
    return joined([shift] * (cells // 128), 1)


def column(row, copies):
    count = row.shape[1]
    down = lax.broadcasted_iota(jnp.int32, (count, count), 0)
    across = lax.broadcasted_iota(jnp.int32, (count, count), 1)
    tall = jnp.sum(jnp.where(down == across, row, 0.0), axis=1, keepdims=True)
    return joined([tall] * copies, 0)


def lanes(value):
    return jnp.broadcast_to(value, (value.shape[0], 128))


def spread(block, rows, columns):
    height, width = block.shape
    tile = jnp.concatenate([block] * (128 // width), axis=1)
    parts = [tile] * (columns // 128)
    if columns % 128:
        parts.append(tile[:, : columns % 128])
    return joined([joined(parts, 1)] * (rows // height), 0)


def fetch_kernel(*refs):
    count = len(refs) // 2
    sems = refs[-1]
    copies = [
        pltpu.make_async_copy(refs[index], refs[count + index], sems.at[index])
        for index in range(count)
    ]
    for copy in copies:
        copy.start()
    for copy in copies:
        copy.wait()


def prepare_kernel(paired, slot_of, count, *refs):
    blocks, outs = refs[:count], refs[count + 6 :]
    conv, conv_shift, taps, tap_shift, mix, mix_shift = refs[count : count + 6]
    frames, row_count = blocks[0].shape[:2]
    patches, outs = outs[0], outs[1:]
    for row in range(row_count):
        lines = [block[frame, row] for block in blocks for frame in range(frames)]
        for place, piece in enumerate(shifted(jnp.concatenate(lines, axis=0))):
            patches[row, place] = piece
    conv_outs, conv_shift_out = outs[:3], outs[3]
    tap_outs = outs[4 : 4 + LEVELS]
    tap_shift_outs = outs[4 + LEVELS : 4 + 2 * LEVELS]
    mix_out, mix_shift_out = outs[4 + 2 * LEVELS :]
    places, fields, channels = conv.shape
    depth = places * fields
    wide = depth * GROUP
    flat = conv[...].astype(F32).reshape(depth, channels).astype(BF16)
    down = lax.broadcasted_iota(jnp.int32, (depth, wide), 0)
    across = lax.broadcasted_iota(jnp.int32, (depth, wide), 1)
    same = (down // fields == across // (GROUP * fields)) & (down % fields == across % fields)
    pick = jnp.where(same, 1.0, 0.0).astype(BF16)
    full = lax.dot_general(flat, pick, (((0,), (0,)), ((), ())), preferred_element_type=F32)
    full = jnp.concatenate([full] * GROUP, axis=0)
    down = lax.broadcasted_iota(jnp.int32, full.shape, 0)
    across = lax.broadcasted_iota(jnp.int32, full.shape, 1)
    keep = down // channels == across // fields % GROUP
    full = jnp.where(keep, 0.5 * full, 0.0)
    third = wide // 3
    turned = jnp.concatenate([full[:, 2 * third :], full[:, third : -third], full[:, :third]], axis=1)
    even = parity(paired) == 0
    conv_outs[0][...] = full.astype(BF16)
    conv_outs[1][...] = jnp.where(even, full, turned).astype(BF16)
    conv_outs[2][...] = jnp.where(even, turned, full).astype(BF16)
    conv_shift_out[...] = lanes(0.5 * column(conv_shift[...], GROUP))
    slots = slot_of(lax.axis_index("tm"))
    for level in range(LEVELS):
        rows, columns = tap_outs[level].shape
        columns //= level + 1

        def frame_of(axis):
            place = lax.broadcasted_iota(jnp.int32, (rows, columns), axis) // channels
            block = place // frames
            start = jnp.zeros((rows, columns), jnp.int32)
            for index, slot in enumerate(slots[: (rows, columns)[axis] // channels // frames]):
                start = jnp.where(block == index, slot * frames, start)
            return start + place % frames

        gap = frame_of(1) - frame_of(0)
        for source in range(level + 1):
            total = jnp.zeros((rows, columns), F32)
            for tap in range(3):
                block = taps[level, tap]
                if source:
                    block = jnp.dot(block, mix[source - 1], preferred_element_type=F32)
                block = spread(block.astype(F32), rows, columns)
                total = jnp.where(gap == (tap - 1) * 2**level, block, total)
            if not source:
                shift = column(tap_shift[level : level + 1], rows // channels)
                if level:
                    held = jnp.sum(mix_shift[:level], axis=0, keepdims=True)
                    held = total * spread(held, 1, columns)
                    shift = shift + jnp.sum(held, axis=1, keepdims=True)
                tap_shift_outs[level][...] = lanes(0.5 * shift)
            part = slice(source * columns, (source + 1) * columns)
            tap_outs[level][:, part] = (0.5 * total).astype(BF16)
    size = mix_out.shape[0]
    down = lax.broadcasted_iota(jnp.int32, (size, size), 0)
    across = lax.broadcasted_iota(jnp.int32, (size, size), 1)
    same = down // channels == across // channels
    mix_out[...] = jnp.concatenate(
        [
            jnp.where(same, spread(mix[level].astype(F32), size, size), 0.0).astype(BF16)
            for level in range(LEVELS)
        ],
        axis=1,
    )
    held = jnp.sum(mix_shift[...], axis=0, keepdims=True)
    mix_shift_out[...] = lanes(column(held, size // channels))


def shifted(lines):
    plane = lines.shape[-1]
    depth = lax.broadcasted_iota(jnp.int32, (1, plane), 1) % NZ
    blank = jnp.zeros_like(lines)
    below = jnp.where(depth == 0, blank, pltpu.roll(lines, 1, 1))
    above = jnp.where(depth == NZ - 1, blank, pltpu.roll(lines, plane - 1, 1))
    for delta_y in (-1, 0, 1):
        for piece in (below, lines, above):
            yield pltpu.roll(piece, -delta_y * NZ % plane, 1) if delta_y else piece


def parity(paired):
    return lax.rem(lax.axis_index("space"), 2) if paired else 0


def encode(windows, weights, frames, store):
    conv_shift, mix, mix_shift = weights[0], *weights[-2:]
    taps, tap_shifts = weights[1 : 1 + LEVELS], weights[1 + LEVELS : 1 + 2 * LEVELS]
    channels = conv_shift.shape[0] // GROUP
    groups = -(-taps[0].shape[1] // conv_shift.shape[0])
    held = []
    for conv, window in windows:
        parts = []
        for group in range(groups):
            summed = jnp.dot(conv[...], window(group), preferred_element_type=F32)
            parts.append(gelu_of_double(summed + wide(conv_shift[...], summed.shape[1])))
        held.append([joined(parts, 0)])
    for level, (tap, shift) in enumerate(zip(taps, tap_shifts)):
        columns = tap.shape[1] // (level + 1)
        for parts in held:
            read = joined([part[:columns] for part in parts], 0)
            summed = jnp.dot(tap[...], read, preferred_element_type=F32)
            parts.append(gelu_of_double(summed + wide(shift[...], summed.shape[1])))
    size = mix.shape[0]
    for index, (first, *gated) in enumerate(held):
        read = joined([part[:size] for part in gated], 0)
        mixed = jnp.dot(mix[...], read, preferred_element_type=F32)
        mixed = mixed + wide(mix_shift[...], mixed.shape[1])
        final = (first[:size].astype(F32) + mixed).astype(BF16)
        for frame in range(frames):
            store(index, frame, final[frame * channels : (frame + 1) * channels])


def stack(sources, group, depth, cells):
    part = slice(group * depth, (group + 1) * depth)
    return jnp.concatenate(
        [source[:, part, cells].reshape(9 * depth, -1) for source in sources], axis=0
    )


def pack_kernel(own, near, *outs):
    frames, row_count = near.shape[:2]
    even = parity(True) == 0
    first = lax.rem(lax.axis_index("tm"), 2) == 0
    rows = []
    for row in (0, row_count - 1):
        mine, beside = [
            jnp.concatenate([block[frame, row] for frame in range(frames)], axis=0)
            for block in (own, near)
        ]
        rows.append(
            jnp.concatenate(
                [jnp.where(first, mine, beside), jnp.where(first, beside, mine)], axis=0
            )
        )
    outs[0][...] = jnp.where(even, rows[0], rows[1])
    outs[1][...] = jnp.where(even, rows[1], rows[0])


def inner_kernel(patches, conv, *rest):
    weights, out = rest[:-1], rest[-1]
    row_count, _, _, plane = patches.shape
    depth = conv.shape[1] // 27
    width = math.gcd(plane, CELLS)
    places = [
        (row, slice(start, start + width))
        for row in range(1, row_count - 1)
        for start in range(0, plane, width)
    ]
    windows = [
        (
            conv,
            functools.partial(
                stack, [patches.at[row + step] for step in (-1, 0, 1)], depth=depth, cells=cells
            ),
        )
        for row, cells in places
    ]

    def store(index, frame, final):
        row, cells = places[index]
        out[frame, row - 1, :, cells] = final

    encode(windows, weights, out.shape[0], store)


def merge_kernel(near, far, out):
    out[...] = jnp.concatenate([near[...], far[...]], axis=0)


def halo_lines(got, other):
    first = lax.rem(lax.axis_index("tm"), 2) == 0
    half = got.shape[0] // 2
    parts = [[], []]
    for held in (jnp.where(first, got, other), jnp.where(first, other, got)):
        upper, lower = held[:half], held[half:]
        parts[0].append(jnp.where(first, upper, lower))
        parts[1].append(jnp.where(first, lower, upper))
    return jnp.concatenate(parts[0] + parts[1], axis=0)


def edge_row(paired, far, row_count):
    top = (parity(paired) == 0) == far
    return jnp.where(top, 0, row_count - 1), jnp.where(top, 1, row_count - 2)


def outer_kernel(paired, near, far, *refs):
    near, far = near[...], far[...]
    if paired:
        half = refs[0].shape[0] // 2
        near = halo_lines(near, refs[0][:half])
        far = halo_lines(far, refs[0][half:])
        refs = refs[1:]
    halos = far, near
    patches, inner, *convs = refs[:4]
    weights, (out, borders, done, sems) = refs[4:-4], refs[-4:]
    row_count, _, _, plane = patches.shape
    depth = convs[0].shape[1] // 27
    width = math.gcd(plane, CELLS)
    rows = [edge_row(paired, far, row_count) for far in (True, False)]
    copies = [pltpu.make_async_copy(inner, out.at[:, 1 : row_count - 1], sems.at[0])]
    copies[0].start()
    windows = []
    places = []
    for side, (edge, inside) in enumerate(rows):
        for place, piece in enumerate(shifted(halos[side])):
            borders[side, place] = piece
        sources = [borders.at[side], patches.at[edge], patches.at[inside]]
        for start in range(0, plane, width):
            cells = slice(start, start + width)
            places.append((side, cells))
            windows.append(
                (convs[side], functools.partial(stack, sources, depth=depth, cells=cells))
            )

    def store(index, frame, final):
        side, cells = places[index]
        done[side, frame, :, cells] = final

    encode(windows, weights, out.shape[0], store)
    for side, (edge, _) in enumerate(rows):
        copies.append(pltpu.make_async_copy(done.at[side], out.at[:, edge], sems.at[side + 1]))
        copies[-1].start()
    for copy in copies:
        copy.wait()


VMEM = pl.BlockSpec(memory_space=pltpu.VMEM)
PARAMS = pltpu.CompilerParams(vmem_limit_bytes=40 * 2**20)


def cost(microseconds):
    size = int(microseconds * 3.7e6)
    return pl.CostEstimate(flops=0, bytes_accessed=size, transcendentals=0)


def ring(count, step):
    return [(index, (index + step) % count) for index in range(count)]


def shards(snapshots, conv_weight, conv_bias, tap_weight, tap_bias, mix_weight, mix_bias):
    frames, row_count, fields, plane = snapshots.shape
    channels = conv_weight.shape[0]
    times = lax.axis_size("tm")
    spaces = lax.axis_size("space")
    offsets, counts = frame_blocks(times, frames)
    paired = times == 4 and sorted(offsets) == [0, 1, 2, 3] and spaces % 2 == 0
    tall = GROUP * channels
    total = len(offsets) * frames * fields

    sources = [
        snapshots,
        conv_weight.transpose(2, 3, 4, 1, 0).reshape(27, fields, channels),
        conv_bias.reshape(1, channels),
        tap_weight.transpose(0, 2, 1, 3),
        tap_bias,
        mix_weight,
        mix_bias,
    ]
    sources = [pltpu.with_memory_space_constraint(source, pltpu.HBM) for source in sources]
    own, *sources = pl.pallas_call(
        fetch_kernel,
        out_shape=[jax.ShapeDtypeStruct(source.shape, source.dtype) for source in sources],
        in_specs=[pl.BlockSpec(memory_space=pl.ANY)] * len(sources),
        out_specs=[VMEM] * len(sources),
        scratch_shapes=[pltpu.SemaphoreType.DMA((len(sources),))],
        compiler_params=PARAMS,
        cost_estimate=cost(0.8),
        name="fetch",
    )(*sources)

    if paired:
        offsets = [0, 2, 1, 3]
        slot_of = lambda index: [index ^ offset for offset in offsets]
        across = [(index, index ^ 2) for index in range(times)]
        beside = [(index, index ^ 1) for index in range(times)]
        near = lax.ppermute(snapshots, "tm", beside)
        both = lax.ppermute(snapshots, "tm", [(index, index ^ 3) for index in range(times)])
        far = lax.ppermute(snapshots, "tm", across)
        to_far, to_near = pl.pallas_call(
            pack_kernel,
            out_shape=[jax.ShapeDtypeStruct((total // 2, plane), BF16)] * 2,
            in_specs=[VMEM] * 2,
            out_specs=[VMEM] * 2,
            compiler_params=PARAMS,
            cost_estimate=cost(0.05),
            name="pack",
        )(own, near)
        far_pairs, near_pairs = [], []
        for time in range(times):
            for space in range(spaces):
                target = (time ^ (time % 2 * 2)) * spaces
                step = 2 * (space % 2) - 1
                far_pairs.append((time * spaces + space, target + (space + step) % spaces))
                near_pairs.append((time * spaces + space, target + space - step))
        near_halo = lax.ppermute(to_near, ("tm", "space"), near_pairs)
        far_halo = lax.ppermute(to_far, ("tm", "space"), far_pairs)
    else:
        slot_of = lambda index: [(index + offset) % times for offset in offsets]

    shapes = [
        jax.ShapeDtypeStruct((row_count, 9, total, plane), BF16),
        *[jax.ShapeDtypeStruct((tall, 27 * GROUP * fields), BF16)] * 3,
        jax.ShapeDtypeStruct((tall, 128), F32),
    ]
    wide_of = [count * frames * channels for count in counts]
    for level in range(LEVELS):
        shape = wide_of[level + 1], wide_of[level] * (level + 1)
        shapes.append(jax.ShapeDtypeStruct(shape, BF16))
    for level in range(LEVELS):
        shapes.append(jax.ShapeDtypeStruct((wide_of[level + 1], 128), F32))
    shapes += [
        jax.ShapeDtypeStruct((wide_of[LEVELS], wide_of[LEVELS] * LEVELS), BF16),
        jax.ShapeDtypeStruct((wide_of[LEVELS], 128), F32),
    ]

    if paired:
        blocks = [own, far, near, both]
    else:
        blocks = [own] + [
            lax.ppermute(snapshots, "tm", ring(times, -offset)) for offset in offsets[1:]
        ]
        low, high = [
            jnp.concatenate([block[:, row] for block in blocks], axis=0).reshape(total, plane)
            for row in (0, row_count - 1)
        ]
        halos = [
            lax.ppermute(low, "space", ring(spaces, -1)),
            lax.ppermute(high, "space", ring(spaces, 1)),
        ]

    patches, conv, conv_far, conv_near, *weights = pl.pallas_call(
        functools.partial(prepare_kernel, paired, slot_of, len(blocks)),
        out_shape=shapes,
        in_specs=[VMEM] * (len(blocks) + len(sources)),
        out_specs=[VMEM] * len(shapes),
        compiler_params=PARAMS,
        cost_estimate=cost(0.9),
        name="prepare",
    )(*blocks, *sources)

    inner = pl.pallas_call(
        inner_kernel,
        out_shape=jax.ShapeDtypeStruct((frames, row_count - 2, channels, plane), BF16),
        in_specs=[VMEM] * (2 + len(weights)),
        out_specs=VMEM,
        compiler_params=PARAMS,
        cost_estimate=cost(1.8),
        name="inner",
    )(patches, conv, *weights)

    if paired:
        near_halo, far_halo, inner = lax.optimization_barrier((near_halo, far_halo, inner))
        merged = pl.pallas_call(
            merge_kernel,
            out_shape=jax.ShapeDtypeStruct((total, plane), BF16),
            in_specs=[VMEM] * 2,
            out_specs=VMEM,
            compiler_params=PARAMS,
            cost_estimate=cost(0.05),
            name="merge",
        )(near_halo, far_halo)
        halos = [near_halo, far_halo, lax.ppermute(merged, "tm", beside)]

    return pl.pallas_call(
        functools.partial(outer_kernel, paired),
        out_shape=jax.ShapeDtypeStruct((frames, row_count, channels, plane), BF16),
        in_specs=[VMEM] * (len(halos) + 4 + len(weights)),
        out_specs=pl.BlockSpec(memory_space=pl.ANY),
        scratch_shapes=[
            pltpu.VMEM((2, 9, total, plane), BF16),
            pltpu.VMEM((2, frames, channels, plane), BF16),
            pltpu.SemaphoreType.DMA((3,)),
        ],
        compiler_params=PARAMS,
        cost_estimate=cost(2.5),
        name="outer",
    )(*halos, patches, inner, conv_far, conv_near, *weights)


def solution(mesh):
    in_specs = (P("tm", "space", None, None), P(), P(), P(), P(), P(), P())
    out_specs = P("tm", "space", None, None)
    return jax.shard_map(shards, mesh=mesh, in_specs=in_specs, out_specs=out_specs, check_vma=False)
```

```python
import functools
import math

import jax
import jax.numpy as jnp
from jax import lax
from jax.experimental import pallas as pl
from jax.experimental.pallas import tpu as pltpu
from jax.sharding import PartitionSpec as P

LEVELS = 3
NZ = 32
GROUP = 4
CELLS = 256
SLOPE = math.sqrt(2.0 / math.pi)
CUBIC = SLOPE * 0.044715
BF16 = jnp.bfloat16
F32 = jnp.float32


def frame_blocks(axis_size, frames):
    needed = [0]
    counts = [1]
    for level in reversed(range(LEVELS)):
        reach = set()
        for offset in needed:
            for frame in range(frames):
                for step in (-(2**level), 2**level):
                    reach.add((offset + (frame + step) // frames) % axis_size)
        needed = needed + sorted(reach - set(needed))
        spare = [offset for offset in range(axis_size) if offset not in needed]
        while len(needed) * frames % GROUP and spare:
            needed.append(spare.pop(0))
        counts.append(len(needed))
    return needed, counts[::-1]


def gelu_of_double(half):
    inner = half * (2 * SLOPE + 8 * CUBIC * (half * half))
    return (half + half * jnp.tanh(inner)).astype(BF16)


def joined(parts, axis):
    return parts[0] if len(parts) == 1 else jnp.concatenate(parts, axis=axis)


def wide(shift, cells):
    return joined([shift] * (cells // 128), 1)


def column(row, copies):
    count = row.shape[1]
    down = lax.broadcasted_iota(jnp.int32, (count, count), 0)
    across = lax.broadcasted_iota(jnp.int32, (count, count), 1)
    tall = jnp.sum(jnp.where(down == across, row, 0.0), axis=1, keepdims=True)
    return joined([tall] * copies, 0)


def lanes(value):
    return jnp.broadcast_to(value, (value.shape[0], 128))


def spread(block, rows, columns):
    height, width = block.shape
    tile = jnp.concatenate([block] * (128 // width), axis=1)
    parts = [tile] * (columns // 128)
    if columns % 128:
        parts.append(tile[:, : columns % 128])
    return joined([joined(parts, 1)] * (rows // height), 0)


def fetch_kernel(*refs):
    count = len(refs) // 2
    sems = refs[-1]
    copies = [
        pltpu.make_async_copy(refs[index], refs[count + index], sems.at[index])
        for index in range(count)
    ]
    for copy in copies:
        copy.start()
    for copy in copies:
        copy.wait()


def conv_kernel(paired, conv, conv_shift, *outs):
    places, fields, channels = conv.shape
    depth = places * fields
    wide = depth * GROUP
    flat = conv[...].astype(F32).reshape(depth, channels).astype(BF16)
    down = lax.broadcasted_iota(jnp.int32, (depth, wide), 0)
    across = lax.broadcasted_iota(jnp.int32, (depth, wide), 1)
    same = (down // fields == across // (GROUP * fields)) & (down % fields == across % fields)
    pick = jnp.where(same, 1.0, 0.0).astype(BF16)
    full = lax.dot_general(flat, pick, (((0,), (0,)), ((), ())), preferred_element_type=F32)
    full = jnp.concatenate([full] * GROUP, axis=0)
    down = lax.broadcasted_iota(jnp.int32, full.shape, 0)
    across = lax.broadcasted_iota(jnp.int32, full.shape, 1)
    keep = down // channels == across // fields % GROUP
    full = jnp.where(keep, 0.5 * full, 0.0)
    third = wide // 3
    turned = jnp.concatenate([full[:, 2 * third :], full[:, third : -third], full[:, :third]], axis=1)
    even = parity(paired) == 0
    outs[0][...] = full.astype(BF16)
    outs[1][...] = jnp.where(even, full, turned).astype(BF16)
    outs[2][...] = jnp.where(even, turned, full).astype(BF16)
    outs[3][...] = lanes(0.5 * column(conv_shift[...], GROUP))


def levels_kernel(slot_of, frames, taps, tap_shift, mix, mix_shift, *outs):
    tap_outs, tap_shift_outs = outs[:LEVELS], outs[LEVELS : 2 * LEVELS]
    mix_out, mix_shift_out = outs[2 * LEVELS :]
    channels = mix.shape[-1]
    slots = slot_of(lax.axis_index("tm"))
    for level in range(LEVELS):
        rows, columns = tap_outs[level].shape
        columns //= level + 1

        def frame_of(axis):
            place = lax.broadcasted_iota(jnp.int32, (rows, columns), axis) // channels
            block = place // frames
            start = jnp.zeros((rows, columns), jnp.int32)
            for index, slot in enumerate(slots[: (rows, columns)[axis] // channels // frames]):
                start = jnp.where(block == index, slot * frames, start)
            return start + place % frames

        gap = frame_of(1) - frame_of(0)
        for source in range(level + 1):
            total = jnp.zeros((rows, columns), F32)
            for tap in range(3):
                block = taps[level, tap]
                if source:
                    block = jnp.dot(block, mix[source - 1], preferred_element_type=F32)
                block = spread(block.astype(F32), rows, columns)
                total = jnp.where(gap == (tap - 1) * 2**level, block, total)
            if not source:
                shift = column(tap_shift[level : level + 1], rows // channels)
                if level:
                    held = jnp.sum(mix_shift[:level], axis=0, keepdims=True)
                    held = total * spread(held, 1, columns)
                    shift = shift + jnp.sum(held, axis=1, keepdims=True)
                tap_shift_outs[level][...] = lanes(0.5 * shift)
            part = slice(source * columns, (source + 1) * columns)
            tap_outs[level][:, part] = (0.5 * total).astype(BF16)
    size = mix_out.shape[0]
    down = lax.broadcasted_iota(jnp.int32, (size, size), 0)
    across = lax.broadcasted_iota(jnp.int32, (size, size), 1)
    same = down // channels == across // channels
    mix_out[...] = jnp.concatenate(
        [
            jnp.where(same, spread(mix[level].astype(F32), size, size), 0.0).astype(BF16)
            for level in range(LEVELS)
        ],
        axis=1,
    )
    held = jnp.sum(mix_shift[...], axis=0, keepdims=True)
    mix_shift_out[...] = lanes(column(held, size // channels))


def shifted(lines):
    plane = lines.shape[-1]
    depth = lax.broadcasted_iota(jnp.int32, (1, plane), 1) % NZ
    blank = jnp.zeros_like(lines)
    below = jnp.where(depth == 0, blank, pltpu.roll(lines, 1, 1))
    above = jnp.where(depth == NZ - 1, blank, pltpu.roll(lines, plane - 1, 1))
    for delta_y in (-1, 0, 1):
        for piece in (below, lines, above):
            yield pltpu.roll(piece, -delta_y * NZ % plane, 1) if delta_y else piece


def parity(paired):
    return lax.rem(lax.axis_index("space"), 2) if paired else 0


def encode(windows, weights, frames, store):
    conv_shift, mix, mix_shift = weights[0], *weights[-2:]
    taps, tap_shifts = weights[1 : 1 + LEVELS], weights[1 + LEVELS : 1 + 2 * LEVELS]
    channels = conv_shift.shape[0] // GROUP
    groups = -(-taps[0].shape[1] // conv_shift.shape[0])
    held = []
    for conv, window in windows:
        parts = []
        for group in range(groups):
            summed = jnp.dot(conv[...], window(group), preferred_element_type=F32)
            parts.append(gelu_of_double(summed + wide(conv_shift[...], summed.shape[1])))
        held.append([joined(parts, 0)])
    for level, (tap, shift) in enumerate(zip(taps, tap_shifts)):
        columns = tap.shape[1] // (level + 1)
        for parts in held:
            read = joined([part[:columns] for part in parts], 0)
            summed = jnp.dot(tap[...], read, preferred_element_type=F32)
            parts.append(gelu_of_double(summed + wide(shift[...], summed.shape[1])))
    size = mix.shape[0]
    for index, (first, *gated) in enumerate(held):
        read = joined([part[:size] for part in gated], 0)
        mixed = jnp.dot(mix[...], read, preferred_element_type=F32)
        mixed = mixed + wide(mix_shift[...], mixed.shape[1])
        final = (first[:size].astype(F32) + mixed).astype(BF16)
        for frame in range(frames):
            store(index, frame, final[frame * channels : (frame + 1) * channels])


def stack(sources, group, depth, cells):
    part = slice(group * depth, (group + 1) * depth)
    return jnp.concatenate(
        [source[:, part, cells].reshape(9 * depth, -1) for source in sources], axis=0
    )


def pack_kernel(own, near, *outs):
    frames, row_count = near.shape[:2]
    even = parity(True) == 0
    first = lax.rem(lax.axis_index("tm"), 2) == 0
    rows = []
    for row in (0, row_count - 1):
        mine, beside = [
            jnp.concatenate([block[frame, row] for frame in range(frames)], axis=0)
            for block in (own, near)
        ]
        rows.append(
            jnp.concatenate(
                [jnp.where(first, mine, beside), jnp.where(first, beside, mine)], axis=0
            )
        )
    outs[2][0] = own[...]
    outs[2][1] = near[...]
    outs[0][...] = jnp.where(even, rows[0], rows[1])
    outs[1][...] = jnp.where(even, rows[1], rows[0])


def inner_kernel(paired, count, *refs):
    blocks, conv, weights, (patches, out) = refs[:count], refs[count], refs[count + 1 : -2], refs[-2:]
    if paired:
        own, near, beyond = blocks
        blocks = own, beyond.at[0], near, beyond.at[1]
    frames, row_count = blocks[0].shape[:2]
    plane = patches.shape[-1]
    for row in range(row_count):
        lines = [block[frame, row] for block in blocks for frame in range(frames)]
        for place, piece in enumerate(shifted(jnp.concatenate(lines, axis=0))):
            patches[row, place] = piece
    depth = conv.shape[1] // 27
    width = math.gcd(plane, CELLS)
    places = [
        (row, slice(start, start + width))
        for row in range(1, row_count - 1)
        for start in range(0, plane, width)
    ]
    windows = [
        (
            conv,
            functools.partial(
                stack, [patches.at[row + step] for step in (-1, 0, 1)], depth=depth, cells=cells
            ),
        )
        for row, cells in places
    ]

    def store(index, frame, final):
        row, cells = places[index]
        out[frame, row - 1, :, cells] = final

    encode(windows, weights, out.shape[0], store)


def merge_kernel(near, far, out):
    out[...] = jnp.concatenate([near[...], far[...]], axis=0)


def halo_lines(got, other):
    first = lax.rem(lax.axis_index("tm"), 2) == 0
    half = got.shape[0] // 2
    parts = [[], []]
    for held in (jnp.where(first, got, other), jnp.where(first, other, got)):
        upper, lower = held[:half], held[half:]
        parts[0].append(jnp.where(first, upper, lower))
        parts[1].append(jnp.where(first, lower, upper))
    return jnp.concatenate(parts[0] + parts[1], axis=0)


def edge_row(paired, far, row_count):
    top = (parity(paired) == 0) == far
    return jnp.where(top, 0, row_count - 1), jnp.where(top, 1, row_count - 2)


def outer_kernel(paired, near, far, *refs):
    near, far = near[...], far[...]
    if paired:
        half = refs[0].shape[0] // 2
        near = halo_lines(near, refs[0][:half])
        far = halo_lines(far, refs[0][half:])
        refs = refs[1:]
    halos = far, near
    patches, inner, *convs = refs[:4]
    weights, (out, borders, done, sems) = refs[4:-4], refs[-4:]
    row_count, _, _, plane = patches.shape
    depth = convs[0].shape[1] // 27
    width = math.gcd(plane, CELLS)
    rows = [edge_row(paired, far, row_count) for far in (True, False)]
    copies = [pltpu.make_async_copy(inner, out.at[:, 1 : row_count - 1], sems.at[0])]
    copies[0].start()
    windows = []
    places = []
    for side, (edge, inside) in enumerate(rows):
        for place, piece in enumerate(shifted(halos[side])):
            borders[side, place] = piece
        sources = [borders.at[side], patches.at[edge], patches.at[inside]]
        for start in range(0, plane, width):
            cells = slice(start, start + width)
            places.append((side, cells))
            windows.append(
                (convs[side], functools.partial(stack, sources, depth=depth, cells=cells))
            )

    def store(index, frame, final):
        side, cells = places[index]
        done[side, frame, :, cells] = final

    encode(windows, weights, out.shape[0], store)
    for side, (edge, _) in enumerate(rows):
        copies.append(pltpu.make_async_copy(done.at[side], out.at[:, edge], sems.at[side + 1]))
        copies[-1].start()
    for copy in copies:
        copy.wait()


VMEM = pl.BlockSpec(memory_space=pltpu.VMEM)
PARAMS = pltpu.CompilerParams(vmem_limit_bytes=40 * 2**20)


def cost(microseconds):
    size = int(microseconds * 3.7e6)
    return pl.CostEstimate(flops=0, bytes_accessed=size, transcendentals=0)


def ring(count, step):
    return [(index, (index + step) % count) for index in range(count)]


def shards(snapshots, conv_weight, conv_bias, tap_weight, tap_bias, mix_weight, mix_bias):
    frames, row_count, fields, plane = snapshots.shape
    channels = conv_weight.shape[0]
    times = lax.axis_size("tm")
    spaces = lax.axis_size("space")
    offsets, counts = frame_blocks(times, frames)
    paired = times == 4 and sorted(offsets) == [0, 1, 2, 3] and spaces % 2 == 0
    tall = GROUP * channels
    total = len(offsets) * frames * fields

    sources = [
        snapshots,
        conv_weight.transpose(2, 3, 4, 1, 0).reshape(27, fields, channels),
        conv_bias.reshape(1, channels),
        tap_weight.transpose(0, 2, 1, 3),
        tap_bias,
        mix_weight,
        mix_bias,
    ]
    sources = [pltpu.with_memory_space_constraint(source, pltpu.HBM) for source in sources]
    sources = pl.pallas_call(
        fetch_kernel,
        out_shape=[jax.ShapeDtypeStruct(source.shape, source.dtype) for source in sources],
        in_specs=[pl.BlockSpec(memory_space=pl.ANY)] * len(sources),
        out_specs=[VMEM] * len(sources),
        scratch_shapes=[pltpu.SemaphoreType.DMA((len(sources),))],
        compiler_params=PARAMS,
        cost_estimate=cost(0.8),
        name="fetch",
    )(*sources)

    if paired:
        offsets = [0, 2, 1, 3]
        slot_of = lambda index: [index ^ offset for offset in offsets]
        across = [(index, index ^ 2) for index in range(times)]
        beside = [(index, index ^ 1) for index in range(times)]
        near = lax.ppermute(snapshots, "tm", beside)
        to_far, to_near, pair = pl.pallas_call(
            pack_kernel,
            out_shape=[jax.ShapeDtypeStruct((total // 2, plane), BF16)] * 2
            + [jax.ShapeDtypeStruct((2,) + snapshots.shape, BF16)],
            in_specs=[VMEM] * 2,
            out_specs=[VMEM] * 3,
            compiler_params=PARAMS,
            cost_estimate=cost(0.05),
            name="pack",
        )(sources[0], near)
        far_pairs, near_pairs = [], []
        for time in range(times):
            for space in range(spaces):
                target = (time ^ (time % 2 * 2)) * spaces
                step = 2 * (space % 2) - 1
                far_pairs.append((time * spaces + space, target + (space + step) % spaces))
                near_pairs.append((time * spaces + space, target + space - step))
        beyond = lax.ppermute(pair, "tm", across)
        near_halo = lax.ppermute(to_near, ("tm", "space"), near_pairs)
        far_halo = lax.ppermute(to_far, ("tm", "space"), far_pairs)
    else:
        slot_of = lambda index: [(index + offset) % times for offset in offsets]

    own, conv, conv_shift, *levels = sources
    *convs, conv_shift = pl.pallas_call(
        functools.partial(conv_kernel, paired),
        out_shape=[jax.ShapeDtypeStruct((tall, 27 * GROUP * fields), BF16)] * 3
        + [jax.ShapeDtypeStruct((tall, 128), F32)],
        in_specs=[VMEM] * 2,
        out_specs=[VMEM] * 4,
        compiler_params=PARAMS,
        cost_estimate=cost(0.3),
        name="conv",
    )(conv, conv_shift)

    wide_of = [count * frames * channels for count in counts]
    shapes = []
    for level in range(LEVELS):
        shape = wide_of[level + 1], wide_of[level] * (level + 1)
        shapes.append(jax.ShapeDtypeStruct(shape, BF16))
    for level in range(LEVELS):
        shapes.append(jax.ShapeDtypeStruct((wide_of[level + 1], 128), F32))
    shapes += [
        jax.ShapeDtypeStruct((wide_of[LEVELS], wide_of[LEVELS] * LEVELS), BF16),
        jax.ShapeDtypeStruct((wide_of[LEVELS], 128), F32),
    ]
    weights = pl.pallas_call(
        functools.partial(levels_kernel, slot_of, frames),
        out_shape=shapes,
        in_specs=[VMEM] * 4,
        out_specs=[VMEM] * len(shapes),
        compiler_params=PARAMS,
        cost_estimate=cost(0.7),
        name="levels",
    )(*levels)
    weights = [conv_shift, *weights]

    if paired:
        blocks = [own, near, beyond]
    else:
        blocks = [own] + [
            lax.ppermute(snapshots, "tm", ring(times, -offset)) for offset in offsets[1:]
        ]
        low, high = [
            jnp.concatenate([block[:, row] for block in blocks], axis=0).reshape(total, plane)
            for row in (0, row_count - 1)
        ]
        halos = [
            lax.ppermute(low, "space", ring(spaces, -1)),
            lax.ppermute(high, "space", ring(spaces, 1)),
        ]

    patches, inner = pl.pallas_call(
        functools.partial(inner_kernel, paired, len(blocks)),
        out_shape=[
            jax.ShapeDtypeStruct((row_count, 9, total, plane), BF16),
            jax.ShapeDtypeStruct((frames, row_count - 2, channels, plane), BF16),
        ],
        in_specs=[VMEM] * (len(blocks) + 1 + len(weights)),
        out_specs=[VMEM] * 2,
        compiler_params=PARAMS,
        cost_estimate=cost(1.8),
        name="inner",
    )(*blocks, convs[0], *weights)

    if paired:
        near_halo, far_halo, inner = lax.optimization_barrier((near_halo, far_halo, inner))
        merged = pl.pallas_call(
            merge_kernel,
            out_shape=jax.ShapeDtypeStruct((total, plane), BF16),
            in_specs=[VMEM] * 2,
            out_specs=VMEM,
            compiler_params=PARAMS,
            cost_estimate=cost(0.05),
            name="merge",
        )(near_halo, far_halo)
        halos = [near_halo, far_halo, lax.ppermute(merged, "tm", beside)]

    return pl.pallas_call(
        functools.partial(outer_kernel, paired),
        out_shape=jax.ShapeDtypeStruct((frames, row_count, channels, plane), BF16),
        in_specs=[VMEM] * (len(halos) + 4 + len(weights)),
        out_specs=pl.BlockSpec(memory_space=pl.ANY),
        scratch_shapes=[
            pltpu.VMEM((2, 9, total, plane), BF16),
            pltpu.VMEM((2, frames, channels, plane), BF16),
            pltpu.SemaphoreType.DMA((3,)),
        ],
        compiler_params=PARAMS,
        cost_estimate=cost(2.5),
        name="outer",
    )(*halos, patches, inner, *convs[1:], *weights)


def solution(mesh):
    in_specs = (P("tm", "space", None, None), P(), P(), P(), P(), P(), P())
    out_specs = P("tm", "space", None, None)
    return jax.shard_map(shards, mesh=mesh, in_specs=in_specs, out_specs=out_specs, check_vma=False)
```

```python
import functools
import math

import jax
import jax.numpy as jnp
from jax import lax
from jax.experimental import pallas as pl
from jax.experimental.pallas import tpu as pltpu
from jax.sharding import PartitionSpec as P

LEVELS = 3
NZ = 32
GROUP = 4
CELLS = 256
SLOPE = math.sqrt(2.0 / math.pi)
CUBIC = SLOPE * 0.044715
BF16 = jnp.bfloat16
F32 = jnp.float32


def frame_blocks(axis_size, frames):
    needed = [0]
    counts = [1]
    for level in reversed(range(LEVELS)):
        reach = set()
        for offset in needed:
            for frame in range(frames):
                for step in (-(2**level), 2**level):
                    reach.add((offset + (frame + step) // frames) % axis_size)
        needed = needed + sorted(reach - set(needed))
        spare = [offset for offset in range(axis_size) if offset not in needed]
        while len(needed) * frames % GROUP and spare:
            needed.append(spare.pop(0))
        counts.append(len(needed))
    return needed, counts[::-1]


def gelu_of_double(half):
    inner = half * (2 * SLOPE + 8 * CUBIC * (half * half))
    return (half + half * jnp.tanh(inner)).astype(BF16)


def joined(parts, axis):
    return parts[0] if len(parts) == 1 else jnp.concatenate(parts, axis=axis)


def wide(shift, cells):
    return joined([shift] * (cells // 128), 1)


def column(row, copies):
    count = row.shape[1]
    down = lax.broadcasted_iota(jnp.int32, (count, count), 0)
    across = lax.broadcasted_iota(jnp.int32, (count, count), 1)
    tall = jnp.sum(jnp.where(down == across, row, 0.0), axis=1, keepdims=True)
    return joined([tall] * copies, 0)


def lanes(value):
    return jnp.broadcast_to(value, (value.shape[0], 128))


def spread(block, rows, columns):
    height, width = block.shape
    tile = jnp.concatenate([block] * (128 // width), axis=1)
    parts = [tile] * (columns // 128)
    if columns % 128:
        parts.append(tile[:, : columns % 128])
    return joined([joined(parts, 1)] * (rows // height), 0)


def fetch_kernel(*refs):
    count = len(refs) // 2
    sems = refs[-1]
    copies = [
        pltpu.make_async_copy(refs[index], refs[count + index], sems.at[index])
        for index in range(count)
    ]
    for copy in copies:
        copy.start()
    for copy in copies:
        copy.wait()


def conv_kernel(paired, conv, conv_shift, *outs):
    places, fields, channels = conv.shape
    depth = places * fields
    wide = depth * GROUP
    flat = conv[...].astype(F32).reshape(depth, channels).astype(BF16)
    down = lax.broadcasted_iota(jnp.int32, (depth, wide), 0)
    across = lax.broadcasted_iota(jnp.int32, (depth, wide), 1)
    same = (down // fields == across // (GROUP * fields)) & (down % fields == across % fields)
    pick = jnp.where(same, 1.0, 0.0).astype(BF16)
    full = lax.dot_general(flat, pick, (((0,), (0,)), ((), ())), preferred_element_type=F32)
    full = jnp.concatenate([full] * GROUP, axis=0)
    down = lax.broadcasted_iota(jnp.int32, full.shape, 0)
    across = lax.broadcasted_iota(jnp.int32, full.shape, 1)
    keep = down // channels == across // fields % GROUP
    full = jnp.where(keep, 0.5 * full, 0.0)
    third = wide // 3
    turned = jnp.concatenate([full[:, 2 * third :], full[:, third : -third], full[:, :third]], axis=1)
    even = parity(paired) == 0
    outs[0][...] = full.astype(BF16)
    outs[1][...] = jnp.where(even, full, turned).astype(BF16)
    outs[2][...] = jnp.where(even, turned, full).astype(BF16)
    outs[3][...] = lanes(0.5 * column(conv_shift[...], GROUP))


def levels_kernel(slot_of, frames, taps, tap_shift, mix, mix_shift, *outs):
    tap_outs, tap_shift_outs = outs[:LEVELS], outs[LEVELS : 2 * LEVELS]
    mix_out, mix_shift_out = outs[2 * LEVELS :]
    channels = mix.shape[-1]
    slots = slot_of(lax.axis_index("tm"))
    for level in range(LEVELS):
        rows, columns = tap_outs[level].shape
        columns //= level + 1

        def frame_of(axis):
            place = lax.broadcasted_iota(jnp.int32, (rows, columns), axis) // channels
            block = place // frames
            start = jnp.zeros((rows, columns), jnp.int32)
            for index, slot in enumerate(slots[: (rows, columns)[axis] // channels // frames]):
                start = jnp.where(block == index, slot * frames, start)
            return start + place % frames

        gap = frame_of(1) - frame_of(0)
        for source in range(level + 1):
            total = jnp.zeros((rows, columns), F32)
            for tap in range(3):
                block = taps[level, tap]
                if source:
                    block = jnp.dot(block, mix[source - 1], preferred_element_type=F32)
                block = spread(block.astype(F32), rows, columns)
                total = jnp.where(gap == (tap - 1) * 2**level, block, total)
            if not source:
                shift = column(tap_shift[level : level + 1], rows // channels)
                if level:
                    held = jnp.sum(mix_shift[:level], axis=0, keepdims=True)
                    held = total * spread(held, 1, columns)
                    shift = shift + jnp.sum(held, axis=1, keepdims=True)
                tap_shift_outs[level][...] = lanes(0.5 * shift)
            part = slice(source * columns, (source + 1) * columns)
            tap_outs[level][:, part] = (0.5 * total).astype(BF16)
    size = mix_out.shape[0]
    down = lax.broadcasted_iota(jnp.int32, (size, size), 0)
    across = lax.broadcasted_iota(jnp.int32, (size, size), 1)
    same = down // channels == across // channels
    mix_out[...] = jnp.concatenate(
        [
            jnp.where(same, spread(mix[level].astype(F32), size, size), 0.0).astype(BF16)
            for level in range(LEVELS)
        ],
        axis=1,
    )
    held = jnp.sum(mix_shift[...], axis=0, keepdims=True)
    mix_shift_out[...] = lanes(column(held, size // channels))


def shifted(lines):
    plane = lines.shape[-1]
    depth = lax.broadcasted_iota(jnp.int32, (1, plane), 1) % NZ
    blank = jnp.zeros_like(lines)
    below = jnp.where(depth == 0, blank, pltpu.roll(lines, 1, 1))
    above = jnp.where(depth == NZ - 1, blank, pltpu.roll(lines, plane - 1, 1))
    for delta_y in (-1, 0, 1):
        for piece in (below, lines, above):
            yield pltpu.roll(piece, -delta_y * NZ % plane, 1) if delta_y else piece


def parity(paired):
    return lax.rem(lax.axis_index("space"), 2) if paired else 0


def encode(windows, weights, frames, store):
    conv_shift, mix, mix_shift = weights[0], *weights[-2:]
    taps, tap_shifts = weights[1 : 1 + LEVELS], weights[1 + LEVELS : 1 + 2 * LEVELS]
    channels = conv_shift.shape[0] // GROUP
    groups = -(-taps[0].shape[1] // conv_shift.shape[0])
    held = []
    for conv, window in windows:
        parts = []
        for group in range(groups):
            summed = jnp.dot(conv[...], window(group), preferred_element_type=F32)
            parts.append(gelu_of_double(summed + wide(conv_shift[...], summed.shape[1])))
        held.append([joined(parts, 0)])
    for level, (tap, shift) in enumerate(zip(taps, tap_shifts)):
        columns = tap.shape[1] // (level + 1)
        for parts in held:
            read = joined([part[:columns] for part in parts], 0)
            summed = jnp.dot(tap[...], read, preferred_element_type=F32)
            parts.append(gelu_of_double(summed + wide(shift[...], summed.shape[1])))
    size = mix.shape[0]
    for index, (first, *gated) in enumerate(held):
        read = joined([part[:size] for part in gated], 0)
        mixed = jnp.dot(mix[...], read, preferred_element_type=F32)
        mixed = mixed + wide(mix_shift[...], mixed.shape[1])
        final = (first[:size].astype(F32) + mixed).astype(BF16)
        for frame in range(frames):
            store(index, frame, final[frame * channels : (frame + 1) * channels])


def stack(sources, group, depth, cells):
    part = slice(group * depth, (group + 1) * depth)
    return jnp.concatenate(
        [source[:, part, cells].reshape(9 * depth, -1) for source in sources], axis=0
    )


def pack_kernel(own, near, *outs):
    frames, row_count = near.shape[:2]
    even = parity(True) == 0
    first = lax.rem(lax.axis_index("tm"), 2) == 0
    rows = []
    for row in (0, row_count - 1):
        mine, beside = [
            jnp.concatenate([block[frame, row] for frame in range(frames)], axis=0)
            for block in (own, near)
        ]
        rows.append(
            jnp.concatenate(
                [jnp.where(first, mine, beside), jnp.where(first, beside, mine)], axis=0
            )
        )
    outs[2][0] = own[...]
    outs[2][1] = near[...]
    outs[0][...] = jnp.where(even, rows[0], rows[1])
    outs[1][...] = jnp.where(even, rows[1], rows[0])


def inner_kernel(paired, count, *refs):
    blocks, conv, weights, (patches, out) = refs[:count], refs[count], refs[count + 1 : -2], refs[-2:]
    if paired:
        own, near, beyond = blocks
        blocks = own, beyond.at[0], near, beyond.at[1]
    frames, row_count = blocks[0].shape[:2]
    plane = patches.shape[-1]
    for row in range(row_count):
        lines = [block[frame, row] for block in blocks for frame in range(frames)]
        for place, piece in enumerate(shifted(jnp.concatenate(lines, axis=0))):
            patches[row, place] = piece
    depth = conv.shape[1] // 27
    width = math.gcd(plane, CELLS)
    places = [
        (row, slice(start, start + width))
        for row in range(1, row_count - 1)
        for start in range(0, plane, width)
    ]
    windows = [
        (
            conv,
            functools.partial(
                stack, [patches.at[row + step] for step in (-1, 0, 1)], depth=depth, cells=cells
            ),
        )
        for row, cells in places
    ]

    def store(index, frame, final):
        row, cells = places[index]
        out[frame, row - 1, :, cells] = final

    encode(windows, weights, out.shape[0], store)


def merge_kernel(near, far, out):
    out[...] = jnp.concatenate([near[...], far[...]], axis=0)


def halo_lines(got, other):
    first = lax.rem(lax.axis_index("tm"), 2) == 0
    half = got.shape[0] // 2
    parts = [[], []]
    for held in (jnp.where(first, got, other), jnp.where(first, other, got)):
        upper, lower = held[:half], held[half:]
        parts[0].append(jnp.where(first, upper, lower))
        parts[1].append(jnp.where(first, lower, upper))
    return jnp.concatenate(parts[0] + parts[1], axis=0)


def edge_row(paired, far, row_count):
    top = (parity(paired) == 0) == far
    return jnp.where(top, 0, row_count - 1), jnp.where(top, 1, row_count - 2)


def outer_kernel(paired, near, far, *refs):
    near, far = near[...], far[...]
    if paired:
        half = refs[0].shape[0] // 2
        near = halo_lines(near, refs[0][:half])
        far = halo_lines(far, refs[0][half:])
        refs = refs[1:]
    halos = far, near
    patches, inner, *convs = refs[:4]
    weights, (out, borders, done, sems) = refs[4:-4], refs[-4:]
    row_count, _, _, plane = patches.shape
    depth = convs[0].shape[1] // 27
    width = math.gcd(plane, CELLS)
    rows = [edge_row(paired, far, row_count) for far in (True, False)]
    copies = [pltpu.make_async_copy(inner, out.at[:, 1 : row_count - 1], sems.at[0])]
    copies[0].start()
    windows = []
    places = []
    for side, (edge, inside) in enumerate(rows):
        for place, piece in enumerate(shifted(halos[side])):
            borders[side, place] = piece
        sources = [borders.at[side], patches.at[edge], patches.at[inside]]
        for start in range(0, plane, width):
            cells = slice(start, start + width)
            places.append((side, cells))
            windows.append(
                (convs[side], functools.partial(stack, sources, depth=depth, cells=cells))
            )

    def store(index, frame, final):
        side, cells = places[index]
        done[side, frame, :, cells] = final

    encode(windows, weights, out.shape[0], store)
    for side, (edge, _) in enumerate(rows):
        copies.append(pltpu.make_async_copy(done.at[side], out.at[:, edge], sems.at[side + 1]))
        copies[-1].start()
    for copy in copies:
        copy.wait()


VMEM = pl.BlockSpec(memory_space=pltpu.VMEM)
PARAMS = pltpu.CompilerParams(vmem_limit_bytes=40 * 2**20)


def cost(microseconds):
    size = int(microseconds * 3.7e6 * 0.5)
    flops = int(microseconds * 1.15e9 * 0.5)
    return pl.CostEstimate(flops=flops, bytes_accessed=size, transcendentals=0)


def ring(count, step):
    return [(index, (index + step) % count) for index in range(count)]


def shards(snapshots, conv_weight, conv_bias, tap_weight, tap_bias, mix_weight, mix_bias):
    frames, row_count, fields, plane = snapshots.shape
    channels = conv_weight.shape[0]
    times = lax.axis_size("tm")
    spaces = lax.axis_size("space")
    offsets, counts = frame_blocks(times, frames)
    paired = times == 4 and sorted(offsets) == [0, 1, 2, 3] and spaces % 2 == 0
    tall = GROUP * channels
    total = len(offsets) * frames * fields

    sources = [
        snapshots,
        conv_weight.transpose(2, 3, 4, 1, 0).reshape(27, fields, channels),
        conv_bias.reshape(1, channels),
        tap_weight.transpose(0, 2, 1, 3),
        tap_bias,
        mix_weight,
        mix_bias,
    ]
    sources = [pltpu.with_memory_space_constraint(source, pltpu.HBM) for source in sources]
    sources = pl.pallas_call(
        fetch_kernel,
        out_shape=[jax.ShapeDtypeStruct(source.shape, source.dtype) for source in sources],
        in_specs=[pl.BlockSpec(memory_space=pl.ANY)] * len(sources),
        out_specs=[VMEM] * len(sources),
        scratch_shapes=[pltpu.SemaphoreType.DMA((len(sources),))],
        compiler_params=PARAMS,
        cost_estimate=cost(0.8),
        name="fetch",
    )(*sources)

    if paired:
        offsets = [0, 2, 1, 3]
        slot_of = lambda index: [index ^ offset for offset in offsets]
        across = [(index, index ^ 2) for index in range(times)]
        beside = [(index, index ^ 1) for index in range(times)]
        near = lax.ppermute(snapshots, "tm", beside)
        to_far, to_near, pair = pl.pallas_call(
            pack_kernel,
            out_shape=[jax.ShapeDtypeStruct((total // 2, plane), BF16)] * 2
            + [jax.ShapeDtypeStruct((2,) + snapshots.shape, BF16)],
            in_specs=[VMEM] * 2,
            out_specs=[VMEM] * 3,
            compiler_params=PARAMS,
            cost_estimate=cost(0.05),
            name="pack",
        )(sources[0], near)
        far_pairs, near_pairs = [], []
        for time in range(times):
            for space in range(spaces):
                target = (time ^ (time % 2 * 2)) * spaces
                step = 2 * (space % 2) - 1
                far_pairs.append((time * spaces + space, target + (space + step) % spaces))
                near_pairs.append((time * spaces + space, target + space - step))
        beyond = lax.ppermute(pair, "tm", across)
        near_halo = lax.ppermute(to_near, ("tm", "space"), near_pairs)
        far_halo = lax.ppermute(to_far, ("tm", "space"), far_pairs)
    else:
        slot_of = lambda index: [(index + offset) % times for offset in offsets]

    own, conv, conv_shift, *levels = sources
    if paired:
        near_halo, conv, conv_shift, *levels = lax.optimization_barrier(
            (near_halo, conv, conv_shift, *levels)
        )
    *convs, conv_shift = pl.pallas_call(
        functools.partial(conv_kernel, paired),
        out_shape=[jax.ShapeDtypeStruct((tall, 27 * GROUP * fields), BF16)] * 3
        + [jax.ShapeDtypeStruct((tall, 128), F32)],
        in_specs=[VMEM] * 2,
        out_specs=[VMEM] * 4,
        compiler_params=PARAMS,
        cost_estimate=cost(0.3),
        name="conv",
    )(conv, conv_shift)

    wide_of = [count * frames * channels for count in counts]
    shapes = []
    for level in range(LEVELS):
        shape = wide_of[level + 1], wide_of[level] * (level + 1)
        shapes.append(jax.ShapeDtypeStruct(shape, BF16))
    for level in range(LEVELS):
        shapes.append(jax.ShapeDtypeStruct((wide_of[level + 1], 128), F32))
    shapes += [
        jax.ShapeDtypeStruct((wide_of[LEVELS], wide_of[LEVELS] * LEVELS), BF16),
        jax.ShapeDtypeStruct((wide_of[LEVELS], 128), F32),
    ]
    weights = pl.pallas_call(
        functools.partial(levels_kernel, slot_of, frames),
        out_shape=shapes,
        in_specs=[VMEM] * 4,
        out_specs=[VMEM] * len(shapes),
        compiler_params=PARAMS,
        cost_estimate=cost(0.7),
        name="levels",
    )(*levels)
    weights = [conv_shift, *weights]

    if paired:
        blocks = [own, near, beyond]
    else:
        blocks = [own] + [
            lax.ppermute(snapshots, "tm", ring(times, -offset)) for offset in offsets[1:]
        ]
        low, high = [
            jnp.concatenate([block[:, row] for block in blocks], axis=0).reshape(total, plane)
            for row in (0, row_count - 1)
        ]
        halos = [
            lax.ppermute(low, "space", ring(spaces, -1)),
            lax.ppermute(high, "space", ring(spaces, 1)),
        ]

    patches, inner = pl.pallas_call(
        functools.partial(inner_kernel, paired, len(blocks)),
        out_shape=[
            jax.ShapeDtypeStruct((row_count, 9, total, plane), BF16),
            jax.ShapeDtypeStruct((frames, row_count - 2, channels, plane), BF16),
        ],
        in_specs=[VMEM] * (len(blocks) + 1 + len(weights)),
        out_specs=[VMEM] * 2,
        compiler_params=PARAMS,
        cost_estimate=cost(1.8),
        name="inner",
    )(*blocks, convs[0], *weights)

    if paired:
        near_halo, far_halo, inner = lax.optimization_barrier((near_halo, far_halo, inner))
        merged = pl.pallas_call(
            merge_kernel,
            out_shape=jax.ShapeDtypeStruct((total, plane), BF16),
            in_specs=[VMEM] * 2,
            out_specs=VMEM,
            compiler_params=PARAMS,
            cost_estimate=cost(0.05),
            name="merge",
        )(near_halo, far_halo)
        halos = [near_halo, far_halo, lax.ppermute(merged, "tm", beside)]

    return pl.pallas_call(
        functools.partial(outer_kernel, paired),
        out_shape=jax.ShapeDtypeStruct((frames, row_count, channels, plane), BF16),
        in_specs=[VMEM] * (len(halos) + 4 + len(weights)),
        out_specs=pl.BlockSpec(memory_space=pl.ANY),
        scratch_shapes=[
            pltpu.VMEM((2, 9, total, plane), BF16),
            pltpu.VMEM((2, frames, channels, plane), BF16),
            pltpu.SemaphoreType.DMA((3,)),
        ],
        compiler_params=PARAMS,
        cost_estimate=cost(2.5),
        name="outer",
    )(*halos, patches, inner, *convs[1:], *weights)


def solution(mesh):
    in_specs = (P("tm", "space", None, None), P(), P(), P(), P(), P(), P())
    out_specs = P("tm", "space", None, None)
    return jax.shard_map(shards, mesh=mesh, in_specs=in_specs, out_specs=out_specs, check_vma=False)
```

```python
import functools
import math

import jax
import jax.numpy as jnp
from jax import lax
from jax.experimental import pallas as pl
from jax.experimental.pallas import tpu as pltpu
from jax.sharding import PartitionSpec as P

LEVELS = 3
NZ = 32
GROUP = 4
CELLS = 256
SLOPE = math.sqrt(2.0 / math.pi)
CUBIC = SLOPE * 0.044715
BF16 = jnp.bfloat16
F32 = jnp.float32


def frame_blocks(axis_size, frames):
    needed = [0]
    counts = [1]
    for level in reversed(range(LEVELS)):
        reach = set()
        for offset in needed:
            for frame in range(frames):
                for step in (-(2**level), 2**level):
                    reach.add((offset + (frame + step) // frames) % axis_size)
        needed = needed + sorted(reach - set(needed))
        spare = [offset for offset in range(axis_size) if offset not in needed]
        while len(needed) * frames % GROUP and spare:
            needed.append(spare.pop(0))
        counts.append(len(needed))
    return needed, counts[::-1]


def gelu_of_double(half):
    inner = half * (2 * SLOPE + 8 * CUBIC * (half * half))
    return (half + half * jnp.tanh(inner)).astype(BF16)


def joined(parts, axis):
    return parts[0] if len(parts) == 1 else jnp.concatenate(parts, axis=axis)


def wide(shift, cells):
    return joined([shift] * (cells // 128), 1)


def column(row, copies):
    count = row.shape[1]
    down = lax.broadcasted_iota(jnp.int32, (count, count), 0)
    across = lax.broadcasted_iota(jnp.int32, (count, count), 1)
    tall = jnp.sum(jnp.where(down == across, row, 0.0), axis=1, keepdims=True)
    return joined([tall] * copies, 0)


def lanes(value):
    return jnp.broadcast_to(value, (value.shape[0], 128))


def spread(block, rows, columns):
    height, width = block.shape
    tile = jnp.concatenate([block] * (128 // width), axis=1)
    parts = [tile] * (columns // 128)
    if columns % 128:
        parts.append(tile[:, : columns % 128])
    return joined([joined(parts, 1)] * (rows // height), 0)


def fetch_kernel(*refs):
    count = len(refs) // 2
    sems = refs[-1]
    copies = [
        pltpu.make_async_copy(refs[index], refs[count + index], sems.at[index])
        for index in range(count)
    ]
    for copy in copies:
        copy.start()
    for copy in copies:
        copy.wait()


def conv_kernel(paired, conv, conv_shift, *outs):
    places, fields, channels = conv.shape
    depth = places * fields
    wide = depth * GROUP
    flat = conv[...].astype(F32).reshape(depth, channels).astype(BF16)
    down = lax.broadcasted_iota(jnp.int32, (depth, wide), 0)
    across = lax.broadcasted_iota(jnp.int32, (depth, wide), 1)
    same = (down // fields == across // (GROUP * fields)) & (down % fields == across % fields)
    pick = jnp.where(same, 1.0, 0.0).astype(BF16)
    full = lax.dot_general(flat, pick, (((0,), (0,)), ((), ())), preferred_element_type=F32)
    full = jnp.concatenate([full] * GROUP, axis=0)
    down = lax.broadcasted_iota(jnp.int32, full.shape, 0)
    across = lax.broadcasted_iota(jnp.int32, full.shape, 1)
    keep = down // channels == across // fields % GROUP
    full = jnp.where(keep, 0.5 * full, 0.0)
    third = wide // 3
    turned = jnp.concatenate([full[:, 2 * third :], full[:, third : -third], full[:, :third]], axis=1)
    even = parity(paired) == 0
    outs[0][...] = full.astype(BF16)
    outs[1][...] = jnp.where(even, full, turned).astype(BF16)
    outs[2][...] = jnp.where(even, turned, full).astype(BF16)
    outs[3][...] = lanes(0.5 * column(conv_shift[...], GROUP))


def levels_kernel(slot_of, frames, taps, tap_shift, mix, mix_shift, *outs):
    tap_outs, tap_shift_outs = outs[:LEVELS], outs[LEVELS : 2 * LEVELS]
    mix_out, mix_shift_out = outs[2 * LEVELS :]
    channels = mix.shape[-1]
    slots = slot_of(lax.axis_index("tm"))
    for level in range(LEVELS):
        rows, columns = tap_outs[level].shape
        columns //= level + 1

        def frame_of(axis):
            place = lax.broadcasted_iota(jnp.int32, (rows, columns), axis) // channels
            block = place // frames
            start = jnp.zeros((rows, columns), jnp.int32)
            for index, slot in enumerate(slots[: (rows, columns)[axis] // channels // frames]):
                start = jnp.where(block == index, slot * frames, start)
            return start + place % frames

        gap = frame_of(1) - frame_of(0)
        for source in range(level + 1):
            total = jnp.zeros((rows, columns), F32)
            for tap in range(3):
                block = taps[level, tap]
                if source:
                    block = jnp.dot(block, mix[source - 1], preferred_element_type=F32)
                block = spread(block.astype(F32), rows, columns)
                total = jnp.where(gap == (tap - 1) * 2**level, block, total)
            if not source:
                shift = column(tap_shift[level : level + 1], rows // channels)
                if level:
                    held = jnp.sum(mix_shift[:level], axis=0, keepdims=True)
                    held = total * spread(held, 1, columns)
                    shift = shift + jnp.sum(held, axis=1, keepdims=True)
                tap_shift_outs[level][...] = lanes(0.5 * shift)
            part = slice(source * columns, (source + 1) * columns)
            tap_outs[level][:, part] = (0.5 * total).astype(BF16)
    size = mix_out.shape[0]
    down = lax.broadcasted_iota(jnp.int32, (size, size), 0)
    across = lax.broadcasted_iota(jnp.int32, (size, size), 1)
    same = down // channels == across // channels
    mix_out[...] = jnp.concatenate(
        [
            jnp.where(same, spread(mix[level].astype(F32), size, size), 0.0).astype(BF16)
            for level in range(LEVELS)
        ],
        axis=1,
    )
    held = jnp.sum(mix_shift[...], axis=0, keepdims=True)
    mix_shift_out[...] = lanes(column(held, size // channels))


def shifted(lines):
    plane = lines.shape[-1]
    depth = lax.broadcasted_iota(jnp.int32, (1, plane), 1) % NZ
    blank = jnp.zeros_like(lines)
    below = jnp.where(depth == 0, blank, pltpu.roll(lines, 1, 1))
    above = jnp.where(depth == NZ - 1, blank, pltpu.roll(lines, plane - 1, 1))
    for delta_y in (-1, 0, 1):
        for piece in (below, lines, above):
            yield pltpu.roll(piece, -delta_y * NZ % plane, 1) if delta_y else piece


def parity(paired):
    return lax.rem(lax.axis_index("space"), 2) if paired else 0


def encode(windows, weights, frames, store):
    conv_shift, mix, mix_shift = weights[0], *weights[-2:]
    taps, tap_shifts = weights[1 : 1 + LEVELS], weights[1 + LEVELS : 1 + 2 * LEVELS]
    channels = conv_shift.shape[0] // GROUP
    groups = -(-taps[0].shape[1] // conv_shift.shape[0])
    held = []
    for conv, window in windows:
        parts = []
        for group in range(groups):
            summed = jnp.dot(conv[...], window(group), preferred_element_type=F32)
            parts.append(gelu_of_double(summed + wide(conv_shift[...], summed.shape[1])))
        held.append([joined(parts, 0)])
    for level, (tap, shift) in enumerate(zip(taps, tap_shifts)):
        columns = tap.shape[1] // (level + 1)
        for parts in held:
            read = joined([part[:columns] for part in parts], 0)
            summed = jnp.dot(tap[...], read, preferred_element_type=F32)
            parts.append(gelu_of_double(summed + wide(shift[...], summed.shape[1])))
    size = mix.shape[0]
    for index, (first, *gated) in enumerate(held):
        read = joined([part[:size] for part in gated], 0)
        mixed = jnp.dot(mix[...], read, preferred_element_type=F32)
        mixed = mixed + wide(mix_shift[...], mixed.shape[1])
        final = (first[:size].astype(F32) + mixed).astype(BF16)
        for frame in range(frames):
            store(index, frame, final[frame * channels : (frame + 1) * channels])


def stack(sources, group, depth, cells):
    part = slice(group * depth, (group + 1) * depth)
    return jnp.concatenate(
        [source[:, part, cells].reshape(9 * depth, -1) for source in sources], axis=0
    )


def pack_kernel(own, near, *outs):
    frames, row_count = near.shape[:2]
    even = parity(True) == 0
    first = lax.rem(lax.axis_index("tm"), 2) == 0
    rows = []
    for row in (0, row_count - 1):
        mine, beside = [
            jnp.concatenate([block[frame, row] for frame in range(frames)], axis=0)
            for block in (own, near)
        ]
        rows.append(
            jnp.concatenate(
                [jnp.where(first, mine, beside), jnp.where(first, beside, mine)], axis=0
            )
        )
    outs[2][0] = own[...]
    outs[2][1] = near[...]
    outs[0][...] = jnp.where(even, rows[0], rows[1])
    outs[1][...] = jnp.where(even, rows[1], rows[0])


def inner_kernel(paired, count, *refs):
    blocks, conv, weights, (patches, out) = refs[:count], refs[count], refs[count + 1 : -2], refs[-2:]
    if paired:
        own, near, beyond = blocks
        blocks = own, beyond.at[0], near, beyond.at[1]
    frames, row_count = blocks[0].shape[:2]
    plane = patches.shape[-1]
    for row in range(row_count):
        lines = [block[frame, row] for block in blocks for frame in range(frames)]
        for place, piece in enumerate(shifted(jnp.concatenate(lines, axis=0))):
            patches[row, place] = piece
    depth = conv.shape[1] // 27
    width = math.gcd(plane, CELLS)
    places = [
        (row, slice(start, start + width))
        for row in range(1, row_count - 1)
        for start in range(0, plane, width)
    ]
    windows = [
        (
            conv,
            functools.partial(
                stack, [patches.at[row + step] for step in (-1, 0, 1)], depth=depth, cells=cells
            ),
        )
        for row, cells in places
    ]

    def store(index, frame, final):
        row, cells = places[index]
        out[frame, row - 1, :, cells] = final

    encode(windows, weights, out.shape[0], store)


def halo_lines(got, other):
    first = lax.rem(lax.axis_index("tm"), 2) == 0
    half = got.shape[0] // 2
    parts = [[], []]
    for held in (jnp.where(first, got, other), jnp.where(first, other, got)):
        upper, lower = held[:half], held[half:]
        parts[0].append(jnp.where(first, upper, lower))
        parts[1].append(jnp.where(first, lower, upper))
    return jnp.concatenate(parts[0] + parts[1], axis=0)


def edge_row(paired, far, row_count):
    top = (parity(paired) == 0) == far
    return jnp.where(top, 0, row_count - 1), jnp.where(top, 1, row_count - 2)


def encode_edge(paired, far, halos, patches, conv, weights, border, frames, store):
    row_count, _, _, plane = patches.shape
    depth = conv.shape[1] // 27
    width = math.gcd(plane, CELLS)
    halo = halo_lines(halos[0][...], halos[1][...]) if paired else halos[0][...]
    for place, piece in enumerate(shifted(halo)):
        border[place] = piece
    edge, inside = edge_row(paired, far, row_count)
    sources = [border, patches.at[edge], patches.at[inside]]
    places = [slice(start, start + width) for start in range(0, plane, width)]
    windows = [
        (conv, functools.partial(stack, sources, depth=depth, cells=cells)) for cells in places
    ]
    encode(windows, weights, frames, lambda index, *result: store(places[index], *result))


def near_kernel(paired, count, *refs):
    halos, patches, conv = refs[:count], refs[count], refs[count + 1]
    weights, (out, border) = refs[count + 2 : -2], refs[-2:]

    def store(cells, frame, final):
        out[frame, :, cells] = final

    encode_edge(paired, False, halos, patches, conv, weights, border, out.shape[0], store)


def far_kernel(paired, count, *refs):
    halos, patches, inner, near, conv = refs[:count], *refs[count : count + 4]
    weights, (out, border, done, sems) = refs[count + 4 : -4], refs[-4:]
    row_count = patches.shape[0]
    far_row, near_row = [edge_row(paired, far, row_count)[0] for far in (True, False)]
    copies = [
        pltpu.make_async_copy(inner, out.at[:, 1 : row_count - 1], sems.at[0]),
        pltpu.make_async_copy(near, out.at[:, near_row], sems.at[1]),
    ]
    for copy in copies:
        copy.start()

    def store(cells, frame, final):
        done[frame, :, cells] = final

    encode_edge(paired, True, halos, patches, conv, weights, border, out.shape[0], store)
    copies.append(pltpu.make_async_copy(done, out.at[:, far_row], sems.at[2]))
    copies[-1].start()
    for copy in copies:
        copy.wait()


VMEM = pl.BlockSpec(memory_space=pltpu.VMEM)
PARAMS = pltpu.CompilerParams(vmem_limit_bytes=40 * 2**20)


def cost(microseconds):
    size, flops = int(microseconds * 3.7e6), int(microseconds * 1.15e9)
    return pl.CostEstimate(flops=flops, bytes_accessed=size, transcendentals=0)


def ring(count, step):
    return [(index, (index + step) % count) for index in range(count)]


def shards(snapshots, conv_weight, conv_bias, tap_weight, tap_bias, mix_weight, mix_bias):
    frames, row_count, fields, plane = snapshots.shape
    channels = conv_weight.shape[0]
    times = lax.axis_size("tm")
    spaces = lax.axis_size("space")
    offsets, counts = frame_blocks(times, frames)
    paired = times == 4 and sorted(offsets) == [0, 1, 2, 3] and spaces % 2 == 0
    tall = GROUP * channels
    total = len(offsets) * frames * fields

    sources = [
        snapshots,
        conv_weight.transpose(2, 3, 4, 1, 0).reshape(27, fields, channels),
        conv_bias.reshape(1, channels),
        tap_weight.transpose(0, 2, 1, 3),
        tap_bias,
        mix_weight,
        mix_bias,
    ]
    sources = [pltpu.with_memory_space_constraint(source, pltpu.HBM) for source in sources]
    sources = pl.pallas_call(
        fetch_kernel,
        out_shape=[jax.ShapeDtypeStruct(source.shape, source.dtype) for source in sources],
        in_specs=[pl.BlockSpec(memory_space=pl.ANY)] * len(sources),
        out_specs=[VMEM] * len(sources),
        scratch_shapes=[pltpu.SemaphoreType.DMA((len(sources),))],
        compiler_params=PARAMS,
        cost_estimate=cost(0.8),
        name="fetch",
    )(*sources)

    if paired:
        offsets = [0, 2, 1, 3]
        slot_of = lambda index: [index ^ offset for offset in offsets]
        across = [(index, index ^ 2) for index in range(times)]
        beside = [(index, index ^ 1) for index in range(times)]
        near = lax.ppermute(snapshots, "tm", beside)
        to_far, to_near, pair = pl.pallas_call(
            pack_kernel,
            out_shape=[jax.ShapeDtypeStruct((total // 2, plane), BF16)] * 2
            + [jax.ShapeDtypeStruct((2,) + snapshots.shape, BF16)],
            in_specs=[VMEM] * 2,
            out_specs=[VMEM] * 3,
            compiler_params=PARAMS,
            cost_estimate=cost(0.05),
            name="pack",
        )(sources[0], near)
        far_pairs, near_pairs = [], []
        for time in range(times):
            for space in range(spaces):
                target = (time ^ (time % 2 * 2)) * spaces
                step = 2 * (space % 2) - 1
                far_pairs.append((time * spaces + space, target + (space + step) % spaces))
                near_pairs.append((time * spaces + space, target + space - step))
        beyond = lax.ppermute(pair, "tm", across)
        near_halo = lax.ppermute(to_near, ("tm", "space"), near_pairs)
        far_halo = lax.ppermute(to_far, ("tm", "space"), far_pairs)
    else:
        slot_of = lambda index: [(index + offset) % times for offset in offsets]

    own, conv, conv_shift, *levels = sources
    if paired:
        near_halo, conv, conv_shift, *levels = lax.optimization_barrier(
            (near_halo, conv, conv_shift, *levels)
        )
    *convs, conv_shift = pl.pallas_call(
        functools.partial(conv_kernel, paired),
        out_shape=[jax.ShapeDtypeStruct((tall, 27 * GROUP * fields), BF16)] * 3
        + [jax.ShapeDtypeStruct((tall, 128), F32)],
        in_specs=[VMEM] * 2,
        out_specs=[VMEM] * 4,
        compiler_params=PARAMS,
        cost_estimate=cost(0.05),
        name="conv",
    )(conv, conv_shift)

    wide_of = [count * frames * channels for count in counts]
    shapes = []
    for level in range(LEVELS):
        shape = wide_of[level + 1], wide_of[level] * (level + 1)
        shapes.append(jax.ShapeDtypeStruct(shape, BF16))
    for level in range(LEVELS):
        shapes.append(jax.ShapeDtypeStruct((wide_of[level + 1], 128), F32))
    shapes += [
        jax.ShapeDtypeStruct((wide_of[LEVELS], wide_of[LEVELS] * LEVELS), BF16),
        jax.ShapeDtypeStruct((wide_of[LEVELS], 128), F32),
    ]
    weights = pl.pallas_call(
        functools.partial(levels_kernel, slot_of, frames),
        out_shape=shapes,
        in_specs=[VMEM] * 4,
        out_specs=[VMEM] * len(shapes),
        compiler_params=PARAMS,
        cost_estimate=cost(0.1),
        name="levels",
    )(*levels)
    weights = [conv_shift, *weights]

    if paired:
        near_halos = [near_halo, lax.ppermute(near_halo, "tm", beside)]
        near_halos[1], own = lax.optimization_barrier((near_halos[1], own))
        blocks = [own, near, beyond]
    else:
        blocks = [own] + [
            lax.ppermute(snapshots, "tm", ring(times, -offset)) for offset in offsets[1:]
        ]
        low, high = [
            jnp.concatenate([block[:, row] for block in blocks], axis=0).reshape(total, plane)
            for row in (0, row_count - 1)
        ]
        near_halos = [lax.ppermute(low, "space", ring(spaces, -1))]
        far_halos = [lax.ppermute(high, "space", ring(spaces, 1))]

    patches, inner = pl.pallas_call(
        functools.partial(inner_kernel, paired, len(blocks)),
        out_shape=[
            jax.ShapeDtypeStruct((row_count, 9, total, plane), BF16),
            jax.ShapeDtypeStruct((frames, row_count - 2, channels, plane), BF16),
        ],
        in_specs=[VMEM] * (len(blocks) + 1 + len(weights)),
        out_specs=[VMEM] * 2,
        compiler_params=PARAMS,
        cost_estimate=cost(0.01),
        name="inner",
    )(*blocks, convs[0], *weights)

    if paired:
        far_halo, patches, inner = lax.optimization_barrier((far_halo, patches, inner))
        far_halos = [far_halo, lax.ppermute(far_halo, "tm", beside)]

    near_row = pl.pallas_call(
        functools.partial(near_kernel, paired, len(near_halos)),
        out_shape=jax.ShapeDtypeStruct((frames, channels, plane), BF16),
        in_specs=[VMEM] * (len(near_halos) + 2 + len(weights)),
        out_specs=VMEM,
        scratch_shapes=[pltpu.VMEM((9, total, plane), BF16)],
        compiler_params=PARAMS,
        cost_estimate=cost(1.0),
        name="near",
    )(*near_halos, patches, convs[2], *weights)

    return pl.pallas_call(
        functools.partial(far_kernel, paired, len(far_halos)),
        out_shape=jax.ShapeDtypeStruct((frames, row_count, channels, plane), BF16),
        in_specs=[VMEM] * (len(far_halos) + 4 + len(weights)),
        out_specs=pl.BlockSpec(memory_space=pl.ANY),
        scratch_shapes=[
            pltpu.VMEM((9, total, plane), BF16),
            pltpu.VMEM((frames, channels, plane), BF16),
            pltpu.SemaphoreType.DMA((3,)),
        ],
        compiler_params=PARAMS,
        cost_estimate=cost(1.7),
        name="far",
    )(*far_halos, patches, inner, near_row, convs[1], *weights)


def solution(mesh):
    in_specs = (P("tm", "space", None, None), P(), P(), P(), P(), P(), P())
    out_specs = P("tm", "space", None, None)
    return jax.shard_map(shards, mesh=mesh, in_specs=in_specs, out_specs=out_specs, check_vma=False)
```

```python
import functools
import math

import jax
import jax.numpy as jnp
from jax import lax
from jax.experimental import pallas as pl
from jax.experimental.pallas import tpu as pltpu
from jax.sharding import PartitionSpec as P

LEVELS = 3
NZ = 32
GROUP = 4
CELLS = 256
SLOPE = math.sqrt(2.0 / math.pi)
CUBIC = SLOPE * 0.044715
BF16 = jnp.bfloat16
F32 = jnp.float32


def frame_blocks(axis_size, frames):
    needed = [0]
    counts = [1]
    for level in reversed(range(LEVELS)):
        reach = set()
        for offset in needed:
            for frame in range(frames):
                for step in (-(2**level), 2**level):
                    reach.add((offset + (frame + step) // frames) % axis_size)
        needed = needed + sorted(reach - set(needed))
        spare = [offset for offset in range(axis_size) if offset not in needed]
        while len(needed) * frames % GROUP and spare:
            needed.append(spare.pop(0))
        counts.append(len(needed))
    return needed, counts[::-1]


def gelu_of_double(half):
    inner = half * (2 * SLOPE + 8 * CUBIC * (half * half))
    return (half + half * jnp.tanh(inner)).astype(BF16)


def joined(parts, axis):
    return parts[0] if len(parts) == 1 else jnp.concatenate(parts, axis=axis)


def wide(shift, cells):
    return joined([shift] * (cells // 128), 1)


def column(row, copies):
    count = row.shape[1]
    down = lax.broadcasted_iota(jnp.int32, (count, count), 0)
    across = lax.broadcasted_iota(jnp.int32, (count, count), 1)
    tall = jnp.sum(jnp.where(down == across, row, 0.0), axis=1, keepdims=True)
    return joined([tall] * copies, 0)


def lanes(value):
    return jnp.broadcast_to(value, (value.shape[0], 128))


def spread(block, rows, columns):
    height, width = block.shape
    tile = jnp.concatenate([block] * (128 // width), axis=1)
    parts = [tile] * (columns // 128)
    if columns % 128:
        parts.append(tile[:, : columns % 128])
    return joined([joined(parts, 1)] * (rows // height), 0)


def fetch_kernel(*refs):
    count = len(refs) // 2
    sems = refs[-1]
    copies = [
        pltpu.make_async_copy(refs[index], refs[count + index], sems.at[index])
        for index in range(count)
    ]
    for copy in copies:
        copy.start()
    for copy in copies:
        copy.wait()


def conv_kernel(paired, conv, conv_shift, *outs):
    places, fields, channels = conv.shape
    depth = places * fields
    wide = depth * GROUP
    flat = conv[...].astype(F32).reshape(depth, channels).astype(BF16)
    down = lax.broadcasted_iota(jnp.int32, (depth, wide), 0)
    across = lax.broadcasted_iota(jnp.int32, (depth, wide), 1)
    same = (down // fields == across // (GROUP * fields)) & (down % fields == across % fields)
    pick = jnp.where(same, 1.0, 0.0).astype(BF16)
    full = lax.dot_general(flat, pick, (((0,), (0,)), ((), ())), preferred_element_type=F32)
    full = jnp.concatenate([full] * GROUP, axis=0)
    down = lax.broadcasted_iota(jnp.int32, full.shape, 0)
    across = lax.broadcasted_iota(jnp.int32, full.shape, 1)
    keep = down // channels == across // fields % GROUP
    full = jnp.where(keep, 0.5 * full, 0.0)
    third = wide // 3
    turned = jnp.concatenate([full[:, 2 * third :], full[:, third : -third], full[:, :third]], axis=1)
    even = parity(paired) == 0
    outs[0][...] = full.astype(BF16)
    outs[1][...] = jnp.where(even, full, turned).astype(BF16)
    outs[2][...] = jnp.where(even, turned, full).astype(BF16)
    outs[3][...] = lanes(0.5 * column(conv_shift[...], GROUP))


def levels_kernel(slot_of, frames, taps, tap_shift, mix, mix_shift, *outs):
    tap_outs, tap_shift_outs = outs[:LEVELS], outs[LEVELS : 2 * LEVELS]
    mix_out, mix_shift_out = outs[2 * LEVELS :]
    channels = mix.shape[-1]
    slots = slot_of(lax.axis_index("tm"))
    for level in range(LEVELS):
        rows, columns = tap_outs[level].shape
        columns //= level + 1

        def frame_of(axis):
            place = lax.broadcasted_iota(jnp.int32, (rows, columns), axis) // channels
            block = place // frames
            start = jnp.zeros((rows, columns), jnp.int32)
            for index, slot in enumerate(slots[: (rows, columns)[axis] // channels // frames]):
                start = jnp.where(block == index, slot * frames, start)
            return start + place % frames

        gap = frame_of(1) - frame_of(0)
        for source in range(level + 1):
            total = jnp.zeros((rows, columns), F32)
            for tap in range(3):
                block = taps[level, tap]
                if source:
                    block = jnp.dot(block, mix[source - 1], preferred_element_type=F32)
                block = spread(block.astype(F32), rows, columns)
                total = jnp.where(gap == (tap - 1) * 2**level, block, total)
            if not source:
                shift = column(tap_shift[level : level + 1], rows // channels)
                if level:
                    held = jnp.sum(mix_shift[:level], axis=0, keepdims=True)
                    held = total * spread(held, 1, columns)
                    shift = shift + jnp.sum(held, axis=1, keepdims=True)
                tap_shift_outs[level][...] = lanes(0.5 * shift)
            part = slice(source * columns, (source + 1) * columns)
            tap_outs[level][:, part] = (0.5 * total).astype(BF16)
    size = mix_out.shape[0]
    down = lax.broadcasted_iota(jnp.int32, (size, size), 0)
    across = lax.broadcasted_iota(jnp.int32, (size, size), 1)
    same = down // channels == across // channels
    mix_out[...] = jnp.concatenate(
        [
            jnp.where(same, spread(mix[level].astype(F32), size, size), 0.0).astype(BF16)
            for level in range(LEVELS)
        ],
        axis=1,
    )
    held = jnp.sum(mix_shift[...], axis=0, keepdims=True)
    mix_shift_out[...] = lanes(column(held, size // channels))


def shifted(lines):
    plane = lines.shape[-1]
    depth = lax.broadcasted_iota(jnp.int32, (1, plane), 1) % NZ
    blank = jnp.zeros_like(lines)
    below = jnp.where(depth == 0, blank, pltpu.roll(lines, 1, 1))
    above = jnp.where(depth == NZ - 1, blank, pltpu.roll(lines, plane - 1, 1))
    for delta_y in (-1, 0, 1):
        for piece in (below, lines, above):
            yield pltpu.roll(piece, -delta_y * NZ % plane, 1) if delta_y else piece


def parity(paired):
    return lax.rem(lax.axis_index("space"), 2) if paired else 0


def encode(windows, weights, frames, store):
    conv_shift, mix, mix_shift = weights[0], *weights[-2:]
    taps, tap_shifts = weights[1 : 1 + LEVELS], weights[1 + LEVELS : 1 + 2 * LEVELS]
    channels = conv_shift.shape[0] // GROUP
    groups = -(-taps[0].shape[1] // conv_shift.shape[0])
    held = []
    for conv, window in windows:
        parts = []
        for group in range(groups):
            summed = jnp.dot(conv[...], window(group), preferred_element_type=F32)
            parts.append(gelu_of_double(summed + wide(conv_shift[...], summed.shape[1])))
        held.append([joined(parts, 0)])
    for level, (tap, shift) in enumerate(zip(taps, tap_shifts)):
        columns = tap.shape[1] // (level + 1)
        for parts in held:
            read = joined([part[:columns] for part in parts], 0)
            summed = jnp.dot(tap[...], read, preferred_element_type=F32)
            parts.append(gelu_of_double(summed + wide(shift[...], summed.shape[1])))
    size = mix.shape[0]
    for index, (first, *gated) in enumerate(held):
        read = joined([part[:size] for part in gated], 0)
        mixed = jnp.dot(mix[...], read, preferred_element_type=F32)
        mixed = mixed + wide(mix_shift[...], mixed.shape[1])
        final = (first[:size].astype(F32) + mixed).astype(BF16)
        for frame in range(frames):
            store(index, frame, final[frame * channels : (frame + 1) * channels])


def stack(sources, group, depth, cells):
    part = slice(group * depth, (group + 1) * depth)
    return jnp.concatenate(
        [source[:, part, cells].reshape(9 * depth, -1) for source in sources], axis=0
    )


def pack_kernel(own, near, *outs):
    frames, row_count = near.shape[:2]
    even = parity(True) == 0
    first = lax.rem(lax.axis_index("tm"), 2) == 0
    rows = []
    for row in (0, row_count - 1):
        mine, beside = [
            jnp.concatenate([block[frame, row] for frame in range(frames)], axis=0)
            for block in (own, near)
        ]
        rows.append(
            jnp.concatenate(
                [jnp.where(first, mine, beside), jnp.where(first, beside, mine)], axis=0
            )
        )
    outs[0][...] = jnp.where(even, rows[0], rows[1])
    outs[1][...] = jnp.where(even, rows[1], rows[0])


def inner_kernel(count, *refs):
    blocks, conv, weights, (patches, out) = refs[:count], refs[count], refs[count + 1 : -2], refs[-2:]
    frames, row_count = blocks[0].shape[:2]
    plane = patches.shape[-1]
    for row in range(row_count):
        lines = [block[frame, row] for block in blocks for frame in range(frames)]
        for place, piece in enumerate(shifted(jnp.concatenate(lines, axis=0))):
            patches[row, place] = piece
    depth = conv.shape[1] // 27
    width = math.gcd(plane, CELLS)
    places = [
        (row, slice(start, start + width))
        for row in range(1, row_count - 1)
        for start in range(0, plane, width)
    ]
    windows = [
        (
            conv,
            functools.partial(
                stack, [patches.at[row + step] for step in (-1, 0, 1)], depth=depth, cells=cells
            ),
        )
        for row, cells in places
    ]

    def store(index, frame, final):
        row, cells = places[index]
        out[frame, row - 1, :, cells] = final

    encode(windows, weights, out.shape[0], store)


def halo_lines(got, other):
    first = lax.rem(lax.axis_index("tm"), 2) == 0
    half = got.shape[0] // 2
    parts = [[], []]
    for held in (jnp.where(first, got, other), jnp.where(first, other, got)):
        upper, lower = held[:half], held[half:]
        parts[0].append(jnp.where(first, upper, lower))
        parts[1].append(jnp.where(first, lower, upper))
    return jnp.concatenate(parts[0] + parts[1], axis=0)


def edge_row(paired, far, row_count):
    top = (parity(paired) == 0) == far
    return jnp.where(top, 0, row_count - 1), jnp.where(top, 1, row_count - 2)


def encode_edge(paired, far, halos, patches, conv, weights, border, frames, store):
    row_count, _, _, plane = patches.shape
    depth = conv.shape[1] // 27
    width = math.gcd(plane, CELLS)
    halo = halo_lines(halos[0][...], halos[1][...]) if paired else halos[0][...]
    for place, piece in enumerate(shifted(halo)):
        border[place] = piece
    edge, inside = edge_row(paired, far, row_count)
    sources = [border, patches.at[edge], patches.at[inside]]
    places = [slice(start, start + width) for start in range(0, plane, width)]
    windows = [
        (conv, functools.partial(stack, sources, depth=depth, cells=cells)) for cells in places
    ]
    encode(windows, weights, frames, lambda index, *result: store(places[index], *result))


def near_kernel(paired, count, *refs):
    halos, patches, conv = refs[:count], refs[count], refs[count + 1]
    weights, (out, border) = refs[count + 2 : -2], refs[-2:]

    def store(cells, frame, final):
        out[frame, :, cells] = final

    encode_edge(paired, False, halos, patches, conv, weights, border, out.shape[0], store)


def far_kernel(paired, count, *refs):
    halos, patches, inner, near, conv = refs[:count], *refs[count : count + 4]
    weights, (out, border, done, sems) = refs[count + 4 : -4], refs[-4:]
    row_count = patches.shape[0]
    far_row, near_row = [edge_row(paired, far, row_count)[0] for far in (True, False)]
    copies = [
        pltpu.make_async_copy(inner, out.at[:, 1 : row_count - 1], sems.at[0]),
        pltpu.make_async_copy(near, out.at[:, near_row], sems.at[1]),
    ]
    for copy in copies:
        copy.start()

    def store(cells, frame, final):
        done[frame, :, cells] = final

    encode_edge(paired, True, halos, patches, conv, weights, border, out.shape[0], store)
    copies.append(pltpu.make_async_copy(done, out.at[:, far_row], sems.at[2]))
    copies[-1].start()
    for copy in copies:
        copy.wait()


VMEM = pl.BlockSpec(memory_space=pltpu.VMEM)
PARAMS = pltpu.CompilerParams(vmem_limit_bytes=40 * 2**20)


def cost(microseconds):
    size, flops = int(microseconds * 3.7e6), int(microseconds * 1.15e9)
    return pl.CostEstimate(flops=flops, bytes_accessed=size, transcendentals=0)


def ring(count, step):
    return [(index, (index + step) % count) for index in range(count)]


def shards(snapshots, conv_weight, conv_bias, tap_weight, tap_bias, mix_weight, mix_bias):
    frames, row_count, fields, plane = snapshots.shape
    channels = conv_weight.shape[0]
    times = lax.axis_size("tm")
    spaces = lax.axis_size("space")
    offsets, counts = frame_blocks(times, frames)
    paired = times == 4 and sorted(offsets) == [0, 1, 2, 3] and spaces % 2 == 0
    tall = GROUP * channels
    total = len(offsets) * frames * fields

    sources = [
        snapshots,
        conv_weight.transpose(2, 3, 4, 1, 0).reshape(27, fields, channels),
        conv_bias.reshape(1, channels),
        tap_weight.transpose(0, 2, 1, 3),
        tap_bias,
        mix_weight,
        mix_bias,
    ]
    sources = [pltpu.with_memory_space_constraint(source, pltpu.HBM) for source in sources]
    sources = pl.pallas_call(
        fetch_kernel,
        out_shape=[jax.ShapeDtypeStruct(source.shape, source.dtype) for source in sources],
        in_specs=[pl.BlockSpec(memory_space=pl.ANY)] * len(sources),
        out_specs=[VMEM] * len(sources),
        scratch_shapes=[pltpu.SemaphoreType.DMA((len(sources),))],
        compiler_params=PARAMS,
        cost_estimate=cost(0.01),
        name="fetch",
    )(*sources)

    if paired:
        offsets = [0, 2, 1, 3]
        slot_of = lambda index: [index ^ offset for offset in offsets]
        across = [(index, index ^ 2) for index in range(times)]
        beside = [(index, index ^ 1) for index in range(times)]
        near = lax.ppermute(snapshots, "tm", beside)
        far = lax.ppermute(snapshots, "tm", across)
        to_far, to_near = pl.pallas_call(
            pack_kernel,
            out_shape=[jax.ShapeDtypeStruct((total // 2, plane), BF16)] * 2,
            in_specs=[VMEM] * 2,
            out_specs=[VMEM] * 2,
            compiler_params=PARAMS,
            cost_estimate=cost(0.3),
            name="pack",
        )(sources[0], near)
        far_pairs, near_pairs = [], []
        for time in range(times):
            for space in range(spaces):
                target = (time ^ (time % 2 * 2)) * spaces
                step = 2 * (space % 2) - 1
                far_pairs.append((time * spaces + space, target + (space + step) % spaces))
                near_pairs.append((time * spaces + space, target + space - step))
        near_halo = lax.ppermute(to_near, ("tm", "space"), near_pairs)
        far_halo = lax.ppermute(to_far, ("tm", "space"), far_pairs)
    else:
        slot_of = lambda index: [(index + offset) % times for offset in offsets]

    own, conv, conv_shift, *levels = sources
    if paired:
        near_halo, far, conv, conv_shift, *levels = lax.optimization_barrier(
            (near_halo, far, conv, conv_shift, *levels)
        )
    *convs, conv_shift = pl.pallas_call(
        functools.partial(conv_kernel, paired),
        out_shape=[jax.ShapeDtypeStruct((tall, 27 * GROUP * fields), BF16)] * 3
        + [jax.ShapeDtypeStruct((tall, 128), F32)],
        in_specs=[VMEM] * 2,
        out_specs=[VMEM] * 4,
        compiler_params=PARAMS,
        cost_estimate=cost(0.3),
        name="conv",
    )(conv, conv_shift)

    wide_of = [count * frames * channels for count in counts]
    shapes = []
    for level in range(LEVELS):
        shape = wide_of[level + 1], wide_of[level] * (level + 1)
        shapes.append(jax.ShapeDtypeStruct(shape, BF16))
    for level in range(LEVELS):
        shapes.append(jax.ShapeDtypeStruct((wide_of[level + 1], 128), F32))
    shapes += [
        jax.ShapeDtypeStruct((wide_of[LEVELS], wide_of[LEVELS] * LEVELS), BF16),
        jax.ShapeDtypeStruct((wide_of[LEVELS], 128), F32),
    ]
    weights = pl.pallas_call(
        functools.partial(levels_kernel, slot_of, frames),
        out_shape=shapes,
        in_specs=[VMEM] * 4,
        out_specs=[VMEM] * len(shapes),
        compiler_params=PARAMS,
        cost_estimate=cost(0.7),
        name="levels",
    )(*levels)
    weights = [conv_shift, *weights]

    if paired:
        both = lax.ppermute(far, "tm", beside)
        near_halos = [near_halo, lax.ppermute(near_halo, "tm", beside)]
        near_halos[1], own = lax.optimization_barrier((near_halos[1], own))
        blocks = [own, far, near, both]
    else:
        blocks = [own] + [
            lax.ppermute(snapshots, "tm", ring(times, -offset)) for offset in offsets[1:]
        ]
        low, high = [
            jnp.concatenate([block[:, row] for block in blocks], axis=0).reshape(total, plane)
            for row in (0, row_count - 1)
        ]
        near_halos = [lax.ppermute(low, "space", ring(spaces, -1))]
        far_halos = [lax.ppermute(high, "space", ring(spaces, 1))]

    patches, inner = pl.pallas_call(
        functools.partial(inner_kernel, len(blocks)),
        out_shape=[
            jax.ShapeDtypeStruct((row_count, 9, total, plane), BF16),
            jax.ShapeDtypeStruct((frames, row_count - 2, channels, plane), BF16),
        ],
        in_specs=[VMEM] * (len(blocks) + 1 + len(weights)),
        out_specs=[VMEM] * 2,
        compiler_params=PARAMS,
        cost_estimate=cost(0.01),
        name="inner",
    )(*blocks, convs[0], *weights)

    if paired:
        far_halo, patches, inner = lax.optimization_barrier((far_halo, patches, inner))
        far_halos = [far_halo, lax.ppermute(far_halo, "tm", beside)]

    near_row = pl.pallas_call(
        functools.partial(near_kernel, paired, len(near_halos)),
        out_shape=jax.ShapeDtypeStruct((frames, channels, plane), BF16),
        in_specs=[VMEM] * (len(near_halos) + 2 + len(weights)),
        out_specs=VMEM,
        scratch_shapes=[pltpu.VMEM((9, total, plane), BF16)],
        compiler_params=PARAMS,
        cost_estimate=cost(1),
        name="near",
    )(*near_halos, patches, convs[2], *weights)

    return pl.pallas_call(
        functools.partial(far_kernel, paired, len(far_halos)),
        out_shape=jax.ShapeDtypeStruct((frames, row_count, channels, plane), BF16),
        in_specs=[VMEM] * (len(far_halos) + 4 + len(weights)),
        out_specs=pl.BlockSpec(memory_space=pl.ANY),
        scratch_shapes=[
            pltpu.VMEM((9, total, plane), BF16),
            pltpu.VMEM((frames, channels, plane), BF16),
            pltpu.SemaphoreType.DMA((3,)),
        ],
        compiler_params=PARAMS,
        cost_estimate=cost(1.7),
        name="far",
    )(*far_halos, patches, inner, near_row, convs[1], *weights)


def solution(mesh):
    in_specs = (P("tm", "space", None, None), P(), P(), P(), P(), P(), P())
    out_specs = P("tm", "space", None, None)
    return jax.shard_map(shards, mesh=mesh, in_specs=in_specs, out_specs=out_specs, check_vma=False)
```

```python
import functools
import math

import jax
import jax.numpy as jnp
from jax import lax
from jax.experimental import pallas as pl
from jax.experimental.pallas import tpu as pltpu
from jax.sharding import PartitionSpec as P

LEVELS = 3
NZ = 32
GROUP = 4
CELLS = 256
SLOPE = math.sqrt(2.0 / math.pi)
CUBIC = SLOPE * 0.044715
BF16 = jnp.bfloat16
F32 = jnp.float32


def frame_blocks(axis_size, frames):
    needed = [0]
    counts = [1]
    for level in reversed(range(LEVELS)):
        reach = set()
        for offset in needed:
            for frame in range(frames):
                for step in (-(2**level), 2**level):
                    reach.add((offset + (frame + step) // frames) % axis_size)
        needed = needed + sorted(reach - set(needed))
        spare = [offset for offset in range(axis_size) if offset not in needed]
        while len(needed) * frames % GROUP and spare:
            needed.append(spare.pop(0))
        counts.append(len(needed))
    return needed, counts[::-1]


def gelu_of_double(half):
    inner = half * (2 * SLOPE + 8 * CUBIC * (half * half))
    return (half + half * jnp.tanh(inner)).astype(BF16)


def joined(parts, axis):
    return parts[0] if len(parts) == 1 else jnp.concatenate(parts, axis=axis)


def wide(shift, cells):
    return joined([shift] * (cells // 128), 1)


def column(row, copies):
    count = row.shape[1]
    down = lax.broadcasted_iota(jnp.int32, (count, count), 0)
    across = lax.broadcasted_iota(jnp.int32, (count, count), 1)
    tall = jnp.sum(jnp.where(down == across, row, 0.0), axis=1, keepdims=True)
    return joined([tall] * copies, 0)


def lanes(value):
    return jnp.broadcast_to(value, (value.shape[0], 128))


def spread(block, rows, columns):
    height, width = block.shape
    tile = jnp.concatenate([block] * (128 // width), axis=1)
    parts = [tile] * (columns // 128)
    if columns % 128:
        parts.append(tile[:, : columns % 128])
    return joined([joined(parts, 1)] * (rows // height), 0)


def fetch_kernel(*refs):
    count = len(refs) // 2
    sems = refs[-1]
    copies = [
        pltpu.make_async_copy(refs[index], refs[count + index], sems.at[index])
        for index in range(count)
    ]
    for copy in copies:
        copy.start()
    for copy in copies:
        copy.wait()


def conv_kernel(paired, conv, conv_shift, *outs):
    places, fields, channels = conv.shape
    depth = places * fields
    wide = depth * GROUP
    flat = conv[...].astype(F32).reshape(depth, channels).astype(BF16)
    down = lax.broadcasted_iota(jnp.int32, (depth, wide), 0)
    across = lax.broadcasted_iota(jnp.int32, (1, wide), 1)
    field, group = lax.rem(across, fields), lax.rem(lax.div(across, fields), GROUP)
    same = down == lax.div(across, GROUP * fields) * fields + field
    pick = jnp.where(same, 1.0, 0.0).astype(BF16)
    full = lax.dot_general(flat, pick, (((0,), (0,)), ((), ())), preferred_element_type=F32)
    full = jnp.concatenate([full] * GROUP, axis=0)
    down = lax.broadcasted_iota(jnp.int32, full.shape, 0)
    keep = lax.div(down, channels) == group
    full = jnp.where(keep, 0.5 * full, 0.0)
    third = wide // 3
    turned = jnp.concatenate([full[:, 2 * third :], full[:, third : -third], full[:, :third]], axis=1)
    even = parity(paired) == 0
    outs[0][...] = full.astype(BF16)
    outs[1][...] = jnp.where(even, full, turned).astype(BF16)
    outs[2][...] = jnp.where(even, turned, full).astype(BF16)
    outs[3][...] = lanes(0.5 * column(conv_shift[...], GROUP))


def levels_kernel(slot_of, frames, taps, tap_shift, mix, mix_shift, *outs):
    tap_outs, tap_shift_outs = outs[:LEVELS], outs[LEVELS : 2 * LEVELS]
    mix_out, mix_shift_out = outs[2 * LEVELS :]
    channels = mix.shape[-1]
    slots = slot_of(lax.axis_index("tm"))
    for level in range(LEVELS):
        rows, columns = tap_outs[level].shape
        columns //= level + 1

        def frame_of(shape, axis, count):
            place = lax.div(lax.broadcasted_iota(jnp.int32, shape, axis), channels)
            block = lax.div(place, frames)
            start = jnp.zeros(shape, jnp.int32)
            for index, slot in enumerate(slots[: count // channels // frames]):
                start = jnp.where(block == index, slot * frames, start)
            return start + lax.rem(place, frames)

        before = spread(frame_of((rows, 128), 0, rows), rows, columns)
        gap = frame_of((1, columns), 1, columns) - before
        for source in range(level + 1):
            total = jnp.zeros((rows, columns), F32)
            for tap in range(3):
                block = taps[level, tap]
                if source:
                    block = jnp.dot(block, mix[source - 1], preferred_element_type=F32)
                block = spread(block.astype(F32), rows, columns)
                total = jnp.where(gap == (tap - 1) * 2**level, block, total)
            if not source:
                shift = column(tap_shift[level : level + 1], rows // channels)
                if level:
                    held = jnp.sum(mix_shift[:level], axis=0, keepdims=True)
                    held = total * spread(held, 1, columns)
                    shift = shift + jnp.sum(held, axis=1, keepdims=True)
                tap_shift_outs[level][...] = lanes(0.5 * shift)
            part = slice(source * columns, (source + 1) * columns)
            tap_outs[level][:, part] = (0.5 * total).astype(BF16)
    size = mix_out.shape[0]
    down = lax.broadcasted_iota(jnp.int32, (size, size), 0)
    across = lax.broadcasted_iota(jnp.int32, (size, size), 1)
    same = down // channels == across // channels
    mix_out[...] = jnp.concatenate(
        [
            jnp.where(same, spread(mix[level].astype(F32), size, size), 0.0).astype(BF16)
            for level in range(LEVELS)
        ],
        axis=1,
    )
    held = jnp.sum(mix_shift[...], axis=0, keepdims=True)
    mix_shift_out[...] = lanes(column(held, size // channels))


def shifted(lines):
    plane = lines.shape[-1]
    depth = lax.broadcasted_iota(jnp.int32, (1, plane), 1) % NZ
    blank = jnp.zeros_like(lines)
    below = jnp.where(depth == 0, blank, pltpu.roll(lines, 1, 1))
    above = jnp.where(depth == NZ - 1, blank, pltpu.roll(lines, plane - 1, 1))
    for delta_y in (-1, 0, 1):
        for piece in (below, lines, above):
            yield pltpu.roll(piece, -delta_y * NZ % plane, 1) if delta_y else piece


def parity(paired):
    return lax.rem(lax.axis_index("space"), 2) if paired else 0


def encode(windows, weights, frames, store):
    conv_shift, mix, mix_shift = weights[0], *weights[-2:]
    taps, tap_shifts = weights[1 : 1 + LEVELS], weights[1 + LEVELS : 1 + 2 * LEVELS]
    channels = conv_shift.shape[0] // GROUP
    groups = -(-taps[0].shape[1] // conv_shift.shape[0])
    held = []
    for conv, window in windows:
        parts = []
        for group in range(groups):
            summed = jnp.dot(conv[...], window(group), preferred_element_type=F32)
            parts.append(gelu_of_double(summed + wide(conv_shift[...], summed.shape[1])))
        held.append([joined(parts, 0)])
    for level, (tap, shift) in enumerate(zip(taps, tap_shifts)):
        columns = tap.shape[1] // (level + 1)
        for parts in held:
            read = joined([part[:columns] for part in parts], 0)
            summed = jnp.dot(tap[...], read, preferred_element_type=F32)
            parts.append(gelu_of_double(summed + wide(shift[...], summed.shape[1])))
    size = mix.shape[0]
    for index, (first, *gated) in enumerate(held):
        read = joined([part[:size] for part in gated], 0)
        mixed = jnp.dot(mix[...], read, preferred_element_type=F32)
        mixed = mixed + wide(mix_shift[...], mixed.shape[1])
        final = (first[:size].astype(F32) + mixed).astype(BF16)
        for frame in range(frames):
            store(index, frame, final[frame * channels : (frame + 1) * channels])


def stack(sources, group, depth, cells):
    part = slice(group * depth, (group + 1) * depth)
    return jnp.concatenate(
        [source[:, part, cells].reshape(9 * depth, -1) for source in sources], axis=0
    )


def pack_kernel(own, near, *outs):
    frames, row_count = near.shape[:2]
    even = parity(True) == 0
    first = lax.rem(lax.axis_index("tm"), 2) == 0
    rows = []
    for row in (0, row_count - 1):
        mine, beside = [
            jnp.concatenate([block[frame, row] for frame in range(frames)], axis=0)
            for block in (own, near)
        ]
        rows.append(
            jnp.concatenate(
                [jnp.where(first, mine, beside), jnp.where(first, beside, mine)], axis=0
            )
        )
    outs[2][0] = own[...]
    outs[2][1] = near[...]
    outs[0][...] = jnp.where(even, rows[0], rows[1])
    outs[1][...] = jnp.where(even, rows[1], rows[0])


def inner_kernel(paired, count, *refs):
    blocks, conv, weights, (patches, out) = refs[:count], refs[count], refs[count + 1 : -2], refs[-2:]
    if paired:
        own, near, beyond = blocks
        blocks = own, beyond.at[0], near, beyond.at[1]
    frames, row_count = blocks[0].shape[:2]
    plane = patches.shape[-1]
    for row in range(row_count):
        lines = [block[frame, row] for block in blocks for frame in range(frames)]
        for place, piece in enumerate(shifted(jnp.concatenate(lines, axis=0))):
            patches[row, place] = piece
    depth = conv.shape[1] // 27
    width = math.gcd(plane, CELLS)
    places = [
        (row, slice(start, start + width))
        for row in range(1, row_count - 1)
        for start in range(0, plane, width)
    ]
    windows = [
        (
            conv,
            functools.partial(
                stack, [patches.at[row + step] for step in (-1, 0, 1)], depth=depth, cells=cells
            ),
        )
        for row, cells in places
    ]

    def store(index, frame, final):
        row, cells = places[index]
        out[frame, row - 1, :, cells] = final

    encode(windows, weights, out.shape[0], store)


def halo_lines(got, other):
    first = lax.rem(lax.axis_index("tm"), 2) == 0
    half = got.shape[0] // 2
    parts = [[], []]
    for held in (jnp.where(first, got, other), jnp.where(first, other, got)):
        upper, lower = held[:half], held[half:]
        parts[0].append(jnp.where(first, upper, lower))
        parts[1].append(jnp.where(first, lower, upper))
    return jnp.concatenate(parts[0] + parts[1], axis=0)


def edge_row(paired, far, row_count):
    top = (parity(paired) == 0) == far
    return jnp.where(top, 0, row_count - 1), jnp.where(top, 1, row_count - 2)


def encode_edge(paired, far, halos, patches, conv, weights, border, frames, store):
    row_count, _, _, plane = patches.shape
    depth = conv.shape[1] // 27
    width = math.gcd(plane, CELLS)
    halo = halo_lines(halos[0][...], halos[1][...]) if paired else halos[0][...]
    for place, piece in enumerate(shifted(halo)):
        border[place] = piece
    edge, inside = edge_row(paired, far, row_count)
    sources = [border, patches.at[edge], patches.at[inside]]
    places = [slice(start, start + width) for start in range(0, plane, width)]
    windows = [
        (conv, functools.partial(stack, sources, depth=depth, cells=cells)) for cells in places
    ]
    encode(windows, weights, frames, lambda index, *result: store(places[index], *result))


def near_kernel(paired, count, *refs):
    halos, patches, conv = refs[:count], refs[count], refs[count + 1]
    weights, (out, border) = refs[count + 2 : -2], refs[-2:]

    def store(cells, frame, final):
        out[frame, :, cells] = final

    encode_edge(paired, False, halos, patches, conv, weights, border, out.shape[0], store)


def far_kernel(paired, count, *refs):
    halos, patches, inner, near, conv = refs[:count], *refs[count : count + 4]
    weights, (out, border, done, sems) = refs[count + 4 : -4], refs[-4:]
    row_count = patches.shape[0]
    far_row, near_row = [edge_row(paired, far, row_count)[0] for far in (True, False)]
    copies = [
        pltpu.make_async_copy(inner, out.at[:, 1 : row_count - 1], sems.at[0]),
        pltpu.make_async_copy(near, out.at[:, near_row], sems.at[1]),
    ]
    for copy in copies:
        copy.start()

    def store(cells, frame, final):
        done[frame, :, cells] = final
        if frame == out.shape[0] - 1:
            index = len(copies)
            copies.append(
                pltpu.make_async_copy(
                    done.at[:, :, cells], out.at[:, far_row, :, cells], sems.at[index]
                )
            )
            copies[index].start()

    encode_edge(paired, True, halos, patches, conv, weights, border, out.shape[0], store)
    for copy in copies:
        copy.wait()


VMEM = pl.BlockSpec(memory_space=pltpu.VMEM)
PARAMS = pltpu.CompilerParams(vmem_limit_bytes=40 * 2**20)


def cost(microseconds):
    size, flops = int(microseconds * 3.7e6), int(microseconds * 1.15e9)
    return pl.CostEstimate(flops=flops, bytes_accessed=size, transcendentals=0)


def ring(count, step):
    return [(index, (index + step) % count) for index in range(count)]


def shards(snapshots, conv_weight, conv_bias, tap_weight, tap_bias, mix_weight, mix_bias):
    frames, row_count, fields, plane = snapshots.shape
    channels = conv_weight.shape[0]
    times = lax.axis_size("tm")
    spaces = lax.axis_size("space")
    offsets, counts = frame_blocks(times, frames)
    paired = times == 4 and sorted(offsets) == [0, 1, 2, 3] and spaces % 2 == 0
    tall = GROUP * channels
    total = len(offsets) * frames * fields

    sources = [
        snapshots,
        conv_weight.transpose(2, 3, 4, 1, 0).reshape(27, fields, channels),
        conv_bias.reshape(1, channels),
        tap_weight.transpose(0, 2, 1, 3),
        tap_bias,
        mix_weight,
        mix_bias,
    ]
    sources = [pltpu.with_memory_space_constraint(source, pltpu.HBM) for source in sources]
    sources = pl.pallas_call(
        fetch_kernel,
        out_shape=[jax.ShapeDtypeStruct(source.shape, source.dtype) for source in sources],
        in_specs=[pl.BlockSpec(memory_space=pl.ANY)] * len(sources),
        out_specs=[VMEM] * len(sources),
        scratch_shapes=[pltpu.SemaphoreType.DMA((len(sources),))],
        compiler_params=PARAMS,
        cost_estimate=cost(0.8),
        name="fetch",
    )(*sources)

    if paired:
        offsets = [0, 2, 1, 3]
        slot_of = lambda index: [index ^ offset for offset in offsets]
        across = [(index, index ^ 2) for index in range(times)]
        beside = [(index, index ^ 1) for index in range(times)]
        near = lax.ppermute(snapshots, "tm", beside)
        to_far, to_near, pair = pl.pallas_call(
            pack_kernel,
            out_shape=[jax.ShapeDtypeStruct((total // 2, plane), BF16)] * 2
            + [jax.ShapeDtypeStruct((2,) + snapshots.shape, BF16)],
            in_specs=[VMEM] * 2,
            out_specs=[VMEM] * 3,
            compiler_params=PARAMS,
            cost_estimate=cost(0.05),
            name="pack",
        )(sources[0], near)
        far_pairs, near_pairs = [], []
        for time in range(times):
            for space in range(spaces):
                target = (time ^ (time % 2 * 2)) * spaces
                step = 2 * (space % 2) - 1
                far_pairs.append((time * spaces + space, target + (space + step) % spaces))
                near_pairs.append((time * spaces + space, target + space - step))
        beyond = lax.ppermute(pair, "tm", across)
        near_halo = lax.ppermute(to_near, ("tm", "space"), near_pairs)
        far_halo = lax.ppermute(to_far, ("tm", "space"), far_pairs)
    else:
        slot_of = lambda index: [(index + offset) % times for offset in offsets]

    own, conv, conv_shift, *levels = sources
    if paired:
        near_halo, conv, conv_shift, *levels = lax.optimization_barrier(
            (near_halo, conv, conv_shift, *levels)
        )
    *convs, conv_shift = pl.pallas_call(
        functools.partial(conv_kernel, paired),
        out_shape=[jax.ShapeDtypeStruct((tall, 27 * GROUP * fields), BF16)] * 3
        + [jax.ShapeDtypeStruct((tall, 128), F32)],
        in_specs=[VMEM] * 2,
        out_specs=[VMEM] * 4,
        compiler_params=PARAMS,
        cost_estimate=cost(0.05),
        name="conv",
    )(conv, conv_shift)

    wide_of = [count * frames * channels for count in counts]
    shapes = []
    for level in range(LEVELS):
        shape = wide_of[level + 1], wide_of[level] * (level + 1)
        shapes.append(jax.ShapeDtypeStruct(shape, BF16))
    for level in range(LEVELS):
        shapes.append(jax.ShapeDtypeStruct((wide_of[level + 1], 128), F32))
    shapes += [
        jax.ShapeDtypeStruct((wide_of[LEVELS], wide_of[LEVELS] * LEVELS), BF16),
        jax.ShapeDtypeStruct((wide_of[LEVELS], 128), F32),
    ]
    weights = pl.pallas_call(
        functools.partial(levels_kernel, slot_of, frames),
        out_shape=shapes,
        in_specs=[VMEM] * 4,
        out_specs=[VMEM] * len(shapes),
        compiler_params=PARAMS,
        cost_estimate=cost(0.1),
        name="levels",
    )(*levels)
    weights = [conv_shift, *weights]

    if paired:
        near_halos = [near_halo, lax.ppermute(near_halo, "tm", beside)]
        blocks = [own, near, beyond]
    else:
        blocks = [own] + [
            lax.ppermute(snapshots, "tm", ring(times, -offset)) for offset in offsets[1:]
        ]
        low, high = [
            jnp.concatenate([block[:, row] for block in blocks], axis=0).reshape(total, plane)
            for row in (0, row_count - 1)
        ]
        near_halos = [lax.ppermute(low, "space", ring(spaces, -1))]
        far_halos = [lax.ppermute(high, "space", ring(spaces, 1))]

    patches, inner = pl.pallas_call(
        functools.partial(inner_kernel, paired, len(blocks)),
        out_shape=[
            jax.ShapeDtypeStruct((row_count, 9, total, plane), BF16),
            jax.ShapeDtypeStruct((frames, row_count - 2, channels, plane), BF16),
        ],
        in_specs=[VMEM] * (len(blocks) + 1 + len(weights)),
        out_specs=[VMEM] * 2,
        compiler_params=PARAMS,
        cost_estimate=cost(0.2),
        name="inner",
    )(*blocks, convs[0], *weights)

    if paired:
        far_halo, patches, inner = lax.optimization_barrier((far_halo, patches, inner))
        far_halos = [far_halo, lax.ppermute(far_halo, "tm", beside)]

    near_row = pl.pallas_call(
        functools.partial(near_kernel, paired, len(near_halos)),
        out_shape=jax.ShapeDtypeStruct((frames, channels, plane), BF16),
        in_specs=[VMEM] * (len(near_halos) + 2 + len(weights)),
        out_specs=VMEM,
        scratch_shapes=[pltpu.VMEM((9, total, plane), BF16)],
        compiler_params=PARAMS,
        cost_estimate=cost(1),
        name="near",
    )(*near_halos, patches, convs[2], *weights)

    return pl.pallas_call(
        functools.partial(far_kernel, paired, len(far_halos)),
        out_shape=jax.ShapeDtypeStruct((frames, row_count, channels, plane), BF16),
        in_specs=[VMEM] * (len(far_halos) + 4 + len(weights)),
        out_specs=pl.BlockSpec(memory_space=pl.ANY),
        scratch_shapes=[
            pltpu.VMEM((9, total, plane), BF16),
            pltpu.VMEM((frames, channels, plane), BF16),
            pltpu.SemaphoreType.DMA((2 + plane // math.gcd(plane, CELLS),)),
        ],
        compiler_params=PARAMS,
        cost_estimate=cost(1.7),
        name="far",
    )(*far_halos, patches, inner, near_row, convs[1], *weights)


def solution(mesh):
    in_specs = (P("tm", "space", None, None), P(), P(), P(), P(), P(), P())
    out_specs = P("tm", "space", None, None)
    return jax.shard_map(shards, mesh=mesh, in_specs=in_specs, out_specs=out_specs, check_vma=False)
```

```python
import functools
import math

import jax
import jax.numpy as jnp
from jax import lax
from jax.experimental import pallas as pl
from jax.experimental.pallas import tpu as pltpu
from jax.sharding import PartitionSpec as P

LEVELS = 3
NZ = 32
GROUP = 4
CELLS = 256
SLOPE = math.sqrt(2.0 / math.pi)
CUBIC = SLOPE * 0.044715
BF16 = jnp.bfloat16
F32 = jnp.float32


def frame_blocks(axis_size, frames):
    needed = [0]
    counts = [1]
    for level in reversed(range(LEVELS)):
        reach = set()
        for offset in needed:
            for frame in range(frames):
                for step in (-(2**level), 2**level):
                    reach.add((offset + (frame + step) // frames) % axis_size)
        needed = needed + sorted(reach - set(needed))
        spare = [offset for offset in range(axis_size) if offset not in needed]
        while len(needed) * frames % GROUP and spare:
            needed.append(spare.pop(0))
        counts.append(len(needed))
    return needed, counts[::-1]


def gelu_of_double(half):
    inner = half * (2 * SLOPE + 8 * CUBIC * (half * half))
    return (half + half * jnp.tanh(inner)).astype(BF16)


def joined(parts, axis):
    return parts[0] if len(parts) == 1 else jnp.concatenate(parts, axis=axis)


def wide(shift, cells):
    return joined([shift] * (cells // 128), 1)


def column(row, copies):
    count = row.shape[1]
    down = lax.broadcasted_iota(jnp.int32, (count, count), 0)
    across = lax.broadcasted_iota(jnp.int32, (count, count), 1)
    tall = jnp.sum(jnp.where(down == across, row, 0.0), axis=1, keepdims=True)
    return joined([tall] * copies, 0)


def lanes(value):
    return jnp.broadcast_to(value, (value.shape[0], 128))


def spread(block, rows, columns):
    height, width = block.shape
    tile = jnp.concatenate([block] * (128 // width), axis=1)
    parts = [tile] * (columns // 128)
    if columns % 128:
        parts.append(tile[:, : columns % 128])
    return joined([joined(parts, 1)] * (rows // height), 0)


def fetch_kernel(*refs):
    count = len(refs) // 2
    sems = refs[-1]
    copies = [
        pltpu.make_async_copy(refs[index], refs[count + index], sems.at[index])
        for index in range(count)
    ]
    for copy in copies:
        copy.start()
    for copy in copies:
        copy.wait()


def conv_kernel(conv, conv_shift, *outs):
    places, fields, channels = conv.shape
    depth = places * fields
    wide = depth * GROUP
    flat = conv[...].astype(F32).reshape(depth, channels).astype(BF16)
    down = lax.broadcasted_iota(jnp.int32, (depth, wide), 0)
    across = lax.broadcasted_iota(jnp.int32, (depth, wide), 1)
    same = (down // fields == across // (GROUP * fields)) & (down % fields == across % fields)
    pick = jnp.where(same, 1.0, 0.0).astype(BF16)
    full = lax.dot_general(flat, pick, (((0,), (0,)), ((), ())), preferred_element_type=F32)
    full = jnp.concatenate([full] * GROUP, axis=0)
    down = lax.broadcasted_iota(jnp.int32, full.shape, 0)
    across = lax.broadcasted_iota(jnp.int32, full.shape, 1)
    keep = down // channels == across // fields % GROUP
    full = jnp.where(keep, 0.5 * full, 0.0)
    third = wide // 3
    turned = jnp.concatenate([full[:, 2 * third :], full[:, third : -third], full[:, :third]], axis=1)
    outs[0][...] = full.astype(BF16)
    outs[1][...] = turned.astype(BF16)
    outs[2][...] = lanes(0.5 * column(conv_shift[...], GROUP))


def levels_kernel(slot_of, frames, taps, tap_shift, mix, mix_shift, *outs):
    tap_outs, tap_shift_outs = outs[:LEVELS], outs[LEVELS : 2 * LEVELS]
    mix_out, mix_shift_out = outs[2 * LEVELS :]
    channels = mix.shape[-1]
    slots = slot_of(lax.axis_index("tm"))
    for level in range(LEVELS):
        rows, columns = tap_outs[level].shape
        columns //= level + 1

        def frame_of(axis):
            place = lax.broadcasted_iota(jnp.int32, (rows, columns), axis) // channels
            block = place // frames
            start = jnp.zeros((rows, columns), jnp.int32)
            for index, slot in enumerate(slots[: (rows, columns)[axis] // channels // frames]):
                start = jnp.where(block == index, slot * frames, start)
            return start + place % frames

        gap = frame_of(1) - frame_of(0)
        for source in range(level + 1):
            total = jnp.zeros((rows, columns), F32)
            for tap in range(3):
                block = taps[level, tap]
                if source:
                    block = jnp.dot(block, mix[source - 1], preferred_element_type=F32)
                block = spread(block.astype(F32), rows, columns)
                total = jnp.where(gap == (tap - 1) * 2**level, block, total)
            if not source:
                shift = column(tap_shift[level : level + 1], rows // channels)
                if level:
                    held = jnp.sum(mix_shift[:level], axis=0, keepdims=True)
                    held = total * spread(held, 1, columns)
                    shift = shift + jnp.sum(held, axis=1, keepdims=True)
                tap_shift_outs[level][...] = lanes(0.5 * shift)
            part = slice(source * columns, (source + 1) * columns)
            tap_outs[level][:, part] = (0.5 * total).astype(BF16)
    size = mix_out.shape[0]
    down = lax.broadcasted_iota(jnp.int32, (size, size), 0)
    across = lax.broadcasted_iota(jnp.int32, (size, size), 1)
    same = down // channels == across // channels
    mix_out[...] = jnp.concatenate(
        [
            jnp.where(same, spread(mix[level].astype(F32), size, size), 0.0).astype(BF16)
            for level in range(LEVELS)
        ],
        axis=1,
    )
    held = jnp.sum(mix_shift[...], axis=0, keepdims=True)
    mix_shift_out[...] = lanes(column(held, size // channels))


def shifted(lines):
    plane = lines.shape[-1]
    depth = lax.broadcasted_iota(jnp.int32, (1, plane), 1) % NZ
    blank = jnp.zeros_like(lines)
    below = jnp.where(depth == 0, blank, pltpu.roll(lines, 1, 1))
    above = jnp.where(depth == NZ - 1, blank, pltpu.roll(lines, plane - 1, 1))
    for delta_y in (-1, 0, 1):
        for piece in (below, lines, above):
            yield pltpu.roll(piece, -delta_y * NZ % plane, 1) if delta_y else piece


def encode(windows, weights, frames, store):
    conv_shift, mix, mix_shift = weights[0], *weights[-2:]
    taps, tap_shifts = weights[1 : 1 + LEVELS], weights[1 + LEVELS : 1 + 2 * LEVELS]
    channels = conv_shift.shape[0] // GROUP
    groups = -(-taps[0].shape[1] // conv_shift.shape[0])
    held = []
    for conv, window in windows:
        parts = []
        for group in range(groups):
            summed = jnp.dot(conv[...], window(group), preferred_element_type=F32)
            parts.append(gelu_of_double(summed + wide(conv_shift[...], summed.shape[1])))
        held.append([joined(parts, 0)])
    for level, (tap, shift) in enumerate(zip(taps, tap_shifts)):
        columns = tap.shape[1] // (level + 1)
        for parts in held:
            read = joined([part[:columns] for part in parts], 0)
            summed = jnp.dot(tap[...], read, preferred_element_type=F32)
            parts.append(gelu_of_double(summed + wide(shift[...], summed.shape[1])))
    size = mix.shape[0]
    for index, (first, *gated) in enumerate(held):
        read = joined([part[:size] for part in gated], 0)
        mixed = jnp.dot(mix[...], read, preferred_element_type=F32)
        mixed = mixed + wide(mix_shift[...], mixed.shape[1])
        final = (first[:size].astype(F32) + mixed).astype(BF16)
        for frame in range(frames):
            store(index, frame, final[frame * channels : (frame + 1) * channels])


def stack(sources, group, depth, cells):
    part = slice(group * depth, (group + 1) * depth)
    return jnp.concatenate(
        [source[:, part, cells].reshape(9 * depth, -1) for source in sources], axis=0
    )


def pack_kernel(own, near, *outs):
    frames, row_count = near.shape[:2]
    first = lax.rem(lax.axis_index("tm"), 2) == 0
    rows = []
    for row in (0, row_count - 1):
        mine, beside = [
            jnp.concatenate([block[frame, row] for frame in range(frames)], axis=0)
            for block in (own, near)
        ]
        rows.append(
            jnp.concatenate(
                [jnp.where(first, mine, beside), jnp.where(first, beside, mine)], axis=0
            )
        )
    outs[2][0] = own[...]
    outs[2][1] = near[...]
    outs[0][...] = rows[1]
    outs[1][...] = rows[0]


def inner_kernel(paired, count, *refs):
    blocks, conv, weights, (patches, out) = refs[:count], refs[count], refs[count + 1 : -2], refs[-2:]
    if paired:
        own, near, beyond = blocks
        blocks = own, beyond.at[0], near, beyond.at[1]
    frames, row_count = blocks[0].shape[:2]
    plane = patches.shape[-1]
    for row in range(row_count):
        lines = [block[frame, row] for block in blocks for frame in range(frames)]
        for place, piece in enumerate(shifted(jnp.concatenate(lines, axis=0))):
            patches[row, place] = piece
    depth = conv.shape[1] // 27
    width = math.gcd(plane, CELLS)
    places = [
        (row, slice(start, start + width))
        for row in range(1, row_count - 1)
        for start in range(0, plane, width)
    ]
    windows = [
        (
            conv,
            functools.partial(
                stack, [patches.at[row + step] for step in (-1, 0, 1)], depth=depth, cells=cells
            ),
        )
        for row, cells in places
    ]

    def store(index, frame, final):
        row, cells = places[index]
        out[frame, row - 1, :, cells] = final

    encode(windows, weights, out.shape[0], store)


def merge_kernel(near, far, out):
    out[...] = jnp.concatenate([near[...], far[...]], axis=0)


def halo_lines(got, other):
    first = lax.rem(lax.axis_index("tm"), 2) == 0
    half = got.shape[0] // 2
    parts = [[], []]
    for held in (jnp.where(first, got, other), jnp.where(first, other, got)):
        upper, lower = held[:half], held[half:]
        parts[0].append(jnp.where(first, upper, lower))
        parts[1].append(jnp.where(first, lower, upper))
    return jnp.concatenate(parts[0] + parts[1], axis=0)


def outer_kernel(paired, near, far, *refs):
    near, far = near[...], far[...]
    if paired:
        half = refs[0].shape[0] // 2
        near = halo_lines(near, refs[0][:half])
        far = halo_lines(far, refs[0][half:])
        refs = refs[1:]
    halos = far, near
    patches, inner, *convs = refs[:4]
    weights, (out, borders, done, sems) = refs[4:-4], refs[-4:]
    row_count, _, _, plane = patches.shape
    depth = convs[0].shape[1] // 27
    width = math.gcd(plane, CELLS)
    rows = [(0, 1), (row_count - 1, row_count - 2)]
    copies = [pltpu.make_async_copy(inner, out.at[:, 1 : row_count - 1], sems.at[0])]
    copies[0].start()
    windows = []
    places = []
    for side, (edge, inside) in enumerate(rows):
        for place, piece in enumerate(shifted(halos[side])):
            borders[side, place] = piece
        sources = [borders.at[side], patches.at[edge], patches.at[inside]]
        for start in range(0, plane, width):
            cells = slice(start, start + width)
            places.append((side, cells))
            windows.append(
                (convs[side], functools.partial(stack, sources, depth=depth, cells=cells))
            )

    def store(index, frame, final):
        side, cells = places[index]
        done[side, frame, :, cells] = final

    encode(windows, weights, out.shape[0], store)
    for side, (edge, _) in enumerate(rows):
        copies.append(pltpu.make_async_copy(done.at[side], out.at[:, edge], sems.at[side + 1]))
        copies[-1].start()
    for copy in copies:
        copy.wait()


VMEM = pl.BlockSpec(memory_space=pltpu.VMEM)
PARAMS = pltpu.CompilerParams(vmem_limit_bytes=40 * 2**20)


def cost(microseconds):
    size, flops = int(microseconds * 3.7e6), int(microseconds * 1.15e9)
    return pl.CostEstimate(flops=flops, bytes_accessed=size, transcendentals=0)


def ring(count, step):
    return [(index, (index + step) % count) for index in range(count)]


def shards(snapshots, conv_weight, conv_bias, tap_weight, tap_bias, mix_weight, mix_bias):
    frames, row_count, fields, plane = snapshots.shape
    channels = conv_weight.shape[0]
    times = lax.axis_size("tm")
    spaces = lax.axis_size("space")
    offsets, counts = frame_blocks(times, frames)
    paired = times == 4 and sorted(offsets) == [0, 1, 2, 3] and spaces % 2 == 0
    tall = GROUP * channels
    total = len(offsets) * frames * fields

    sources = [
        snapshots,
        conv_weight.transpose(2, 3, 4, 1, 0).reshape(27, fields, channels),
        conv_bias.reshape(1, channels),
        tap_weight.transpose(0, 2, 1, 3),
        tap_bias,
        mix_weight,
        mix_bias,
    ]
    sources = [pltpu.with_memory_space_constraint(source, pltpu.HBM) for source in sources]
    sources = pl.pallas_call(
        fetch_kernel,
        out_shape=[jax.ShapeDtypeStruct(source.shape, source.dtype) for source in sources],
        in_specs=[pl.BlockSpec(memory_space=pl.ANY)] * len(sources),
        out_specs=[VMEM] * len(sources),
        scratch_shapes=[pltpu.SemaphoreType.DMA((len(sources),))],
        compiler_params=PARAMS,
        cost_estimate=cost(0.8),
        name="fetch",
    )(*sources)

    if paired:
        offsets = [0, 2, 1, 3]
        slot_of = lambda index: [index ^ offset for offset in offsets]
        across = [(index, index ^ 2) for index in range(times)]
        beside = [(index, index ^ 1) for index in range(times)]
        near = lax.ppermute(snapshots, "tm", beside)
        to_far, to_near, pair = pl.pallas_call(
            pack_kernel,
            out_shape=[jax.ShapeDtypeStruct((total // 2, plane), BF16)] * 2
            + [jax.ShapeDtypeStruct((2,) + snapshots.shape, BF16)],
            in_specs=[VMEM] * 2,
            out_specs=[VMEM] * 3,
            compiler_params=PARAMS,
            cost_estimate=cost(0.05),
            name="pack",
        )(sources[0], near)
        far_pairs, near_pairs = [], []
        for time in range(times):
            for space in range(spaces):
                target = (time ^ (time % 2 * 2)) * spaces
                far_pairs.append((time * spaces + space, target + (space + 1) % spaces))
                near_pairs.append((time * spaces + space, target + (space - 1) % spaces))
        beyond = lax.ppermute(pair, "tm", across)
        near_halo = lax.ppermute(to_near, ("tm", "space"), near_pairs)
        far_halo = lax.ppermute(to_far, ("tm", "space"), far_pairs)
    else:
        slot_of = lambda index: [(index + offset) % times for offset in offsets]

    own, conv, conv_shift, *levels = sources
    *convs, conv_shift = pl.pallas_call(
        conv_kernel,
        out_shape=[jax.ShapeDtypeStruct((tall, 27 * GROUP * fields), BF16)] * 2
        + [jax.ShapeDtypeStruct((tall, 128), F32)],
        in_specs=[VMEM] * 2,
        out_specs=[VMEM] * 3,
        compiler_params=PARAMS,
        cost_estimate=cost(0.01),
        name="conv",
    )(conv, conv_shift)

    wide_of = [count * frames * channels for count in counts]
    shapes = []
    for level in range(LEVELS):
        shape = wide_of[level + 1], wide_of[level] * (level + 1)
        shapes.append(jax.ShapeDtypeStruct(shape, BF16))
    for level in range(LEVELS):
        shapes.append(jax.ShapeDtypeStruct((wide_of[level + 1], 128), F32))
    shapes += [
        jax.ShapeDtypeStruct((wide_of[LEVELS], wide_of[LEVELS] * LEVELS), BF16),
        jax.ShapeDtypeStruct((wide_of[LEVELS], 128), F32),
    ]
    weights = pl.pallas_call(
        functools.partial(levels_kernel, slot_of, frames),
        out_shape=shapes,
        in_specs=[VMEM] * 4,
        out_specs=[VMEM] * len(shapes),
        compiler_params=PARAMS,
        cost_estimate=cost(0.02),
        name="levels",
    )(*levels)
    weights = [conv_shift, *weights]

    if paired:
        blocks = [own, near, beyond]
    else:
        blocks = [own] + [
            lax.ppermute(snapshots, "tm", ring(times, -offset)) for offset in offsets[1:]
        ]
        low, high = [
            jnp.concatenate([block[:, row] for block in blocks], axis=0).reshape(total, plane)
            for row in (0, row_count - 1)
        ]
        halos = [
            lax.ppermute(low, "space", ring(spaces, -1)),
            lax.ppermute(high, "space", ring(spaces, 1)),
        ]

    if paired:
        far_halo, near_halo, *weights = lax.optimization_barrier((far_halo, near_halo, *weights))
        merged = pl.pallas_call(
            merge_kernel,
            out_shape=jax.ShapeDtypeStruct((total, plane), BF16),
            in_specs=[VMEM] * 2,
            out_specs=VMEM,
            compiler_params=PARAMS,
            cost_estimate=cost(0.05),
            name="merge",
        )(near_halo, far_halo)
        halos = [near_halo, far_halo, lax.ppermute(merged, "tm", beside)]

    patches, inner = pl.pallas_call(
        functools.partial(inner_kernel, paired, len(blocks)),
        out_shape=[
            jax.ShapeDtypeStruct((row_count, 9, total, plane), BF16),
            jax.ShapeDtypeStruct((frames, row_count - 2, channels, plane), BF16),
        ],
        in_specs=[VMEM] * (len(blocks) + 1 + len(weights)),
        out_specs=[VMEM] * 2,
        compiler_params=PARAMS,
        cost_estimate=cost(0.5),
        name="inner",
    )(*blocks, convs[0], *weights)

    return pl.pallas_call(
        functools.partial(outer_kernel, paired),
        out_shape=jax.ShapeDtypeStruct((frames, row_count, channels, plane), BF16),
        in_specs=[VMEM] * (len(halos) + 4 + len(weights)),
        out_specs=pl.BlockSpec(memory_space=pl.ANY),
        scratch_shapes=[
            pltpu.VMEM((2, 9, total, plane), BF16),
            pltpu.VMEM((2, frames, channels, plane), BF16),
            pltpu.SemaphoreType.DMA((3,)),
        ],
        compiler_params=PARAMS,
        cost_estimate=cost(2.5),
        name="outer",
    )(*halos, patches, inner, *convs, *weights)


def solution(mesh):
    in_specs = (P("tm", "space", None, None), P(), P(), P(), P(), P(), P())
    out_specs = P("tm", "space", None, None)
    return jax.shard_map(shards, mesh=mesh, in_specs=in_specs, out_specs=out_specs, check_vma=False)
```

```python
import functools
import math

import jax
import jax.numpy as jnp
from jax import lax
from jax.experimental import pallas as pl
from jax.experimental.pallas import tpu as pltpu
from jax.sharding import PartitionSpec as P

LEVELS = 3
NZ = 32
GROUP = 4
CELLS = 256
SLOPE = math.sqrt(2.0 / math.pi)
CUBIC = SLOPE * 0.044715
BF16 = jnp.bfloat16
F32 = jnp.float32


def frame_blocks(axis_size, frames):
    needed = [0]
    counts = [1]
    for level in reversed(range(LEVELS)):
        reach = set()
        for offset in needed:
            for frame in range(frames):
                for step in (-(2**level), 2**level):
                    reach.add((offset + (frame + step) // frames) % axis_size)
        needed = needed + sorted(reach - set(needed))
        spare = [offset for offset in range(axis_size) if offset not in needed]
        while len(needed) * frames % GROUP and spare:
            needed.append(spare.pop(0))
        counts.append(len(needed))
    return needed, counts[::-1]


def gelu_of_double(half):
    inner = half * (2 * SLOPE + 8 * CUBIC * (half * half))
    return (half + half * jnp.tanh(inner)).astype(BF16)


def joined(parts, axis):
    return parts[0] if len(parts) == 1 else jnp.concatenate(parts, axis=axis)


def wide(shift, cells):
    return joined([shift] * (cells // 128), 1)


def column(row, copies):
    count = row.shape[1]
    down = lax.broadcasted_iota(jnp.int32, (count, count), 0)
    across = lax.broadcasted_iota(jnp.int32, (count, count), 1)
    tall = jnp.sum(jnp.where(down == across, row, 0.0), axis=1, keepdims=True)
    return joined([tall] * copies, 0)


def lanes(value):
    return jnp.broadcast_to(value, (value.shape[0], 128))


def spread(block, rows, columns):
    height, width = block.shape
    tile = jnp.concatenate([block] * (128 // width), axis=1)
    parts = [tile] * (columns // 128)
    if columns % 128:
        parts.append(tile[:, : columns % 128])
    return joined([joined(parts, 1)] * (rows // height), 0)


def fetch_kernel(*refs):
    count = len(refs) // 2
    sems = refs[-1]
    copies = [
        pltpu.make_async_copy(refs[index], refs[count + index], sems.at[index])
        for index in range(count)
    ]
    for copy in copies:
        copy.start()
    for copy in copies:
        copy.wait()


def conv_kernel(conv, conv_shift, *outs):
    places, fields, channels = conv.shape
    depth = places * fields
    wide = depth * GROUP
    flat = conv[...].astype(F32).reshape(depth, channels).astype(BF16)
    down = lax.broadcasted_iota(jnp.int32, (depth, wide), 0)
    across = lax.broadcasted_iota(jnp.int32, (depth, wide), 1)
    same = (down // fields == across // (GROUP * fields)) & (down % fields == across % fields)
    pick = jnp.where(same, 1.0, 0.0).astype(BF16)
    full = lax.dot_general(flat, pick, (((0,), (0,)), ((), ())), preferred_element_type=F32)
    full = jnp.concatenate([full] * GROUP, axis=0)
    down = lax.broadcasted_iota(jnp.int32, full.shape, 0)
    across = lax.broadcasted_iota(jnp.int32, full.shape, 1)
    keep = down // channels == across // fields % GROUP
    full = jnp.where(keep, 0.5 * full, 0.0)
    third = wide // 3
    turned = jnp.concatenate([full[:, 2 * third :], full[:, third : -third], full[:, :third]], axis=1)
    outs[0][...] = full.astype(BF16)
    outs[1][...] = turned.astype(BF16)
    outs[2][...] = lanes(0.5 * column(conv_shift[...], GROUP))


def levels_kernel(slot_of, frames, taps, tap_shift, mix, mix_shift, *outs):
    tap_outs, tap_shift_outs = outs[:LEVELS], outs[LEVELS : 2 * LEVELS]
    mix_out, mix_shift_out = outs[2 * LEVELS :]
    channels = mix.shape[-1]
    slots = slot_of(lax.axis_index("tm"))
    for level in range(LEVELS):
        rows, columns = tap_outs[level].shape
        columns //= level + 1

        def frame_of(axis):
            place = lax.broadcasted_iota(jnp.int32, (rows, columns), axis) // channels
            block = place // frames
            start = jnp.zeros((rows, columns), jnp.int32)
            for index, slot in enumerate(slots[: (rows, columns)[axis] // channels // frames]):
                start = jnp.where(block == index, slot * frames, start)
            return start + place % frames

        gap = frame_of(1) - frame_of(0)
        for source in range(level + 1):
            total = jnp.zeros((rows, columns), F32)
            for tap in range(3):
                block = taps[level, tap]
                if source:
                    block = jnp.dot(block, mix[source - 1], preferred_element_type=F32)
                block = spread(block.astype(F32), rows, columns)
                total = jnp.where(gap == (tap - 1) * 2**level, block, total)
            if not source:
                shift = column(tap_shift[level : level + 1], rows // channels)
                if level:
                    held = jnp.sum(mix_shift[:level], axis=0, keepdims=True)
                    held = total * spread(held, 1, columns)
                    shift = shift + jnp.sum(held, axis=1, keepdims=True)
                tap_shift_outs[level][...] = lanes(0.5 * shift)
            part = slice(source * columns, (source + 1) * columns)
            tap_outs[level][:, part] = (0.5 * total).astype(BF16)
    size = mix_out.shape[0]
    down = lax.broadcasted_iota(jnp.int32, (size, size), 0)
    across = lax.broadcasted_iota(jnp.int32, (size, size), 1)
    same = down // channels == across // channels
    mix_out[...] = jnp.concatenate(
        [
            jnp.where(same, spread(mix[level].astype(F32), size, size), 0.0).astype(BF16)
            for level in range(LEVELS)
        ],
        axis=1,
    )
    held = jnp.sum(mix_shift[...], axis=0, keepdims=True)
    mix_shift_out[...] = lanes(column(held, size // channels))


def shifted(lines):
    plane = lines.shape[-1]
    depth = lax.broadcasted_iota(jnp.int32, (1, plane), 1) % NZ
    blank = jnp.zeros_like(lines)
    below = jnp.where(depth == 0, blank, pltpu.roll(lines, 1, 1))
    above = jnp.where(depth == NZ - 1, blank, pltpu.roll(lines, plane - 1, 1))
    for delta_y in (-1, 0, 1):
        for piece in (below, lines, above):
            yield pltpu.roll(piece, -delta_y * NZ % plane, 1) if delta_y else piece


def encode(windows, weights, frames, store):
    conv_shift, mix, mix_shift = weights[0], *weights[-2:]
    taps, tap_shifts = weights[1 : 1 + LEVELS], weights[1 + LEVELS : 1 + 2 * LEVELS]
    channels = conv_shift.shape[0] // GROUP
    groups = -(-taps[0].shape[1] // conv_shift.shape[0])
    held = []
    for conv, window in windows:
        parts = []
        for group in range(groups):
            summed = jnp.dot(conv[...], window(group), preferred_element_type=F32)
            parts.append(gelu_of_double(summed + wide(conv_shift[...], summed.shape[1])))
        held.append([joined(parts, 0)])
    for level, (tap, shift) in enumerate(zip(taps, tap_shifts)):
        columns = tap.shape[1] // (level + 1)
        for parts in held:
            read = joined([part[:columns] for part in parts], 0)
            summed = jnp.dot(tap[...], read, preferred_element_type=F32)
            parts.append(gelu_of_double(summed + wide(shift[...], summed.shape[1])))
    size = mix.shape[0]
    for index, (first, *gated) in enumerate(held):
        read = joined([part[:size] for part in gated], 0)
        mixed = jnp.dot(mix[...], read, preferred_element_type=F32)
        mixed = mixed + wide(mix_shift[...], mixed.shape[1])
        final = (first[:size].astype(F32) + mixed).astype(BF16)
        for frame in range(frames):
            store(index, frame, final[frame * channels : (frame + 1) * channels])


def stack(sources, group, depth, cells):
    part = slice(group * depth, (group + 1) * depth)
    return jnp.concatenate(
        [source[:, part, cells].reshape(9 * depth, -1) for source in sources], axis=0
    )


def pack_kernel(own, near, *outs):
    frames, row_count = near.shape[:2]
    first = lax.rem(lax.axis_index("tm"), 2) == 0
    rows = []
    for row in (0, row_count - 1):
        mine, beside = [
            jnp.concatenate([block[frame, row] for frame in range(frames)], axis=0)
            for block in (own, near)
        ]
        rows.append(
            jnp.concatenate(
                [jnp.where(first, mine, beside), jnp.where(first, beside, mine)], axis=0
            )
        )
    outs[2][0] = own[...]
    outs[2][1] = near[...]
    outs[0][...] = rows[1]
    outs[1][...] = rows[0]


def inner_kernel(paired, count, *refs):
    blocks, conv, weights, (patches, out) = refs[:count], refs[count], refs[count + 1 : -2], refs[-2:]
    if paired:
        own, near, beyond = blocks
        blocks = own, beyond.at[0], near, beyond.at[1]
    frames, row_count = blocks[0].shape[:2]
    plane = patches.shape[-1]
    for row in range(row_count):
        lines = [block[frame, row] for block in blocks for frame in range(frames)]
        for place, piece in enumerate(shifted(jnp.concatenate(lines, axis=0))):
            patches[row, place] = piece
    depth = conv.shape[1] // 27
    width = math.gcd(plane, CELLS)
    places = [
        (row, slice(start, start + width))
        for row in range(1, row_count - 1)
        for start in range(0, plane, width)
    ]
    windows = [
        (
            conv,
            functools.partial(
                stack, [patches.at[row + step] for step in (-1, 0, 1)], depth=depth, cells=cells
            ),
        )
        for row, cells in places
    ]

    def store(index, frame, final):
        row, cells = places[index]
        out[frame, row - 1, :, cells] = final

    encode(windows, weights, out.shape[0], store)


def merge_kernel(near, far, out):
    out[...] = jnp.concatenate([near[...], far[...]], axis=0)


def halo_lines(got, other):
    first = lax.rem(lax.axis_index("tm"), 2) == 0
    half = got.shape[0] // 2
    parts = [[], []]
    for held in (jnp.where(first, got, other), jnp.where(first, other, got)):
        upper, lower = held[:half], held[half:]
        parts[0].append(jnp.where(first, upper, lower))
        parts[1].append(jnp.where(first, lower, upper))
    return jnp.concatenate(parts[0] + parts[1], axis=0)


def outer_kernel(paired, near, far, *refs):
    near, far = near[...], far[...]
    if paired:
        half = refs[0].shape[0] // 2
        near = halo_lines(near, refs[0][:half])
        far = halo_lines(far, refs[0][half:])
        refs = refs[1:]
    halos = far, near
    patches, inner, *convs = refs[:4]
    weights, (out, borders, done, sems) = refs[4:-4], refs[-4:]
    row_count, _, _, plane = patches.shape
    depth = convs[0].shape[1] // 27
    width = math.gcd(plane, CELLS)
    rows = [(0, 1), (row_count - 1, row_count - 2)]
    copies = [pltpu.make_async_copy(inner, out.at[:, 1 : row_count - 1], sems.at[0])]
    copies[0].start()
    windows = []
    places = []
    for side, (edge, inside) in enumerate(rows):
        for place, piece in enumerate(shifted(halos[side])):
            borders[side, place] = piece
        sources = [borders.at[side], patches.at[edge], patches.at[inside]]
        for start in range(0, plane, width):
            cells = slice(start, start + width)
            places.append((side, cells))
            windows.append(
                (convs[side], functools.partial(stack, sources, depth=depth, cells=cells))
            )

    def store(index, frame, final):
        side, cells = places[index]
        done[side, frame, :, cells] = final

    encode(windows, weights, out.shape[0], store)
    for side, (edge, _) in enumerate(rows):
        copies.append(pltpu.make_async_copy(done.at[side], out.at[:, edge], sems.at[side + 1]))
        copies[-1].start()
    for copy in copies:
        copy.wait()


VMEM = pl.BlockSpec(memory_space=pltpu.VMEM)
PARAMS = pltpu.CompilerParams(vmem_limit_bytes=40 * 2**20)


def cost(microseconds):
    size, flops = int(microseconds * 3.7e6), int(microseconds * 1.15e9)
    return pl.CostEstimate(flops=flops, bytes_accessed=size, transcendentals=0)


def ring(count, step):
    return [(index, (index + step) % count) for index in range(count)]


def shards(snapshots, conv_weight, conv_bias, tap_weight, tap_bias, mix_weight, mix_bias):
    frames, row_count, fields, plane = snapshots.shape
    channels = conv_weight.shape[0]
    times = lax.axis_size("tm")
    spaces = lax.axis_size("space")
    offsets, counts = frame_blocks(times, frames)
    paired = times == 4 and sorted(offsets) == [0, 1, 2, 3] and spaces % 2 == 0
    tall = GROUP * channels
    total = len(offsets) * frames * fields

    sources = [
        snapshots,
        conv_weight.transpose(2, 3, 4, 1, 0).reshape(27, fields, channels),
        conv_bias.reshape(1, channels),
        tap_weight.transpose(0, 2, 1, 3),
        tap_bias,
        mix_weight,
        mix_bias,
    ]
    sources = [pltpu.with_memory_space_constraint(source, pltpu.HBM) for source in sources]
    sources = pl.pallas_call(
        fetch_kernel,
        out_shape=[jax.ShapeDtypeStruct(source.shape, source.dtype) for source in sources],
        in_specs=[pl.BlockSpec(memory_space=pl.ANY)] * len(sources),
        out_specs=[VMEM] * len(sources),
        scratch_shapes=[pltpu.SemaphoreType.DMA((len(sources),))],
        compiler_params=PARAMS,
        cost_estimate=cost(0.8),
        name="fetch",
    )(*sources)

    if paired:
        offsets = [0, 2, 1, 3]
        slot_of = lambda index: [index ^ offset for offset in offsets]
        across = [(index, index ^ 2) for index in range(times)]
        beside = [(index, index ^ 1) for index in range(times)]
        near = lax.ppermute(snapshots, "tm", beside)
        to_far, to_near, pair = pl.pallas_call(
            pack_kernel,
            out_shape=[jax.ShapeDtypeStruct((total // 2, plane), BF16)] * 2
            + [jax.ShapeDtypeStruct((2,) + snapshots.shape, BF16)],
            in_specs=[VMEM] * 2,
            out_specs=[VMEM] * 3,
            compiler_params=PARAMS,
            cost_estimate=cost(0.05),
            name="pack",
        )(sources[0], near)
        far_pairs, near_pairs = [], []
        for time in range(times):
            for space in range(spaces):
                target = (time ^ (time % 2 * 2)) * spaces
                far_pairs.append((time * spaces + space, target + (space + 1) % spaces))
                near_pairs.append((time * spaces + space, target + (space - 1) % spaces))
        beyond = lax.ppermute(pair, "tm", across)
        near_halo = lax.ppermute(to_near, ("tm", "space"), near_pairs)
        far_halo = lax.ppermute(to_far, ("tm", "space"), far_pairs)
    else:
        slot_of = lambda index: [(index + offset) % times for offset in offsets]

    own, conv, conv_shift, *levels = sources
    if paired:
        far_halo, conv, conv_shift, *levels = lax.optimization_barrier(
            (far_halo, conv, conv_shift, *levels)
        )
    *convs, conv_shift = pl.pallas_call(
        conv_kernel,
        out_shape=[jax.ShapeDtypeStruct((tall, 27 * GROUP * fields), BF16)] * 2
        + [jax.ShapeDtypeStruct((tall, 128), F32)],
        in_specs=[VMEM] * 2,
        out_specs=[VMEM] * 3,
        compiler_params=PARAMS,
        cost_estimate=cost(0.15),
        name="conv",
    )(conv, conv_shift)

    wide_of = [count * frames * channels for count in counts]
    shapes = []
    for level in range(LEVELS):
        shape = wide_of[level + 1], wide_of[level] * (level + 1)
        shapes.append(jax.ShapeDtypeStruct(shape, BF16))
    for level in range(LEVELS):
        shapes.append(jax.ShapeDtypeStruct((wide_of[level + 1], 128), F32))
    shapes += [
        jax.ShapeDtypeStruct((wide_of[LEVELS], wide_of[LEVELS] * LEVELS), BF16),
        jax.ShapeDtypeStruct((wide_of[LEVELS], 128), F32),
    ]
    weights = pl.pallas_call(
        functools.partial(levels_kernel, slot_of, frames),
        out_shape=shapes,
        in_specs=[VMEM] * 4,
        out_specs=[VMEM] * len(shapes),
        compiler_params=PARAMS,
        cost_estimate=cost(0.35),
        name="levels",
    )(*levels)
    weights = [conv_shift, *weights]

    if paired:
        blocks = [own, near, beyond]
    else:
        blocks = [own] + [
            lax.ppermute(snapshots, "tm", ring(times, -offset)) for offset in offsets[1:]
        ]
        low, high = [
            jnp.concatenate([block[:, row] for block in blocks], axis=0).reshape(total, plane)
            for row in (0, row_count - 1)
        ]
        halos = [
            lax.ppermute(low, "space", ring(spaces, -1)),
            lax.ppermute(high, "space", ring(spaces, 1)),
        ]

    if paired:
        far_halo, near_halo, *weights = lax.optimization_barrier((far_halo, near_halo, *weights))
        merged = pl.pallas_call(
            merge_kernel,
            out_shape=jax.ShapeDtypeStruct((total, plane), BF16),
            in_specs=[VMEM] * 2,
            out_specs=VMEM,
            compiler_params=PARAMS,
            cost_estimate=cost(0.05),
            name="merge",
        )(near_halo, far_halo)
        halos = [near_halo, far_halo, lax.ppermute(merged, "tm", beside)]

    patches, inner = pl.pallas_call(
        functools.partial(inner_kernel, paired, len(blocks)),
        out_shape=[
            jax.ShapeDtypeStruct((row_count, 9, total, plane), BF16),
            jax.ShapeDtypeStruct((frames, row_count - 2, channels, plane), BF16),
        ],
        in_specs=[VMEM] * (len(blocks) + 1 + len(weights)),
        out_specs=[VMEM] * 2,
        compiler_params=PARAMS,
        cost_estimate=cost(0.5),
        name="inner",
    )(*blocks, convs[0], *weights)

    return pl.pallas_call(
        functools.partial(outer_kernel, paired),
        out_shape=jax.ShapeDtypeStruct((frames, row_count, channels, plane), BF16),
        in_specs=[VMEM] * (len(halos) + 4 + len(weights)),
        out_specs=pl.BlockSpec(memory_space=pl.ANY),
        scratch_shapes=[
            pltpu.VMEM((2, 9, total, plane), BF16),
            pltpu.VMEM((2, frames, channels, plane), BF16),
            pltpu.SemaphoreType.DMA((3,)),
        ],
        compiler_params=PARAMS,
        cost_estimate=cost(2.5),
        name="outer",
    )(*halos, patches, inner, *convs, *weights)


def solution(mesh):
    in_specs = (P("tm", "space", None, None), P(), P(), P(), P(), P(), P())
    out_specs = P("tm", "space", None, None)
    return jax.shard_map(shards, mesh=mesh, in_specs=in_specs, out_specs=out_specs, check_vma=False)
```

```python
import functools
import math

import jax
import jax.numpy as jnp
from jax import lax
from jax.experimental import pallas as pl
from jax.experimental.pallas import tpu as pltpu
from jax.sharding import PartitionSpec as P

LEVELS = 3
NZ = 32
GROUP = 4
CELLS = 256
SLOPE = math.sqrt(2.0 / math.pi)
CUBIC = SLOPE * 0.044715
BF16 = jnp.bfloat16
F32 = jnp.float32


def frame_blocks(axis_size, frames):
    needed = [0]
    counts = [1]
    for level in reversed(range(LEVELS)):
        reach = set()
        for offset in needed:
            for frame in range(frames):
                for step in (-(2**level), 2**level):
                    reach.add((offset + (frame + step) // frames) % axis_size)
        needed = needed + sorted(reach - set(needed))
        spare = [offset for offset in range(axis_size) if offset not in needed]
        while len(needed) * frames % GROUP and spare:
            needed.append(spare.pop(0))
        counts.append(len(needed))
    return needed, counts[::-1]


def gelu_of_double(half):
    inner = half * (2 * SLOPE + 8 * CUBIC * (half * half))
    return (half + half * jnp.tanh(inner)).astype(BF16)


def joined(parts, axis):
    return parts[0] if len(parts) == 1 else jnp.concatenate(parts, axis=axis)


def wide(shift, cells):
    return joined([shift] * (cells // 128), 1)


def column(row, copies):
    count = row.shape[1]
    down = lax.broadcasted_iota(jnp.int32, (count, count), 0)
    across = lax.broadcasted_iota(jnp.int32, (count, count), 1)
    tall = jnp.sum(jnp.where(down == across, row, 0.0), axis=1, keepdims=True)
    return joined([tall] * copies, 0)


def lanes(value):
    return jnp.broadcast_to(value, (value.shape[0], 128))


def spread(block, rows, columns):
    height, width = block.shape
    tile = jnp.concatenate([block] * (128 // width), axis=1)
    parts = [tile] * (columns // 128)
    if columns % 128:
        parts.append(tile[:, : columns % 128])
    return joined([joined(parts, 1)] * (rows // height), 0)


def fetch_kernel(*refs):
    count = len(refs) // 2
    sems = refs[-1]
    copies = [
        pltpu.make_async_copy(refs[index], refs[count + index], sems.at[index])
        for index in range(count)
    ]
    for copy in copies:
        copy.start()
    for copy in copies:
        copy.wait()


def conv_kernel(conv, conv_shift, *outs):
    places, fields, channels = conv.shape
    depth = places * fields
    wide = depth * GROUP
    flat = conv[...].astype(F32).reshape(depth, channels).astype(BF16)
    down = lax.broadcasted_iota(jnp.int32, (depth, wide), 0)
    across = lax.broadcasted_iota(jnp.int32, (depth, wide), 1)
    same = (down // fields == across // (GROUP * fields)) & (down % fields == across % fields)
    pick = jnp.where(same, 1.0, 0.0).astype(BF16)
    full = lax.dot_general(flat, pick, (((0,), (0,)), ((), ())), preferred_element_type=F32)
    full = jnp.concatenate([full] * GROUP, axis=0)
    down = lax.broadcasted_iota(jnp.int32, full.shape, 0)
    across = lax.broadcasted_iota(jnp.int32, full.shape, 1)
    keep = down // channels == across // fields % GROUP
    full = jnp.where(keep, 0.5 * full, 0.0)
    third = wide // 3
    turned = jnp.concatenate([full[:, 2 * third :], full[:, third : -third], full[:, :third]], axis=1)
    outs[0][...] = full.astype(BF16)
    outs[1][...] = turned.astype(BF16)
    outs[2][...] = lanes(0.5 * column(conv_shift[...], GROUP))


def levels_kernel(slot_of, frames, taps, tap_shift, mix, mix_shift, *outs):
    tap_outs, tap_shift_outs = outs[:LEVELS], outs[LEVELS : 2 * LEVELS]
    mix_out, mix_shift_out = outs[2 * LEVELS :]
    channels = mix.shape[-1]
    slots = slot_of(lax.axis_index("tm"))
    for level in range(LEVELS):
        rows, columns = tap_outs[level].shape
        columns //= level + 1

        def frame_of(axis):
            place = lax.broadcasted_iota(jnp.int32, (rows, columns), axis) // channels
            block = place // frames
            start = jnp.zeros((rows, columns), jnp.int32)
            for index, slot in enumerate(slots[: (rows, columns)[axis] // channels // frames]):
                start = jnp.where(block == index, slot * frames, start)
            return start + place % frames

        gap = frame_of(1) - frame_of(0)
        for source in range(level + 1):
            total = jnp.zeros((rows, columns), F32)
            for tap in range(3):
                block = taps[level, tap]
                if source:
                    block = jnp.dot(block, mix[source - 1], preferred_element_type=F32)
                block = spread(block.astype(F32), rows, columns)
                total = jnp.where(gap == (tap - 1) * 2**level, block, total)
            if not source:
                shift = column(tap_shift[level : level + 1], rows // channels)
                if level:
                    held = jnp.sum(mix_shift[:level], axis=0, keepdims=True)
                    held = total * spread(held, 1, columns)
                    shift = shift + jnp.sum(held, axis=1, keepdims=True)
                tap_shift_outs[level][...] = lanes(0.5 * shift)
            part = slice(source * columns, (source + 1) * columns)
            tap_outs[level][:, part] = (0.5 * total).astype(BF16)
    size = mix_out.shape[0]
    down = lax.broadcasted_iota(jnp.int32, (size, size), 0)
    across = lax.broadcasted_iota(jnp.int32, (size, size), 1)
    same = down // channels == across // channels
    mix_out[...] = jnp.concatenate(
        [
            jnp.where(same, spread(mix[level].astype(F32), size, size), 0.0).astype(BF16)
            for level in range(LEVELS)
        ],
        axis=1,
    )
    held = jnp.sum(mix_shift[...], axis=0, keepdims=True)
    mix_shift_out[...] = lanes(column(held, size // channels))


def shifted(lines):
    plane = lines.shape[-1]
    depth = lax.broadcasted_iota(jnp.int32, (1, plane), 1) % NZ
    blank = jnp.zeros_like(lines)
    below = jnp.where(depth == 0, blank, pltpu.roll(lines, 1, 1))
    above = jnp.where(depth == NZ - 1, blank, pltpu.roll(lines, plane - 1, 1))
    for delta_y in (-1, 0, 1):
        for piece in (below, lines, above):
            yield pltpu.roll(piece, -delta_y * NZ % plane, 1) if delta_y else piece


def encode(windows, weights, frames, store):
    conv_shift, mix, mix_shift = weights[0], *weights[-2:]
    taps, tap_shifts = weights[1 : 1 + LEVELS], weights[1 + LEVELS : 1 + 2 * LEVELS]
    channels = conv_shift.shape[0] // GROUP
    groups = -(-taps[0].shape[1] // conv_shift.shape[0])
    held = []
    for conv, window in windows:
        parts = []
        for group in range(groups):
            summed = jnp.dot(conv[...], window(group), preferred_element_type=F32)
            parts.append(gelu_of_double(summed + wide(conv_shift[...], summed.shape[1])))
        held.append([joined(parts, 0)])
    for level, (tap, shift) in enumerate(zip(taps, tap_shifts)):
        columns = tap.shape[1] // (level + 1)
        for parts in held:
            read = joined([part[:columns] for part in parts], 0)
            summed = jnp.dot(tap[...], read, preferred_element_type=F32)
            parts.append(gelu_of_double(summed + wide(shift[...], summed.shape[1])))
    size = mix.shape[0]
    for index, (first, *gated) in enumerate(held):
        read = joined([part[:size] for part in gated], 0)
        mixed = jnp.dot(mix[...], read, preferred_element_type=F32)
        mixed = mixed + wide(mix_shift[...], mixed.shape[1])
        final = (first[:size].astype(F32) + mixed).astype(BF16)
        for frame in range(frames):
            store(index, frame, final[frame * channels : (frame + 1) * channels])


def stack(sources, group, depth, cells):
    part = slice(group * depth, (group + 1) * depth)
    return jnp.concatenate(
        [source[:, part, cells].reshape(9 * depth, -1) for source in sources], axis=0
    )


def pack_kernel(own, near, *outs):
    frames, row_count = near.shape[:2]
    first = lax.rem(lax.axis_index("tm"), 2) == 0
    rows = []
    for row in (0, row_count - 1):
        mine, beside = [
            jnp.concatenate([block[frame, row] for frame in range(frames)], axis=0)
            for block in (own, near)
        ]
        rows.append(
            jnp.concatenate(
                [jnp.where(first, mine, beside), jnp.where(first, beside, mine)], axis=0
            )
        )
    outs[2][0] = own[...]
    outs[2][1] = near[...]
    outs[0][...] = rows[1]
    outs[1][...] = rows[0]


def patch_kernel(paired, *refs):
    blocks, patches = refs[:-1], refs[-1]
    if paired:
        own, near, beyond = blocks
        blocks = own, beyond.at[0], near, beyond.at[1]
    frames, row_count = blocks[0].shape[:2]
    for row in range(row_count):
        lines = [block[frame, row] for block in blocks for frame in range(frames)]
        for place, piece in enumerate(shifted(jnp.concatenate(lines, axis=0))):
            patches[row, place] = piece


def inner_kernel(patches, conv, *rest):
    weights, out = rest[:-1], rest[-1]
    row_count, _, _, plane = patches.shape
    depth = conv.shape[1] // 27
    width = math.gcd(plane, CELLS)
    places = [
        (row, slice(start, start + width))
        for row in range(1, row_count - 1)
        for start in range(0, plane, width)
    ]
    windows = [
        (
            conv,
            functools.partial(
                stack, [patches.at[row + step] for step in (-1, 0, 1)], depth=depth, cells=cells
            ),
        )
        for row, cells in places
    ]

    def store(index, frame, final):
        row, cells = places[index]
        out[frame, row - 1, :, cells] = final

    encode(windows, weights, out.shape[0], store)


def merge_kernel(near, far, out):
    out[...] = jnp.concatenate([near[...], far[...]], axis=0)


def halo_lines(got, other):
    first = lax.rem(lax.axis_index("tm"), 2) == 0
    half = got.shape[0] // 2
    parts = [[], []]
    for held in (jnp.where(first, got, other), jnp.where(first, other, got)):
        upper, lower = held[:half], held[half:]
        parts[0].append(jnp.where(first, upper, lower))
        parts[1].append(jnp.where(first, lower, upper))
    return jnp.concatenate(parts[0] + parts[1], axis=0)


def outer_kernel(paired, near, far, *refs):
    near, far = near[...], far[...]
    if paired:
        half = refs[0].shape[0] // 2
        near = halo_lines(near, refs[0][:half])
        far = halo_lines(far, refs[0][half:])
        refs = refs[1:]
    halos = far, near
    patches, inner, *convs = refs[:4]
    weights, (out, borders, done, sems) = refs[4:-4], refs[-4:]
    row_count, _, _, plane = patches.shape
    depth = convs[0].shape[1] // 27
    width = math.gcd(plane, CELLS)
    rows = [(0, 1), (row_count - 1, row_count - 2)]
    copies = [pltpu.make_async_copy(inner, out.at[:, 1 : row_count - 1], sems.at[0])]
    copies[0].start()
    windows = []
    places = []
    for side, (edge, inside) in enumerate(rows):
        for place, piece in enumerate(shifted(halos[side])):
            borders[side, place] = piece
        sources = [borders.at[side], patches.at[edge], patches.at[inside]]
        for start in range(0, plane, width):
            cells = slice(start, start + width)
            places.append((side, cells))
            windows.append(
                (convs[side], functools.partial(stack, sources, depth=depth, cells=cells))
            )

    def store(index, frame, final):
        side, cells = places[index]
        done[side, frame, :, cells] = final

    encode(windows, weights, out.shape[0], store)
    for side, (edge, _) in enumerate(rows):
        copies.append(pltpu.make_async_copy(done.at[side], out.at[:, edge], sems.at[side + 1]))
        copies[-1].start()
    for copy in copies:
        copy.wait()


VMEM = pl.BlockSpec(memory_space=pltpu.VMEM)
PARAMS = pltpu.CompilerParams(vmem_limit_bytes=40 * 2**20)


def cost(microseconds):
    size, flops = int(microseconds * 3.7e6), int(microseconds * 1.15e9)
    return pl.CostEstimate(flops=flops, bytes_accessed=size, transcendentals=0)


def ring(count, step):
    return [(index, (index + step) % count) for index in range(count)]


def shards(snapshots, conv_weight, conv_bias, tap_weight, tap_bias, mix_weight, mix_bias):
    frames, row_count, fields, plane = snapshots.shape
    channels = conv_weight.shape[0]
    times = lax.axis_size("tm")
    spaces = lax.axis_size("space")
    offsets, counts = frame_blocks(times, frames)
    paired = times == 4 and sorted(offsets) == [0, 1, 2, 3] and spaces % 2 == 0
    tall = GROUP * channels
    total = len(offsets) * frames * fields

    sources = [
        snapshots,
        conv_weight.transpose(2, 3, 4, 1, 0).reshape(27, fields, channels),
        conv_bias.reshape(1, channels),
        tap_weight.transpose(0, 2, 1, 3),
        tap_bias,
        mix_weight,
        mix_bias,
    ]
    sources = [pltpu.with_memory_space_constraint(source, pltpu.HBM) for source in sources]
    sources = pl.pallas_call(
        fetch_kernel,
        out_shape=[jax.ShapeDtypeStruct(source.shape, source.dtype) for source in sources],
        in_specs=[pl.BlockSpec(memory_space=pl.ANY)] * len(sources),
        out_specs=[VMEM] * len(sources),
        scratch_shapes=[pltpu.SemaphoreType.DMA((len(sources),))],
        compiler_params=PARAMS,
        cost_estimate=cost(0.8),
        name="fetch",
    )(*sources)

    if paired:
        offsets = [0, 2, 1, 3]
        slot_of = lambda index: [index ^ offset for offset in offsets]
        across = [(index, index ^ 2) for index in range(times)]
        beside = [(index, index ^ 1) for index in range(times)]
        near = lax.ppermute(snapshots, "tm", beside)
        to_far, to_near, pair = pl.pallas_call(
            pack_kernel,
            out_shape=[jax.ShapeDtypeStruct((total // 2, plane), BF16)] * 2
            + [jax.ShapeDtypeStruct((2,) + snapshots.shape, BF16)],
            in_specs=[VMEM] * 2,
            out_specs=[VMEM] * 3,
            compiler_params=PARAMS,
            cost_estimate=cost(0.05),
            name="pack",
        )(sources[0], near)
        far_pairs, near_pairs = [], []
        for time in range(times):
            for space in range(spaces):
                target = (time ^ (time % 2 * 2)) * spaces
                far_pairs.append((time * spaces + space, target + (space + 1) % spaces))
                near_pairs.append((time * spaces + space, target + (space - 1) % spaces))
        beyond = lax.ppermute(pair, "tm", across)
        near_halo = lax.ppermute(to_near, ("tm", "space"), near_pairs)
        far_halo = lax.ppermute(to_far, ("tm", "space"), far_pairs)
    else:
        slot_of = lambda index: [(index + offset) % times for offset in offsets]

    own, conv, conv_shift, *levels = sources
    if paired:
        far_halo, conv, conv_shift, *levels = lax.optimization_barrier(
            (far_halo, conv, conv_shift, *levels)
        )
    *convs, conv_shift = pl.pallas_call(
        conv_kernel,
        out_shape=[jax.ShapeDtypeStruct((tall, 27 * GROUP * fields), BF16)] * 2
        + [jax.ShapeDtypeStruct((tall, 128), F32)],
        in_specs=[VMEM] * 2,
        out_specs=[VMEM] * 3,
        compiler_params=PARAMS,
        cost_estimate=cost(0.15),
        name="conv",
    )(conv, conv_shift)

    wide_of = [count * frames * channels for count in counts]
    shapes = []
    for level in range(LEVELS):
        shape = wide_of[level + 1], wide_of[level] * (level + 1)
        shapes.append(jax.ShapeDtypeStruct(shape, BF16))
    for level in range(LEVELS):
        shapes.append(jax.ShapeDtypeStruct((wide_of[level + 1], 128), F32))
    shapes += [
        jax.ShapeDtypeStruct((wide_of[LEVELS], wide_of[LEVELS] * LEVELS), BF16),
        jax.ShapeDtypeStruct((wide_of[LEVELS], 128), F32),
    ]
    weights = pl.pallas_call(
        functools.partial(levels_kernel, slot_of, frames),
        out_shape=shapes,
        in_specs=[VMEM] * 4,
        out_specs=[VMEM] * len(shapes),
        compiler_params=PARAMS,
        cost_estimate=cost(0.35),
        name="levels",
    )(*levels)
    weights = [conv_shift, *weights]

    if paired:
        blocks = [own, near, beyond]
    else:
        blocks = [own] + [
            lax.ppermute(snapshots, "tm", ring(times, -offset)) for offset in offsets[1:]
        ]
        low, high = [
            jnp.concatenate([block[:, row] for block in blocks], axis=0).reshape(total, plane)
            for row in (0, row_count - 1)
        ]
        halos = [
            lax.ppermute(low, "space", ring(spaces, -1)),
            lax.ppermute(high, "space", ring(spaces, 1)),
        ]

    patches = pl.pallas_call(
        functools.partial(patch_kernel, paired),
        out_shape=jax.ShapeDtypeStruct((row_count, 9, total, plane), BF16),
        in_specs=[VMEM] * len(blocks),
        out_specs=VMEM,
        compiler_params=PARAMS,
        cost_estimate=cost(0.01),
        name="patch",
    )(*blocks)

    if paired:
        far_halo, near_halo, patches, *weights = lax.optimization_barrier(
            (far_halo, near_halo, patches, *weights)
        )
        merged = pl.pallas_call(
            merge_kernel,
            out_shape=jax.ShapeDtypeStruct((total, plane), BF16),
            in_specs=[VMEM] * 2,
            out_specs=VMEM,
            compiler_params=PARAMS,
            cost_estimate=cost(0.05),
            name="merge",
        )(near_halo, far_halo)
        halos = [near_halo, far_halo, lax.ppermute(merged, "tm", beside)]

    inner = pl.pallas_call(
        inner_kernel,
        out_shape=jax.ShapeDtypeStruct((frames, row_count - 2, channels, plane), BF16),
        in_specs=[VMEM] * (2 + len(weights)),
        out_specs=VMEM,
        compiler_params=PARAMS,
        cost_estimate=cost(0.5),
        name="inner",
    )(patches, convs[0], *weights)

    return pl.pallas_call(
        functools.partial(outer_kernel, paired),
        out_shape=jax.ShapeDtypeStruct((frames, row_count, channels, plane), BF16),
        in_specs=[VMEM] * (len(halos) + 4 + len(weights)),
        out_specs=pl.BlockSpec(memory_space=pl.ANY),
        scratch_shapes=[
            pltpu.VMEM((2, 9, total, plane), BF16),
            pltpu.VMEM((2, frames, channels, plane), BF16),
            pltpu.SemaphoreType.DMA((3,)),
        ],
        compiler_params=PARAMS,
        cost_estimate=cost(2.5),
        name="outer",
    )(*halos, patches, inner, *convs, *weights)


def solution(mesh):
    in_specs = (P("tm", "space", None, None), P(), P(), P(), P(), P(), P())
    out_specs = P("tm", "space", None, None)
    return jax.shard_map(shards, mesh=mesh, in_specs=in_specs, out_specs=out_specs, check_vma=False)
```

```python
import functools
import math

import jax
import jax.numpy as jnp
from jax import lax
from jax.experimental import pallas as pl
from jax.experimental.pallas import tpu as pltpu
from jax.sharding import PartitionSpec as P

LEVELS = 3
NZ = 32
GROUP = 4
CELLS = 256
SLOPE = math.sqrt(2.0 / math.pi)
CUBIC = SLOPE * 0.044715
BF16 = jnp.bfloat16
F32 = jnp.float32


def frame_blocks(axis_size, frames):
    needed = [0]
    counts = [1]
    for level in reversed(range(LEVELS)):
        reach = set()
        for offset in needed:
            for frame in range(frames):
                for step in (-(2**level), 2**level):
                    reach.add((offset + (frame + step) // frames) % axis_size)
        needed = needed + sorted(reach - set(needed))
        spare = [offset for offset in range(axis_size) if offset not in needed]
        while len(needed) * frames % GROUP and spare:
            needed.append(spare.pop(0))
        counts.append(len(needed))
    return needed, counts[::-1]


def gelu_of_double(half):
    inner = half * (2 * SLOPE + 8 * CUBIC * (half * half))
    return (half + half * jnp.tanh(inner)).astype(BF16)


def joined(parts, axis):
    return parts[0] if len(parts) == 1 else jnp.concatenate(parts, axis=axis)


def wide(shift, cells):
    return joined([shift] * (cells // 128), 1)


def column(row, copies):
    count = row.shape[1]
    down = lax.broadcasted_iota(jnp.int32, (count, count), 0)
    across = lax.broadcasted_iota(jnp.int32, (count, count), 1)
    tall = jnp.sum(jnp.where(down == across, row, 0.0), axis=1, keepdims=True)
    return joined([tall] * copies, 0)


def lanes(value):
    return jnp.broadcast_to(value, (value.shape[0], 128))


def spread(block, rows, columns):
    height, width = block.shape
    tile = jnp.concatenate([block] * (128 // width), axis=1)
    parts = [tile] * (columns // 128)
    if columns % 128:
        parts.append(tile[:, : columns % 128])
    return joined([joined(parts, 1)] * (rows // height), 0)


def fetch_kernel(*refs):
    count = len(refs) // 2
    sems = refs[-1]
    copies = [
        pltpu.make_async_copy(refs[index], refs[count + index], sems.at[index])
        for index in range(count)
    ]
    for copy in copies:
        copy.start()
    for copy in copies:
        copy.wait()


def conv_kernel(conv, conv_shift, *outs):
    places, fields, channels = conv.shape
    depth = places * fields
    wide = depth * GROUP
    flat = conv[...].astype(F32).reshape(depth, channels).astype(BF16)
    down = lax.broadcasted_iota(jnp.int32, (depth, wide), 0)
    across = lax.broadcasted_iota(jnp.int32, (depth, wide), 1)
    same = (down // fields == across // (GROUP * fields)) & (down % fields == across % fields)
    pick = jnp.where(same, 1.0, 0.0).astype(BF16)
    full = lax.dot_general(flat, pick, (((0,), (0,)), ((), ())), preferred_element_type=F32)
    full = jnp.concatenate([full] * GROUP, axis=0)
    down = lax.broadcasted_iota(jnp.int32, full.shape, 0)
    across = lax.broadcasted_iota(jnp.int32, full.shape, 1)
    keep = down // channels == across // fields % GROUP
    full = jnp.where(keep, 0.5 * full, 0.0)
    third = wide // 3
    turned = jnp.concatenate([full[:, 2 * third :], full[:, third : -third], full[:, :third]], axis=1)
    outs[0][...] = full.astype(BF16)
    outs[1][...] = turned.astype(BF16)
    outs[2][...] = lanes(0.5 * column(conv_shift[...], GROUP))


def levels_kernel(slot_of, frames, taps, tap_shift, mix, mix_shift, *outs):
    tap_outs, tap_shift_outs = outs[:LEVELS], outs[LEVELS : 2 * LEVELS]
    mix_out, mix_shift_out = outs[2 * LEVELS :]
    channels = mix.shape[-1]
    slots = slot_of(lax.axis_index("tm"))
    for level in range(LEVELS):
        rows, columns = tap_outs[level].shape
        columns //= level + 1

        def frame_of(axis):
            place = lax.broadcasted_iota(jnp.int32, (rows, columns), axis) // channels
            block = place // frames
            start = jnp.zeros((rows, columns), jnp.int32)
            for index, slot in enumerate(slots[: (rows, columns)[axis] // channels // frames]):
                start = jnp.where(block == index, slot * frames, start)
            return start + place % frames

        gap = frame_of(1) - frame_of(0)
        for source in range(level + 1):
            total = jnp.zeros((rows, columns), F32)
            for tap in range(3):
                block = taps[level, tap]
                if source:
                    block = jnp.dot(block, mix[source - 1], preferred_element_type=F32)
                block = spread(block.astype(F32), rows, columns)
                total = jnp.where(gap == (tap - 1) * 2**level, block, total)
            if not source:
                shift = column(tap_shift[level : level + 1], rows // channels)
                if level:
                    held = jnp.sum(mix_shift[:level], axis=0, keepdims=True)
                    held = total * spread(held, 1, columns)
                    shift = shift + jnp.sum(held, axis=1, keepdims=True)
                tap_shift_outs[level][...] = lanes(0.5 * shift)
            part = slice(source * columns, (source + 1) * columns)
            tap_outs[level][:, part] = (0.5 * total).astype(BF16)
    size = mix_out.shape[0]
    down = lax.broadcasted_iota(jnp.int32, (size, size), 0)
    across = lax.broadcasted_iota(jnp.int32, (size, size), 1)
    same = down // channels == across // channels
    mix_out[...] = jnp.concatenate(
        [
            jnp.where(same, spread(mix[level].astype(F32), size, size), 0.0).astype(BF16)
            for level in range(LEVELS)
        ],
        axis=1,
    )
    held = jnp.sum(mix_shift[...], axis=0, keepdims=True)
    mix_shift_out[...] = lanes(column(held, size // channels))


def shifted(lines):
    plane = lines.shape[-1]
    depth = lax.broadcasted_iota(jnp.int32, (1, plane), 1) % NZ
    blank = jnp.zeros_like(lines)
    below = jnp.where(depth == 0, blank, pltpu.roll(lines, 1, 1))
    above = jnp.where(depth == NZ - 1, blank, pltpu.roll(lines, plane - 1, 1))
    for delta_y in (-1, 0, 1):
        for piece in (below, lines, above):
            yield pltpu.roll(piece, -delta_y * NZ % plane, 1) if delta_y else piece


def encode(windows, weights, frames, store):
    conv_shift, mix, mix_shift = weights[0], *weights[-2:]
    taps, tap_shifts = weights[1 : 1 + LEVELS], weights[1 + LEVELS : 1 + 2 * LEVELS]
    channels = conv_shift.shape[0] // GROUP
    groups = -(-taps[0].shape[1] // conv_shift.shape[0])
    held = []
    for conv, window in windows:
        parts = []
        for group in range(groups):
            summed = jnp.dot(conv[...], window(group), preferred_element_type=F32)
            parts.append(gelu_of_double(summed + wide(conv_shift[...], summed.shape[1])))
        held.append([joined(parts, 0)])
    for level, (tap, shift) in enumerate(zip(taps, tap_shifts)):
        columns = tap.shape[1] // (level + 1)
        for parts in held:
            read = joined([part[:columns] for part in parts], 0)
            summed = jnp.dot(tap[...], read, preferred_element_type=F32)
            parts.append(gelu_of_double(summed + wide(shift[...], summed.shape[1])))
    size = mix.shape[0]
    for index, (first, *gated) in enumerate(held):
        read = joined([part[:size] for part in gated], 0)
        mixed = jnp.dot(mix[...], read, preferred_element_type=F32)
        mixed = mixed + wide(mix_shift[...], mixed.shape[1])
        final = (first[:size].astype(F32) + mixed).astype(BF16)
        for frame in range(frames):
            store(index, frame, final[frame * channels : (frame + 1) * channels])


def stack(sources, group, depth, cells):
    part = slice(group * depth, (group + 1) * depth)
    return jnp.concatenate(
        [source[:, part, cells].reshape(9 * depth, -1) for source in sources], axis=0
    )


def pack_kernel(own, near, *outs):
    frames, row_count = near.shape[:2]
    first = lax.rem(lax.axis_index("tm"), 2) == 0
    rows = []
    for row in (0, row_count - 1):
        mine, beside = [
            jnp.concatenate([block[frame, row] for frame in range(frames)], axis=0)
            for block in (own, near)
        ]
        rows.append(
            jnp.concatenate(
                [jnp.where(first, mine, beside), jnp.where(first, beside, mine)], axis=0
            )
        )
    outs[2][0] = own[...]
    outs[2][1] = near[...]
    outs[0][...] = rows[1]
    outs[1][...] = rows[0]


def patch_kernel(paired, *refs):
    blocks, patches = refs[:-1], refs[-1]
    if paired:
        own, near, beyond = blocks
        blocks = own, beyond.at[0], near, beyond.at[1]
    frames, row_count = blocks[0].shape[:2]
    for row in range(row_count):
        lines = [block[frame, row] for block in blocks for frame in range(frames)]
        for place, piece in enumerate(shifted(jnp.concatenate(lines, axis=0))):
            patches[row, place] = piece


def prepare_kernel(paired, count, *refs):
    blocks, (conv, conv_shift), outs = refs[:count], refs[count : count + 2], refs[count + 2 :]
    patch_kernel(paired, *blocks, outs[0])
    conv_kernel(conv, conv_shift, *outs[1:])


def inner_kernel(patches, conv, *rest):
    weights, out = rest[:-1], rest[-1]
    row_count, _, _, plane = patches.shape
    depth = conv.shape[1] // 27
    width = math.gcd(plane, CELLS)
    places = [
        (row, slice(start, start + width))
        for row in range(1, row_count - 1)
        for start in range(0, plane, width)
    ]
    windows = [
        (
            conv,
            functools.partial(
                stack, [patches.at[row + step] for step in (-1, 0, 1)], depth=depth, cells=cells
            ),
        )
        for row, cells in places
    ]

    def store(index, frame, final):
        row, cells = places[index]
        out[frame, row - 1, :, cells] = final

    encode(windows, weights, out.shape[0], store)


def merge_kernel(near, far, out):
    out[...] = jnp.concatenate([near[...], far[...]], axis=0)


def halo_lines(got, other):
    first = lax.rem(lax.axis_index("tm"), 2) == 0
    half = got.shape[0] // 2
    parts = [[], []]
    for held in (jnp.where(first, got, other), jnp.where(first, other, got)):
        upper, lower = held[:half], held[half:]
        parts[0].append(jnp.where(first, upper, lower))
        parts[1].append(jnp.where(first, lower, upper))
    return jnp.concatenate(parts[0] + parts[1], axis=0)


def outer_kernel(paired, near, far, *refs):
    near, far = near[...], far[...]
    if paired:
        half = refs[0].shape[0] // 2
        near = halo_lines(near, refs[0][:half])
        far = halo_lines(far, refs[0][half:])
        refs = refs[1:]
    halos = far, near
    patches, inner, *convs = refs[:4]
    weights, (out, borders, done, sems) = refs[4:-4], refs[-4:]
    row_count, _, _, plane = patches.shape
    depth = convs[0].shape[1] // 27
    width = math.gcd(plane, CELLS)
    rows = [(0, 1), (row_count - 1, row_count - 2)]
    copies = [pltpu.make_async_copy(inner, out.at[:, 1 : row_count - 1], sems.at[0])]
    copies[0].start()
    windows = []
    places = []
    for side, (edge, inside) in enumerate(rows):
        for place, piece in enumerate(shifted(halos[side])):
            borders[side, place] = piece
        sources = [borders.at[side], patches.at[edge], patches.at[inside]]
        for start in range(0, plane, width):
            cells = slice(start, start + width)
            places.append((side, cells))
            windows.append(
                (convs[side], functools.partial(stack, sources, depth=depth, cells=cells))
            )

    def store(index, frame, final):
        side, cells = places[index]
        done[side, frame, :, cells] = final

    encode(windows, weights, out.shape[0], store)
    for side, (edge, _) in enumerate(rows):
        copies.append(pltpu.make_async_copy(done.at[side], out.at[:, edge], sems.at[side + 1]))
        copies[-1].start()
    for copy in copies:
        copy.wait()


VMEM = pl.BlockSpec(memory_space=pltpu.VMEM)
PARAMS = pltpu.CompilerParams(vmem_limit_bytes=40 * 2**20)


def cost(microseconds):
    size, flops = int(microseconds * 3.7e6), int(microseconds * 1.15e9)
    return pl.CostEstimate(flops=flops, bytes_accessed=size, transcendentals=0)


def ring(count, step):
    return [(index, (index + step) % count) for index in range(count)]


def shards(snapshots, conv_weight, conv_bias, tap_weight, tap_bias, mix_weight, mix_bias):
    frames, row_count, fields, plane = snapshots.shape
    channels = conv_weight.shape[0]
    times = lax.axis_size("tm")
    spaces = lax.axis_size("space")
    offsets, counts = frame_blocks(times, frames)
    paired = times == 4 and sorted(offsets) == [0, 1, 2, 3] and spaces % 2 == 0
    tall = GROUP * channels
    total = len(offsets) * frames * fields

    sources = [
        snapshots,
        conv_weight.transpose(2, 3, 4, 1, 0).reshape(27, fields, channels),
        conv_bias.reshape(1, channels),
        tap_weight.transpose(0, 2, 1, 3),
        tap_bias,
        mix_weight,
        mix_bias,
    ]
    sources = [pltpu.with_memory_space_constraint(source, pltpu.HBM) for source in sources]
    sources = pl.pallas_call(
        fetch_kernel,
        out_shape=[jax.ShapeDtypeStruct(source.shape, source.dtype) for source in sources],
        in_specs=[pl.BlockSpec(memory_space=pl.ANY)] * len(sources),
        out_specs=[VMEM] * len(sources),
        scratch_shapes=[pltpu.SemaphoreType.DMA((len(sources),))],
        compiler_params=PARAMS,
        cost_estimate=cost(0.8),
        name="fetch",
    )(*sources)

    if paired:
        offsets = [0, 2, 1, 3]
        slot_of = lambda index: [index ^ offset for offset in offsets]
        across = [(index, index ^ 2) for index in range(times)]
        beside = [(index, index ^ 1) for index in range(times)]
        near = lax.ppermute(snapshots, "tm", beside)
        to_far, to_near, pair = pl.pallas_call(
            pack_kernel,
            out_shape=[jax.ShapeDtypeStruct((total // 2, plane), BF16)] * 2
            + [jax.ShapeDtypeStruct((2,) + snapshots.shape, BF16)],
            in_specs=[VMEM] * 2,
            out_specs=[VMEM] * 3,
            compiler_params=PARAMS,
            cost_estimate=cost(0.05),
            name="pack",
        )(sources[0], near)
        far_pairs, near_pairs = [], []
        for time in range(times):
            for space in range(spaces):
                target = (time ^ (time % 2 * 2)) * spaces
                far_pairs.append((time * spaces + space, target + (space + 1) % spaces))
                near_pairs.append((time * spaces + space, target + (space - 1) % spaces))
        beyond = lax.ppermute(pair, "tm", across)
        near_halo = lax.ppermute(to_near, ("tm", "space"), near_pairs)
        far_halo = lax.ppermute(to_far, ("tm", "space"), far_pairs)
    else:
        slot_of = lambda index: [(index + offset) % times for offset in offsets]

    own, conv, conv_shift, *levels = sources
    if paired:
        far_halo, conv, conv_shift, *levels = lax.optimization_barrier(
            (far_halo, conv, conv_shift, *levels)
        )
    wide_of = [count * frames * channels for count in counts]
    shapes = []
    for level in range(LEVELS):
        shape = wide_of[level + 1], wide_of[level] * (level + 1)
        shapes.append(jax.ShapeDtypeStruct(shape, BF16))
    for level in range(LEVELS):
        shapes.append(jax.ShapeDtypeStruct((wide_of[level + 1], 128), F32))
    shapes += [
        jax.ShapeDtypeStruct((wide_of[LEVELS], wide_of[LEVELS] * LEVELS), BF16),
        jax.ShapeDtypeStruct((wide_of[LEVELS], 128), F32),
    ]
    weights = pl.pallas_call(
        functools.partial(levels_kernel, slot_of, frames),
        out_shape=shapes,
        in_specs=[VMEM] * 4,
        out_specs=[VMEM] * len(shapes),
        compiler_params=PARAMS,
        cost_estimate=cost(0.52),
        name="levels",
    )(*levels)

    if paired:
        blocks = [own, near, beyond]
    else:
        blocks = [own] + [
            lax.ppermute(snapshots, "tm", ring(times, -offset)) for offset in offsets[1:]
        ]
        low, high = [
            jnp.concatenate([block[:, row] for block in blocks], axis=0).reshape(total, plane)
            for row in (0, row_count - 1)
        ]
        halos = [
            lax.ppermute(low, "space", ring(spaces, -1)),
            lax.ppermute(high, "space", ring(spaces, 1)),
        ]

    patches, *convs, conv_shift = pl.pallas_call(
        functools.partial(prepare_kernel, paired, len(blocks)),
        out_shape=[jax.ShapeDtypeStruct((row_count, 9, total, plane), BF16)]
        + [jax.ShapeDtypeStruct((tall, 27 * GROUP * fields), BF16)] * 2
        + [jax.ShapeDtypeStruct((tall, 128), F32)],
        in_specs=[VMEM] * (len(blocks) + 2),
        out_specs=[VMEM] * 4,
        compiler_params=PARAMS,
        cost_estimate=cost(0.01),
        name="prepare",
    )(*blocks, conv, conv_shift)
    weights = [conv_shift, *weights]

    if paired:
        far_halo, near_halo, patches, *weights = lax.optimization_barrier(
            (far_halo, near_halo, patches, *weights)
        )
        merged = pl.pallas_call(
            merge_kernel,
            out_shape=jax.ShapeDtypeStruct((total, plane), BF16),
            in_specs=[VMEM] * 2,
            out_specs=VMEM,
            compiler_params=PARAMS,
            cost_estimate=cost(0.05),
            name="merge",
        )(near_halo, far_halo)
        halos = [near_halo, far_halo, lax.ppermute(merged, "tm", beside)]

    inner = pl.pallas_call(
        inner_kernel,
        out_shape=jax.ShapeDtypeStruct((frames, row_count - 2, channels, plane), BF16),
        in_specs=[VMEM] * (2 + len(weights)),
        out_specs=VMEM,
        compiler_params=PARAMS,
        cost_estimate=cost(0.5),
        name="inner",
    )(patches, convs[0], *weights)

    return pl.pallas_call(
        functools.partial(outer_kernel, paired),
        out_shape=jax.ShapeDtypeStruct((frames, row_count, channels, plane), BF16),
        in_specs=[VMEM] * (len(halos) + 4 + len(weights)),
        out_specs=pl.BlockSpec(memory_space=pl.ANY),
        scratch_shapes=[
            pltpu.VMEM((2, 9, total, plane), BF16),
            pltpu.VMEM((2, frames, channels, plane), BF16),
            pltpu.SemaphoreType.DMA((3,)),
        ],
        compiler_params=PARAMS,
        cost_estimate=cost(2.5),
        name="outer",
    )(*halos, patches, inner, *convs, *weights)


def solution(mesh):
    in_specs = (P("tm", "space", None, None), P(), P(), P(), P(), P(), P())
    out_specs = P("tm", "space", None, None)
    return jax.shard_map(shards, mesh=mesh, in_specs=in_specs, out_specs=out_specs, check_vma=False)
```

```python
import functools
import math

import jax
import jax.numpy as jnp
from jax import lax
from jax.experimental import pallas as pl
from jax.experimental.pallas import tpu as pltpu
from jax.sharding import PartitionSpec as P

LEVELS = 3
NZ = 32
GROUP = 4
CELLS = 256
SLOPE = math.sqrt(2.0 / math.pi)
CUBIC = SLOPE * 0.044715
BF16 = jnp.bfloat16
F32 = jnp.float32


def frame_blocks(axis_size, frames):
    needed = [0]
    counts = [1]
    for level in reversed(range(LEVELS)):
        reach = set()
        for offset in needed:
            for frame in range(frames):
                for step in (-(2**level), 2**level):
                    reach.add((offset + (frame + step) // frames) % axis_size)
        needed = needed + sorted(reach - set(needed))
        spare = [offset for offset in range(axis_size) if offset not in needed]
        while len(needed) * frames % GROUP and spare:
            needed.append(spare.pop(0))
        counts.append(len(needed))
    return needed, counts[::-1]


def gelu_of_double(half):
    inner = half * (2 * SLOPE + 8 * CUBIC * (half * half))
    return (half + half * jnp.tanh(inner)).astype(BF16)


def joined(parts, axis):
    return parts[0] if len(parts) == 1 else jnp.concatenate(parts, axis=axis)


def wide(shift, cells):
    return joined([shift] * (cells // 128), 1)


def column(row, copies):
    count = row.shape[1]
    down = lax.broadcasted_iota(jnp.int32, (count, count), 0)
    across = lax.broadcasted_iota(jnp.int32, (count, count), 1)
    tall = jnp.sum(jnp.where(down == across, row, 0.0), axis=1, keepdims=True)
    return joined([tall] * copies, 0)


def lanes(value):
    return jnp.broadcast_to(value, (value.shape[0], 128))


def spread(block, rows, columns):
    height, width = block.shape
    tile = jnp.concatenate([block] * (128 // width), axis=1)
    parts = [tile] * (columns // 128)
    if columns % 128:
        parts.append(tile[:, : columns % 128])
    return joined([joined(parts, 1)] * (rows // height), 0)


def fetch_kernel(*refs):
    count = len(refs) // 2
    sems = refs[-1]
    copies = [
        pltpu.make_async_copy(refs[index], refs[count + index], sems.at[index])
        for index in range(count)
    ]
    for copy in copies:
        copy.start()
    for copy in copies:
        copy.wait()


def conv_kernel(conv, conv_shift, *outs):
    places, fields, channels = conv.shape
    depth = places * fields
    wide = depth * GROUP
    flat = conv[...].astype(F32).reshape(depth, channels).astype(BF16)
    down = lax.broadcasted_iota(jnp.int32, (depth, wide), 0)
    across = lax.broadcasted_iota(jnp.int32, (depth, wide), 1)
    same = (down // fields == across // (GROUP * fields)) & (down % fields == across % fields)
    pick = jnp.where(same, 1.0, 0.0).astype(BF16)
    full = lax.dot_general(flat, pick, (((0,), (0,)), ((), ())), preferred_element_type=F32)
    full = jnp.concatenate([full] * GROUP, axis=0)
    down = lax.broadcasted_iota(jnp.int32, full.shape, 0)
    across = lax.broadcasted_iota(jnp.int32, full.shape, 1)
    keep = down // channels == across // fields % GROUP
    full = jnp.where(keep, 0.5 * full, 0.0)
    third = wide // 3
    turned = jnp.concatenate([full[:, 2 * third :], full[:, third : -third], full[:, :third]], axis=1)
    outs[0][...] = full.astype(BF16)
    outs[1][...] = turned.astype(BF16)
    outs[2][...] = lanes(0.5 * column(conv_shift[...], GROUP))


def levels_kernel(slot_of, frames, taps, tap_shift, mix, mix_shift, *outs):
    tap_outs, tap_shift_outs = outs[:LEVELS], outs[LEVELS : 2 * LEVELS]
    mix_out, mix_shift_out = outs[2 * LEVELS :]
    channels = mix.shape[-1]
    slots = slot_of(lax.axis_index("tm"))
    for level in range(LEVELS):
        rows, columns = tap_outs[level].shape
        columns //= level + 1

        def frame_of(axis):
            place = lax.broadcasted_iota(jnp.int32, (rows, columns), axis) // channels
            block = place // frames
            start = jnp.zeros((rows, columns), jnp.int32)
            for index, slot in enumerate(slots[: (rows, columns)[axis] // channels // frames]):
                start = jnp.where(block == index, slot * frames, start)
            return start + place % frames

        gap = frame_of(1) - frame_of(0)
        for source in range(level + 1):
            total = jnp.zeros((rows, columns), F32)
            for tap in range(3):
                block = taps[level, tap]
                if source:
                    block = jnp.dot(block, mix[source - 1], preferred_element_type=F32)
                block = spread(block.astype(F32), rows, columns)
                total = jnp.where(gap == (tap - 1) * 2**level, block, total)
            if not source:
                shift = column(tap_shift[level : level + 1], rows // channels)
                if level:
                    held = jnp.sum(mix_shift[:level], axis=0, keepdims=True)
                    held = total * spread(held, 1, columns)
                    shift = shift + jnp.sum(held, axis=1, keepdims=True)
                tap_shift_outs[level][...] = lanes(0.5 * shift)
            part = slice(source * columns, (source + 1) * columns)
            tap_outs[level][:, part] = (0.5 * total).astype(BF16)
    size = mix_out.shape[0]
    down = lax.broadcasted_iota(jnp.int32, (size, size), 0)
    across = lax.broadcasted_iota(jnp.int32, (size, size), 1)
    same = down // channels == across // channels
    mix_out[...] = jnp.concatenate(
        [
            jnp.where(same, spread(mix[level].astype(F32), size, size), 0.0).astype(BF16)
            for level in range(LEVELS)
        ],
        axis=1,
    )
    held = jnp.sum(mix_shift[...], axis=0, keepdims=True)
    mix_shift_out[...] = lanes(column(held, size // channels))


def shifted(lines):
    plane = lines.shape[-1]
    depth = lax.broadcasted_iota(jnp.int32, (1, plane), 1) % NZ
    blank = jnp.zeros_like(lines)
    below = jnp.where(depth == 0, blank, pltpu.roll(lines, 1, 1))
    above = jnp.where(depth == NZ - 1, blank, pltpu.roll(lines, plane - 1, 1))
    for delta_y in (-1, 0, 1):
        for piece in (below, lines, above):
            yield pltpu.roll(piece, -delta_y * NZ % plane, 1) if delta_y else piece


def encode(windows, weights, frames, store):
    conv_shift, mix, mix_shift = weights[0], *weights[-2:]
    taps, tap_shifts = weights[1 : 1 + LEVELS], weights[1 + LEVELS : 1 + 2 * LEVELS]
    channels = conv_shift.shape[0] // GROUP
    groups = -(-taps[0].shape[1] // conv_shift.shape[0])
    held = []
    for conv, window in windows:
        parts = []
        for group in range(groups):
            summed = jnp.dot(conv[...], window(group), preferred_element_type=F32)
            parts.append(gelu_of_double(summed + wide(conv_shift[...], summed.shape[1])))
        held.append([joined(parts, 0)])
    for level, (tap, shift) in enumerate(zip(taps, tap_shifts)):
        columns = tap.shape[1] // (level + 1)
        for parts in held:
            read = joined([part[:columns] for part in parts], 0)
            summed = jnp.dot(tap[...], read, preferred_element_type=F32)
            parts.append(gelu_of_double(summed + wide(shift[...], summed.shape[1])))
    size = mix.shape[0]
    for index, (first, *gated) in enumerate(held):
        read = joined([part[:size] for part in gated], 0)
        mixed = jnp.dot(mix[...], read, preferred_element_type=F32)
        mixed = mixed + wide(mix_shift[...], mixed.shape[1])
        final = (first[:size].astype(F32) + mixed).astype(BF16)
        for frame in range(frames):
            store(index, frame, final[frame * channels : (frame + 1) * channels])


def stack(sources, group, depth, cells):
    part = slice(group * depth, (group + 1) * depth)
    return jnp.concatenate(
        [source[:, part, cells].reshape(9 * depth, -1) for source in sources], axis=0
    )


def pack_kernel(own, near, *outs):
    frames, row_count = near.shape[:2]
    first = lax.rem(lax.axis_index("tm"), 2) == 0
    rows = []
    for row in (0, row_count - 1):
        mine, beside = [
            jnp.concatenate([block[frame, row] for frame in range(frames)], axis=0)
            for block in (own, near)
        ]
        rows.append(
            jnp.concatenate(
                [jnp.where(first, mine, beside), jnp.where(first, beside, mine)], axis=0
            )
        )
    outs[2][0] = own[...]
    outs[2][1] = near[...]
    outs[0][...] = rows[1]
    outs[1][...] = rows[0]


def patch_kernel(paired, *refs):
    blocks, patches = refs[:-1], refs[-1]
    if paired:
        own, near, beyond = blocks
        blocks = own, beyond.at[0], near, beyond.at[1]
    frames, row_count = blocks[0].shape[:2]
    for row in range(row_count):
        lines = [block[frame, row] for block in blocks for frame in range(frames)]
        for place, piece in enumerate(shifted(jnp.concatenate(lines, axis=0))):
            patches[row, place] = piece


def prepare_kernel(slot_of, frames, conv, conv_shift, *refs):
    conv_kernel(conv, conv_shift, *refs[4:7])
    levels_kernel(slot_of, frames, *refs[:4], *refs[7:])


def inner_kernel(patches, conv, *rest):
    weights, out = rest[:-1], rest[-1]
    row_count, _, _, plane = patches.shape
    depth = conv.shape[1] // 27
    width = math.gcd(plane, CELLS)
    places = [
        (row, slice(start, start + width))
        for row in range(1, row_count - 1)
        for start in range(0, plane, width)
    ]
    windows = [
        (
            conv,
            functools.partial(
                stack, [patches.at[row + step] for step in (-1, 0, 1)], depth=depth, cells=cells
            ),
        )
        for row, cells in places
    ]

    def store(index, frame, final):
        row, cells = places[index]
        out[frame, row - 1, :, cells] = final

    encode(windows, weights, out.shape[0], store)


def merge_kernel(near, far, out):
    out[...] = jnp.concatenate([near[...], far[...]], axis=0)


def halo_lines(got, other):
    first = lax.rem(lax.axis_index("tm"), 2) == 0
    half = got.shape[0] // 2
    parts = [[], []]
    for held in (jnp.where(first, got, other), jnp.where(first, other, got)):
        upper, lower = held[:half], held[half:]
        parts[0].append(jnp.where(first, upper, lower))
        parts[1].append(jnp.where(first, lower, upper))
    return jnp.concatenate(parts[0] + parts[1], axis=0)


def outer_kernel(paired, near, far, *refs):
    near, far = near[...], far[...]
    if paired:
        half = refs[0].shape[0] // 2
        near = halo_lines(near, refs[0][:half])
        far = halo_lines(far, refs[0][half:])
        refs = refs[1:]
    halos = far, near
    patches, inner, *convs = refs[:4]
    weights, (out, borders, done, sems) = refs[4:-4], refs[-4:]
    row_count, _, _, plane = patches.shape
    depth = convs[0].shape[1] // 27
    width = math.gcd(plane, CELLS)
    rows = [(0, 1), (row_count - 1, row_count - 2)]
    copies = [pltpu.make_async_copy(inner, out.at[:, 1 : row_count - 1], sems.at[0])]
    copies[0].start()
    windows = []
    places = []
    for side, (edge, inside) in enumerate(rows):
        for place, piece in enumerate(shifted(halos[side])):
            borders[side, place] = piece
        sources = [borders.at[side], patches.at[edge], patches.at[inside]]
        for start in range(0, plane, width):
            cells = slice(start, start + width)
            places.append((side, cells))
            windows.append(
                (convs[side], functools.partial(stack, sources, depth=depth, cells=cells))
            )

    def store(index, frame, final):
        side, cells = places[index]
        done[side, frame, :, cells] = final

    encode(windows, weights, out.shape[0], store)
    for side, (edge, _) in enumerate(rows):
        copies.append(pltpu.make_async_copy(done.at[side], out.at[:, edge], sems.at[side + 1]))
        copies[-1].start()
    for copy in copies:
        copy.wait()


VMEM = pl.BlockSpec(memory_space=pltpu.VMEM)
PARAMS = pltpu.CompilerParams(vmem_limit_bytes=40 * 2**20)


def cost(microseconds):
    size, flops = int(microseconds * 3.7e6), int(microseconds * 1.15e9)
    return pl.CostEstimate(flops=flops, bytes_accessed=size, transcendentals=0)


def ring(count, step):
    return [(index, (index + step) % count) for index in range(count)]


def shards(snapshots, conv_weight, conv_bias, tap_weight, tap_bias, mix_weight, mix_bias):
    frames, row_count, fields, plane = snapshots.shape
    channels = conv_weight.shape[0]
    times = lax.axis_size("tm")
    spaces = lax.axis_size("space")
    offsets, counts = frame_blocks(times, frames)
    paired = times == 4 and sorted(offsets) == [0, 1, 2, 3] and spaces % 2 == 0
    tall = GROUP * channels
    total = len(offsets) * frames * fields

    sources = [
        snapshots,
        conv_weight.transpose(2, 3, 4, 1, 0).reshape(27, fields, channels),
        conv_bias.reshape(1, channels),
        tap_weight.transpose(0, 2, 1, 3),
        tap_bias,
        mix_weight,
        mix_bias,
    ]
    sources = [pltpu.with_memory_space_constraint(source, pltpu.HBM) for source in sources]
    sources = pl.pallas_call(
        fetch_kernel,
        out_shape=[jax.ShapeDtypeStruct(source.shape, source.dtype) for source in sources],
        in_specs=[pl.BlockSpec(memory_space=pl.ANY)] * len(sources),
        out_specs=[VMEM] * len(sources),
        scratch_shapes=[pltpu.SemaphoreType.DMA((len(sources),))],
        compiler_params=PARAMS,
        cost_estimate=cost(0.8),
        name="fetch",
    )(*sources)

    if paired:
        offsets = [0, 2, 1, 3]
        slot_of = lambda index: [index ^ offset for offset in offsets]
        across = [(index, index ^ 2) for index in range(times)]
        beside = [(index, index ^ 1) for index in range(times)]
        near = lax.ppermute(snapshots, "tm", beside)
        to_far, to_near, pair = pl.pallas_call(
            pack_kernel,
            out_shape=[jax.ShapeDtypeStruct((total // 2, plane), BF16)] * 2
            + [jax.ShapeDtypeStruct((2,) + snapshots.shape, BF16)],
            in_specs=[VMEM] * 2,
            out_specs=[VMEM] * 3,
            compiler_params=PARAMS,
            cost_estimate=cost(0.05),
            name="pack",
        )(sources[0], near)
        far_pairs, near_pairs = [], []
        for time in range(times):
            for space in range(spaces):
                target = (time ^ (time % 2 * 2)) * spaces
                far_pairs.append((time * spaces + space, target + (space + 1) % spaces))
                near_pairs.append((time * spaces + space, target + (space - 1) % spaces))
        beyond = lax.ppermute(pair, "tm", across)
        near_halo = lax.ppermute(to_near, ("tm", "space"), near_pairs)
        far_halo = lax.ppermute(to_far, ("tm", "space"), far_pairs)
    else:
        slot_of = lambda index: [(index + offset) % times for offset in offsets]

    own, conv, conv_shift, *levels = sources
    if paired:
        far_halo, conv, conv_shift, *levels = lax.optimization_barrier(
            (far_halo, conv, conv_shift, *levels)
        )
    wide_of = [count * frames * channels for count in counts]
    shapes = []
    for level in range(LEVELS):
        shape = wide_of[level + 1], wide_of[level] * (level + 1)
        shapes.append(jax.ShapeDtypeStruct(shape, BF16))
    for level in range(LEVELS):
        shapes.append(jax.ShapeDtypeStruct((wide_of[level + 1], 128), F32))
    shapes += [
        jax.ShapeDtypeStruct((wide_of[LEVELS], wide_of[LEVELS] * LEVELS), BF16),
        jax.ShapeDtypeStruct((wide_of[LEVELS], 128), F32),
    ]
    made = pl.pallas_call(
        functools.partial(prepare_kernel, slot_of, frames),
        out_shape=[jax.ShapeDtypeStruct((tall, 27 * GROUP * fields), BF16)] * 2
        + [jax.ShapeDtypeStruct((tall, 128), F32)]
        + shapes,
        in_specs=[VMEM] * 6,
        out_specs=[VMEM] * (3 + len(shapes)),
        compiler_params=PARAMS,
        cost_estimate=cost(0.52),
        name="prepare",
    )(conv, conv_shift, *levels)
    convs, weights = made[:2], made[2:]

    if paired:
        blocks = [own, near, beyond]
    else:
        blocks = [own] + [
            lax.ppermute(snapshots, "tm", ring(times, -offset)) for offset in offsets[1:]
        ]
        low, high = [
            jnp.concatenate([block[:, row] for block in blocks], axis=0).reshape(total, plane)
            for row in (0, row_count - 1)
        ]
        halos = [
            lax.ppermute(low, "space", ring(spaces, -1)),
            lax.ppermute(high, "space", ring(spaces, 1)),
        ]

    patches = pl.pallas_call(
        functools.partial(patch_kernel, paired),
        out_shape=jax.ShapeDtypeStruct((row_count, 9, total, plane), BF16),
        in_specs=[VMEM] * len(blocks),
        out_specs=VMEM,
        compiler_params=PARAMS,
        cost_estimate=cost(0.01),
        name="patch",
    )(*blocks)

    if paired:
        far_halo, near_halo, patches, *weights = lax.optimization_barrier(
            (far_halo, near_halo, patches, *weights)
        )
        merged = pl.pallas_call(
            merge_kernel,
            out_shape=jax.ShapeDtypeStruct((total, plane), BF16),
            in_specs=[VMEM] * 2,
            out_specs=VMEM,
            compiler_params=PARAMS,
            cost_estimate=cost(0.05),
            name="merge",
        )(near_halo, far_halo)
        halos = [near_halo, far_halo, lax.ppermute(merged, "tm", beside)]

    inner = pl.pallas_call(
        inner_kernel,
        out_shape=jax.ShapeDtypeStruct((frames, row_count - 2, channels, plane), BF16),
        in_specs=[VMEM] * (2 + len(weights)),
        out_specs=VMEM,
        compiler_params=PARAMS,
        cost_estimate=cost(0.5),
        name="inner",
    )(patches, convs[0], *weights)

    return pl.pallas_call(
        functools.partial(outer_kernel, paired),
        out_shape=jax.ShapeDtypeStruct((frames, row_count, channels, plane), BF16),
        in_specs=[VMEM] * (len(halos) + 4 + len(weights)),
        out_specs=pl.BlockSpec(memory_space=pl.ANY),
        scratch_shapes=[
            pltpu.VMEM((2, 9, total, plane), BF16),
            pltpu.VMEM((2, frames, channels, plane), BF16),
            pltpu.SemaphoreType.DMA((3,)),
        ],
        compiler_params=PARAMS,
        cost_estimate=cost(2.5),
        name="outer",
    )(*halos, patches, inner, *convs, *weights)


def solution(mesh):
    in_specs = (P("tm", "space", None, None), P(), P(), P(), P(), P(), P())
    out_specs = P("tm", "space", None, None)
    return jax.shard_map(shards, mesh=mesh, in_specs=in_specs, out_specs=out_specs, check_vma=False)
```
